32 devices in a mesh: dom: 2 (over y), freq: 4 (over z), win: 2 (over x), rep: 2 (over core).
Axes of the slice: x: 2, y: 2, z: 4, core: 2. Of those that a mesh axis runs over, the one named last changes fastest.
Arguments:
- recorded: float32 [2, 128, 4, 1024], P(None, 'freq', ('dom', 'win'), 'rep'), parts along dimension 2, may hold values from -8 to 8
- geometry: float32 [2, 4, 1024], P(None, ('dom', 'win'), 'rep'), parts along dimension 1, may hold values from -1 to 1
- present: int32 [4, 1024], P(('dom', 'win'), 'rep'), parts along dimension 0, may hold values 0 or 1
- intersection_index: int32 [4, 2, 128], P(('dom', 'win'), 'rep'), parts along dimension 0, may hold values from 0 to 127, each once within a row
- pattern: int32 [128, 8, 8], P('freq', None, 'rep'), may hold values from 0 to 1
- group_scale: float32 [512], replicated, may hold values from 0.05 to 1.5
Outputs:
- coefficients: float32 [2, 128, 4, 512], P(None, 'freq', ('dom', 'win')), parts along dimension 2
- reconstruction: float32 [2, 128, 4, 1024], P(None, 'freq', ('dom', 'win'), 'rep'), parts along dimension 2
The draws below stay inside these ranges and needn't reach their ends.
There are 2 independent parts, one for each index of `dom`. The reference program is written for one: setup_inputs(seed, part) draws one part's arguments, and reference() takes and returns one part's arrays. A program takes and returns all parts, laid end to end along the dimension named above; an argument that names none is the same for every part. Nothing has to cross between parts.
Inputs may be any that keep to these rules, and one draw needn't show every extreme that they name: Each row intersection_index[w, r] is an ordering of 0 to 127: leading trace j of strip r of window w is the same point as trailing trace intersection_index[w, r, j] of strip r of window w - 1.
All inputs are finite; a program needn't handle non-finite values. No bound on the sum of `present` on one device may be relied on, other than what follows from the above.
Results may differ from the reference program's by a relative error of at most 0.0051.
Values may be sent and summed in bfloat16 or wider, within the bound.
No kernel may reach another device: no remote copies, remote signals or barrier semaphores. Data moves between devices by JAX's collectives and lax.ppermute only.
A program may use at most 64 MiB of HBM per device.

```python
import math
import jax
import jax.numpy as jnp
from jax import lax

PX = 16
PY = 32
SLOW = 512
SPB = 64
SBLK = 8
OBS = 128
XL = 512
STRIPS = 2
TRACES = 1024
OBLK = 8
OV = 128
FREQS = 128
WINDOWS = 2
ITERS = 3


def draw_pattern(key, part):
    levels = jnp.arange(FREQS, dtype=jnp.int32)
    limits = jnp.where(levels < FREQS // 4, 4, 1)
    values = jax.random.randint(key, (FREQS, SBLK, OBLK), 0, 5)
    return (values < limits[:, None, None]).astype(jnp.int32)


def draw_recorded(key, part):
    levels = jnp.arange(FREQS, dtype=jnp.int32)
    spread = jnp.where(levels < FREQS // 4, 0.5, 2.0).astype(jnp.float32)[None, :, None, None]
    shape = (2, FREQS, WINDOWS, TRACES)
    base = jnp.clip(jax.random.normal(key, shape, jnp.float32), -4.0, 4.0)
    return (base * spread).astype(jnp.float32)


def place_ends(array, own_key, least, largest):
    spot = [jax.random.randint(jax.random.fold_in(own_key, axis), (), 0, length) for axis, length in enumerate(array.shape)]
    longest = array.shape.index(max(array.shape))
    next_to = spot[:longest] + [(spot[longest] + 1) % array.shape[longest]] + spot[longest + 1:]
    return array.at[tuple(spot)].set(least).at[tuple(next_to)].set(largest)


def block_levels(key, extent, pieces, smallest, high):
    factor_of, own = 1.0, jax.random.fold_in(key, 6)
    for position, blocks in pieces:
        heights = jnp.exp(jax.random.uniform(jax.random.fold_in(own, position), (blocks,), jnp.float32, smallest / len(pieces), high / len(pieces)))
        factor_of = factor_of * jnp.repeat(heights, extent[position] // blocks).reshape([-1 if axis == position else 1 for axis in range(len(extent))])
    return factor_of


def setup_inputs(seed: int = 0, part: int = 0) -> dict:
    seeds = jax.random.split(jax.random.key(seed), 7)
    part_keys = jax.random.split(jax.random.fold_in(seeds[6], part), 7)
    recorded = draw_recorded(jax.random.fold_in(jax.random.fold_in(seeds[6], part), 71), part)
    geometry = jnp.clip(jax.random.uniform(part_keys[1], (2, WINDOWS, TRACES), jnp.float32, -1.0, 1.0) * block_levels(part_keys[1], (2, WINDOWS, TRACES), ((1, 2), (2, 2)), -0.4, 0.0), -1.0, 1.0)
    present = place_ends((jax.random.randint(part_keys[2], (WINDOWS, TRACES), 0, 4) < 3).astype(jnp.int32), jax.random.fold_in(part_keys[2], 1), 0, 1)
    intersection_index = jax.vmap(lambda own: jax.random.permutation(own, OV))(jax.random.split(part_keys[3], WINDOWS * STRIPS)).reshape((WINDOWS, STRIPS, OV)).astype(jnp.int32)
    pattern = draw_pattern(jax.random.fold_in(seeds[6], 71), part)
    group_scale = jnp.clip(jnp.exp(jax.random.uniform(seeds[5], (SLOW,), jnp.float32, math.log(0.05), math.log(1.5))), 0.05, 1.5)
    return dict(recorded=recorded, geometry=geometry, present=present, intersection_index=intersection_index, pattern=pattern, group_scale=group_scale)


wave_scale = 32.0
step_length = 1.0
epsilon = 1e-06

def round_half(values):
    return lax.optimization_barrier(values.astype(jnp.bfloat16)).astype(jnp.float32)

def make_tables(angular, layout, pattern):
    inline_slow = (jnp.arange(PX, dtype=jnp.float32) + 0.5) * (2.0 / PX) - 1.0
    cross_slow = (jnp.arange(PY, dtype=jnp.float32) + 0.5) * (2.0 / PY) - 1.0
    phase_inline = angular[:, None, None] * layout[0][None, :, None] * inline_slow[None, None, :]
    phase_cross = angular[:, None, None] * layout[1][None, :, None] * cross_slow[None, None, :]
    active = jnp.repeat(jnp.repeat(pattern.astype(jnp.float32), SPB // PY, axis=1), OBS, axis=2)
    weight = jnp.transpose(active, (0, 2, 1)) * (1.0 / math.sqrt(TRACES))
    inline_real = round_half(jnp.cos(phase_inline) * weight)
    inline_imag = round_half(-(jnp.sin(phase_inline) * weight))
    cross_real = round_half(jnp.cos(phase_cross))
    cross_imag = round_half(-jnp.sin(phase_cross))
    return (inline_real, inline_imag, cross_real, cross_imag)

def predict_window(coeffs, layout, angular, pattern):
    inline_real, inline_imag, cross_real, cross_imag = make_tables(angular, layout, pattern)
    highest = lax.Precision.HIGHEST
    rounded = round_half(coeffs).reshape(2, FREQS, PX, PY)
    part_real = jnp.einsum('fxb,fab->fxa', cross_real, rounded[0], precision=highest) - jnp.einsum('fxb,fab->fxa', cross_imag, rounded[1], precision=highest)
    part_imag = jnp.einsum('fxb,fab->fxa', cross_real, rounded[1], precision=highest) + jnp.einsum('fxb,fab->fxa', cross_imag, rounded[0], precision=highest)
    out_real = lax.optimization_barrier(jnp.sum(inline_real * part_real - inline_imag * part_imag, axis=2))
    out_imag = lax.optimization_barrier(jnp.sum(inline_real * part_imag + inline_imag * part_real, axis=2))
    return jnp.stack([out_real, out_imag])

def project_window(residual, layout, angular, pattern):
    inline_real, inline_imag, cross_real, cross_imag = make_tables(angular, layout, pattern)
    highest = lax.Precision.HIGHEST
    res_real = residual[0][:, :, None]
    res_imag = residual[1][:, :, None]
    hidden_real = round_half(inline_real * res_real + inline_imag * res_imag)
    hidden_imag = round_half(inline_real * res_imag - inline_imag * res_real)
    grad_real = jnp.einsum('fxb,fxa->fab', cross_real, hidden_real, precision=highest) + jnp.einsum('fxb,fxa->fab', cross_imag, hidden_imag, precision=highest)
    grad_imag = jnp.einsum('fxb,fxa->fab', cross_real, hidden_imag, precision=highest) - jnp.einsum('fxb,fxa->fab', cross_imag, hidden_real, precision=highest)
    return jnp.stack([grad_real, grad_imag]).reshape(2, FREQS, SLOW)

def blend_all(predicted, intersection_index):
    highest = lax.Precision.HIGHEST
    halves = predicted.reshape(WINDOWS, 2, FREQS, STRIPS, XL)
    leading = halves[..., :OV]
    trailing = halves[..., XL - OV:]
    positions = jnp.arange(OV, dtype=jnp.int32)
    permute = (intersection_index[:, :, :, None] == positions[None, None, None, :]).astype(jnp.float32)
    leading_moved = jnp.einsum('wcfrj,wrjk->wcfrk', leading, permute, precision=highest)
    lower_trail = jnp.concatenate([jnp.zeros_like(trailing[:1]), trailing[:-1]], axis=0)
    from_lower = jnp.einsum('wcfrk,wrjk->wcfrj', lower_trail, permute, precision=highest)
    from_upper = jnp.concatenate([leading_moved[1:], jnp.zeros_like(leading_moved[:1])], axis=0)
    ramp_lead = ((intersection_index.astype(jnp.float32) + 0.5) / OV)[:, None, None, :, :]
    ramp_own = (positions.astype(jnp.float32) + 0.5) / OV
    window = jnp.arange(WINDOWS, dtype=jnp.int32)[:, None, None, None, None]
    new_lead = jnp.where(window > 0, (1.0 - ramp_lead) * from_lower + ramp_lead * leading, leading)
    new_trail = jnp.where(window < WINDOWS - 1, (1.0 - ramp_own) * trailing + ramp_own * from_upper, trailing)
    joined = jnp.concatenate([new_lead, halves[..., OV:XL - OV], new_trail], axis=-1)
    return joined.reshape(WINDOWS, 2, FREQS, TRACES)

def reference(recorded, geometry, present, intersection_index, pattern, group_scale):
    angular = math.pi * wave_scale * (0.25 + 0.75 * (jnp.arange(FREQS, dtype=jnp.int32).astype(jnp.float32) + 0.5) / FREQS)
    observed = jnp.transpose(recorded, (2, 0, 1, 3))
    layouts = jnp.transpose(geometry, (1, 0, 2))
    weight_mask = present.astype(jnp.float32)[:, None, None, :]

    def predict_one(inputs):
        return predict_window(inputs[0], inputs[1], angular, pattern)

    def project_one(inputs):
        return project_window(inputs[0], inputs[1], angular, pattern)
    current = jnp.zeros((WINDOWS, 2, FREQS, SLOW), jnp.float32)
    for iteration in range(ITERS):
        if iteration == 0:
            residual = -(weight_mask * observed)
        else:
            blended = blend_all(lax.map(predict_one, (current, layouts)), intersection_index)
            residual = weight_mask * (blended - observed)
        gradient = lax.map(project_one, (residual, layouts))
        updated = current - step_length * gradient
        energy = lax.optimization_barrier(jnp.sum(updated * updated, axis=(1, 2))) / FREQS
        factor = jnp.maximum(0.0, 1.0 - group_scale[None, :] / jnp.sqrt(energy + epsilon))
        current = updated * factor[:, None, None, :]
    reconstruction = blend_all(lax.map(predict_one, (current, layouts)), intersection_index)
    return (jnp.transpose(current, (1, 2, 0, 3)), jnp.transpose(reconstruction, (1, 2, 0, 3)))
```

```python
import functools
import math

import jax
import jax.numpy as jnp
from jax import lax
from jax.experimental import pallas as pl
from jax.experimental.pallas import tpu as pltpu
from jax.sharding import PartitionSpec as P

PX = 16
PY = 32
SPB = 64
OBS = 128
ITERS = 3
LANES = 128
GROUP = 4

step_length = 1.0
epsilon = 1e-06
HIGHEST = lax.Precision.HIGHEST
VMEM_LIMIT = 56 * 1024 * 1024


def iota(shape, dim):
    return lax.broadcasted_iota(jnp.int32, shape, dim)


def half_turns(y):
    quarter = jnp.floor(2.0 * y + 0.5)
    r = y - 0.5 * quarter
    q = quarter.astype(jnp.int32)
    r2 = r * r
    pi = math.pi
    sine = r * (
        pi
        + r2
        * (
            -(pi**3) / 6
            + r2 * (pi**5 / 120 + r2 * (-(pi**7) / 5040 + r2 * (pi**9 / 362880)))
        )
    )
    cosine = 1.0 + r2 * (
        -(pi**2) / 2 + r2 * (pi**4 / 24 + r2 * (-(pi**6) / 720 + r2 * (pi**8 / 40320)))
    )
    odd = (q & 1) == 1
    c = jnp.where(odd, sine, cosine)
    s = jnp.where(odd, cosine, sine)
    c = jnp.where(((q + 1) & 2) != 0, -c, c)
    s = jnp.where((q & 2) != 0, s, -s)
    return c, s


def times(p, q):
    return p[0] * q[0] - p[1] * q[1], p[0] * q[1] + p[1] * q[0]


def pack_kernel(place, recorded, geometry, present, intersection, pattern, keep, send):
    half = recorded.shape[1] // 2
    rep = place[1]
    for out, part in ((keep, rep), (send, 1 - rep)):
        for c in range(2):
            out[c * half : (c + 1) * half, :] = recorded[
                c, pl.ds(pl.multiple_of(part * half, 8), half), :
            ]
        base = 2 * half
        out[base : base + 8, :] = jnp.zeros((8, out.shape[1]), jnp.float32)
        pat = pattern[pl.ds(pl.multiple_of(part * half, 8), half), :].astype(jnp.float32)
        for h in range(half // 8):
            out[base : base + 8, h * LANES : h * LANES + pat.shape[1]] = pat[8 * h : 8 * h + 8]
        for t in range(4):
            sl = slice(t * LANES, (t + 1) * LANES)
            out[base + t : base + t + 1, 256:384] = geometry[0:1, sl]
            out[base + 4 + t : base + 5 + t, 256:384] = geometry[1:2, sl]
            out[base + t : base + t + 1, 384:512] = present[0:1, sl].astype(jnp.float32)
        out[base + 4 : base + 5, 384:512] = intersection[...].astype(jnp.float32)


def doubled(rows):
    turned = pltpu.roll(rows, 4, 0)
    low = iota(rows.shape, 0) < 4
    return jnp.where(low, rows, turned), jnp.where(low, turned, rows)


def project_group(hb, cross, low_rows, first_lanes, sign):
    g = lax.dot_general(hb, cross, (((1,), (1,)), ((), ())), preferred_element_type=jnp.float32)
    g = jnp.where(low_rows, g[:, :LANES], g[:, LANES:])
    g = jnp.where(first_lanes, g, 0.0)
    g = g + pltpu.roll(g, 64, 1)
    swapped = pltpu.roll(g, 32, 1)
    half = g.shape[0] // 2
    top = g[:half] + sign * swapped[half:]
    bottom = g[half:] - sign * swapped[:half]
    return top, bottom


def fold_masks():
    rows = iota((2 * PX * GROUP, LANES), 0) % GROUP
    lanes = iota((2 * PX * GROUP, LANES), 1) // 64
    low_rows = rows < 2
    first_lanes = (rows % 2) == lanes
    sign = jnp.where((iota((PX * GROUP, LANES), 1) // 32) % 2 == 0, 1.0, -1.0)
    return low_rows, first_lanes, sign


def weigh(inline, w, g, tile, r_re, r_im, hb):
    half = PX * GROUP
    sl = pl.ds(tile * LANES, LANES)
    for i in range(half // 16):
        rows = slice(16 * i, 16 * i + 16)
        low = slice(half + 16 * i, half + 16 * i + 16)
        a_re = inline[w, g, rows, sl].astype(jnp.float32)
        a_im = inline[w, g, low, sl].astype(jnp.float32)
        rr = jnp.concatenate([r_re, r_re], axis=0)
        ri = jnp.concatenate([r_im, r_im], axis=0)
        hb[w, rows, sl] = (a_re * rr + a_im * ri).astype(jnp.bfloat16)
        hb[w, low, sl] = (a_re * ri - a_im * rr).astype(jnp.bfloat16)


def pack_energy(acc, energy, windows):
    block = iota((16, LANES), 1) // 32
    own = iota((16, LANES), 0) // GROUP
    for w in range(windows):
        both = acc[w] + pltpu.roll(acc[w], 32, 1)
        for j in range(4):
            rows = jnp.where(block == own, both[16 * j : 16 * j + 16], 0.0)
            energy[w * 4 + j : w * 4 + j + 1, :] = jnp.sum(rows, axis=0, keepdims=True)


def table_kernel(
    windows, nfreq, amplitude, count, place, *refs
):
    pays = refs[:count]
    cross, inline, observed, mask, matching, updated, energy, pay, hb, acc, weights = refs[count:]
    win, first = place[0], place[2]
    half = pay.shape[2] - 8
    freqs = half // 2
    groups = freqs // GROUP
    base = half
    if count == 4:
        for s in range(2):
            pay[win, s] = pays[s][...]
            pay[1 - win, s] = pays[2 + s][...]
    else:
        for w in range(windows):
            for s in range(2):
                pay[w, s] = pays[s][w]

    for s in range(2):
        index = pay[win, s, base + 4 : base + 5, 384:512].astype(jnp.int32)
        hot = (iota((LANES, LANES), 0) == index).astype(jnp.float32)
        eye = (iota((LANES, LANES), 0) == iota((LANES, LANES), 1)).astype(jnp.float32)
        matching[s] = jnp.where(win > 0, hot, eye)
    nt = (((1,), (1,)), ((), ()))

    def align(n, _):
        w, s = 1 + n // 2, n % 2
        index = pay[w, s, base + 4 : base + 5, 384:512].astype(jnp.int32)
        hot = (iota((LANES, LANES), 0) == index).astype(jnp.float32)
        dot = functools.partial(
            lax.dot_general,
            dimension_numbers=nt,
            precision=HIGHEST,
            preferred_element_type=jnp.float32,
        )
        pay[w, s, 0:half, 0:LANES] = dot(pay[w, s, 0:half, 0:LANES], hot)
        geo = dot(pay[w, s, base : base + 8, 256:384], hot)
        pay[w, s, base : base + 1, 256:384] = geo[0:1]
        pay[w, s, base + 4 : base + 5, 256:384] = geo[4:5]
        here = dot(pay[w, s, base : base + 8, 384:512], hot)
        pay[w, s, base : base + 1, 384:512] = here[0:1]
        return 0

    lax.fori_loop(0, 2 * (windows - 1), align, 0)

    for s in range(2):
        for h in range(freqs // 8):
            low, high = doubled(pay[0, s, base : base + 8, h * LANES : (h + 1) * LANES])
            weights[s, 2 * h] = low * amplitude
            weights[s, 2 * h + 1] = high * amplitude

    sub = iota((8, LANES), 0)
    delta = 0.75 / nfreq
    start = first.astype(jnp.float32)
    scale0 = 0.25 + 0.75 * ((start + 0.5) / nfreq)
    group_scale0 = 0.25 + 0.75 * ((start + (sub % GROUP).astype(jnp.float32) + 0.5) / nfreq)
    odd_cross = (2 * sub - (PY - 1)).astype(jnp.float32)
    odd_inline = (2 * (2 * (sub // GROUP) - (PX - 1))).astype(jnp.float32)

    def strip_tables(n, _):
        w, s = n // 2, n % 2
        for t in range(4):
            off = pl.multiple_of(s * 512 + t * LANES, LANES)
            sl = pl.ds(off, LANES)
            g0 = pay[w, s, base + t : base + t + 1, 256:384]
            g1 = pay[w, s, base + 4 + t : base + 5 + t, 256:384]
            here = jnp.broadcast_to(pay[w, s, base + t : base + t + 1, 384:512], (8, LANES))
            mask[w, :, sl] = here
            now = half_turns((scale0 * g1) * odd_cross)
            more = half_turns((delta * g1) * odd_cross)
            g1b = jnp.broadcast_to(g1, (8, LANES))
            rot = half_turns((scale0 * g1b) * 16.0)
            rot_more = half_turns((delta * g1b) * 16.0)
            for f in range(freqs):
                v0 = now
                v1 = times(v0, rot)
                v2 = times(v1, rot)
                v3 = times(v2, rot)
                row = (f % GROUP) * 64
                for part in range(2):
                    cross[w, f // GROUP, row + 32 * part : row + 32 * part + 16, sl] = (
                        jnp.concatenate([v0[part], v1[part]], axis=0).astype(jnp.bfloat16)
                    )
                    cross[w, f // GROUP, row + 32 * part + 16 : row + 32 * part + 32, sl] = (
                        jnp.concatenate([v2[part], v3[part]], axis=0).astype(jnp.bfloat16)
                    )
                if f + 1 < freqs:
                    now = times(now, more)
                    rot = times(rot, rot_more)
            now = half_turns((group_scale0 * g0) * odd_inline)
            more = half_turns((GROUP * delta * g0) * odd_inline)
            rot = half_turns((group_scale0 * g0) * 8.0)
            rot_more = half_turns((GROUP * delta * jnp.broadcast_to(g0, (8, LANES))) * 8.0)
            for g in range(groups):
                v = now
                for i in range(PX // 4):
                    u = times(v, rot)
                    cv = weights[s, g, :, 8 * i + t : 8 * i + t + 1]
                    cu = weights[s, g, :, 8 * i + 4 + t : 8 * i + 5 + t]
                    for part in range(2):
                        row = part * PX * GROUP + 16 * i
                        inline[w, g, row : row + 16, sl] = jnp.concatenate(
                            [v[part] * cv, u[part] * cu], axis=0
                        ).astype(jnp.bfloat16)
                    if i + 1 < PX // 4:
                        v = times(u, rot)
                if g + 1 < groups:
                    now = times(now, more)
                    rot = times(rot, rot_more)
        for c in range(2):
            for h in range(freqs // 8):
                for t in range(4):
                    sl = pl.ds(pl.multiple_of(s * 512 + t * LANES, LANES), LANES)
                    here = jnp.broadcast_to(
                        pay[w, s, base + t : base + t + 1, 384:512], (8, LANES)
                    )
                    rows = here * pay[
                        w, s, c * freqs + 8 * h : c * freqs + 8 * h + 8, t * LANES : (t + 1) * LANES
                    ]
                    low, high = doubled(rows)
                    observed[c, w, 2 * h, :, sl] = low
                    observed[c, w, 2 * h + 1, :, sl] = high
        return 0

    lax.fori_loop(0, 2 * windows, strip_tables, 0)

    low_rows, first_lanes, sign = fold_masks()
    rows = PX * GROUP
    acc[...] = jnp.zeros_like(acc)

    def first_group(n, _):
        g, w = n % groups, n // groups
        for tile in range(8):
            sl = slice(tile * LANES, (tile + 1) * LANES)
            weigh(inline, w, g, tile, -observed[0, w, g, :, sl], -observed[1, w, g, :, sl], hb)
        top, bottom = project_group(hb[w], cross[w, g], low_rows, first_lanes, sign)
        top, bottom = -step_length * top, -step_length * bottom
        updated[w, g, :rows] = top
        updated[w, g, rows:] = bottom
        acc[w] += top * top
        return 0

    lax.fori_loop(0, windows * groups, first_group, 0)
    pack_energy(acc, energy, windows)


def spread_factor(energies, threshold, factor, windows, nfreq):
    total = energies[0][...]
    for e in energies[1:]:
        total = total + e[...]
    limit = jnp.concatenate([threshold[...]] * windows, axis=0)
    packed = jnp.maximum(0.0, 1.0 - limit / jnp.sqrt(total / nfreq + epsilon))
    block = iota((8, LANES), 1) // 32
    own = iota((8, LANES), 0) // GROUP
    for w in range(windows):
        for j in range(4):
            row = jnp.broadcast_to(packed[w * 4 + j : w * 4 + j + 1], (8, LANES))
            for k in range(2):
                y = jnp.where(block == own + 2 * k, row, 0.0)
                y = y + pltpu.roll(y, 32, 1)
                y = y + pltpu.roll(y, 64, 1)
                factor[w, 16 * j + 8 * k : 16 * j + 8 * k + 8, :] = y


def mixing_masks():
    rows = iota((2 * PX * GROUP, LANES), 0) % GROUP
    lanes = iota((2 * PX * GROUP, LANES), 1) // 64
    return rows == lanes, rows == lanes + 2


def scaled(updated, factor, w, g):
    rows = PX * GROUP
    shrink = factor[w]
    return updated[w, g, :rows] * shrink, updated[w, g, rows:] * shrink


def predict_group(current, cross, inline, w, g, masks):
    m = jnp.concatenate(current, axis=0)
    mixing = jnp.concatenate(
        [jnp.where(masks[0], m, 0.0), jnp.where(masks[1], m, 0.0)], axis=1
    ).astype(jnp.bfloat16)
    rows = PX * GROUP
    out = []
    for pair in range(4):
        part = jnp.dot(
            mixing,
            cross[w, g, :, pair * 256 : (pair + 1) * 256],
            preferred_element_type=jnp.float32,
        )
        for k in range(2):
            tile = 2 * pair + k
            sl = slice(tile * LANES, (tile + 1) * LANES)
            p_re = p_im = None
            for i in range(rows // 16):
                a_re = inline[w, g, 16 * i : 16 * i + 16, sl].astype(jnp.float32)
                a_im = inline[w, g, rows + 16 * i : rows + 16 * i + 16, sl].astype(jnp.float32)
                b_re = part[16 * i : 16 * i + 16, k * LANES : (k + 1) * LANES]
                b_im = part[rows + 16 * i : rows + 16 * i + 16, k * LANES : (k + 1) * LANES]
                re = a_re * b_re - a_im * b_im
                im = a_re * b_im + a_im * b_re
                p_re = re if p_re is None else p_re + re
                p_im = im if p_im is None else p_im + im
            p_re = p_re[:8] + p_re[8:]
            p_im = p_im[:8] + p_im[8:]
            out.append((p_re + pltpu.roll(p_re, 4, 0), p_im + pltpu.roll(p_im, 4, 0)))
    return out


def blend(predicted, windows):
    ramp = (iota((8, LANES), 1).astype(jnp.float32) + 0.5) / LANES
    for w in range(windows - 1):
        for s in range(2):
            lower, upper = predicted[w][4 * s + 3], predicted[w + 1][4 * s]
            both = tuple((1.0 - ramp) * lower[c] + ramp * upper[c] for c in range(2))
            predicted[w][4 * s + 3] = both
            predicted[w + 1][4 * s] = both
    return predicted


def step_kernel(windows, nfreq, count, *refs):
    energies = refs[:count]
    threshold, updated, cross, inline, observed, mask = refs[count : count + 6]
    new, energy, factor, hb, acc = refs[count + 6 :]
    spread_factor(energies, threshold, factor, windows, nfreq)
    masks = mixing_masks()
    low_rows, first_lanes, sign = fold_masks()
    rows = PX * GROUP
    acc[...] = jnp.zeros_like(acc)

    def one_group(g, _):
        predicted = []
        for w in range(windows):
            current = scaled(updated, factor, w, g)
            predicted.append(predict_group(current, cross, inline, w, g, masks))
        predicted = blend(predicted, windows)
        for w in range(windows):
            for tile in range(8):
                sl = slice(tile * LANES, (tile + 1) * LANES)
                here = mask[w, :, sl]
                p_re, p_im = predicted[w][tile]
                r_re = here * p_re - observed[0, w, g, :, sl]
                r_im = here * p_im - observed[1, w, g, :, sl]
                weigh(inline, w, g, tile, r_re, r_im, hb)
            top, bottom = project_group(hb[w], cross[w, g], low_rows, first_lanes, sign)
            current = scaled(updated, factor, w, g)
            top = current[0] - step_length * top
            bottom = current[1] - step_length * bottom
            new[w, g, :rows] = top
            new[w, g, rows:] = bottom
            acc[w] += top * top
        return 0

    lax.fori_loop(0, updated.shape[1], one_group, 0)
    pack_energy(acc, energy, windows)


def final_kernel(windows, nfreq, count, place, *refs):
    energies = refs[:count]
    threshold, updated, cross, inline, matching = refs[count : count + 5]
    swap, keep, factor = refs[count + 5 :]
    win = place[0]
    spread_factor(energies, threshold, factor, windows, nfreq)
    masks = mixing_masks()
    rows = PX * GROUP
    low = iota((8, LANES), 0) < 4
    even = (iota((rows, LANES), 1) // 32) % 2 == 0
    block = iota((8, LANES), 1) // 32
    own = iota((8, LANES), 0) // GROUP

    def pick(values):
        out = values[0]
        for w in range(1, windows):
            out = jnp.where(win == w, values[w], out)
        return out

    def two_groups(h, _):
        coeffs, traces = [], []
        for k in range(2):
            g = 2 * h + k
            current = [scaled(updated, factor, w, g) for w in range(windows)]
            predicted = blend(
                [predict_group(current[w], cross, inline, w, g, masks) for w in range(windows)],
                windows,
            )
            traces.append(
                [[pick([predicted[w][t][c] for w in range(windows)]) for t in range(8)] for c in range(2)]
            )
            top = pick([current[w][0] for w in range(windows)])
            bottom = pick([current[w][1] for w in range(windows)])
            parts = (jnp.where(even, top, bottom), jnp.where(even, bottom, -top))
            lines = []
            for m in parts:
                line = []
                for j in range(4):
                    v = jnp.where(block == own, m[16 * j : 16 * j + 8], 0.0) + jnp.where(
                        block == own + 2, m[16 * j + 8 : 16 * j + 16], 0.0
                    )
                    line.append(v + pltpu.roll(v, 4, 0))
                lines.append(line)
            coeffs.append(lines)
        sl = pl.ds(pl.multiple_of(8 * h, 8), 8)
        for c in range(2):
            for j in range(4):
                lanes = slice(j * LANES, (j + 1) * LANES)
                both = jnp.where(low, coeffs[0][c][j], coeffs[1][c][j])
                swap[0, c, sl, lanes] = both
                keep[0, c, sl, lanes] = both
            for t in range(8):
                lanes = slice((t % 4) * LANES, (t % 4 + 1) * LANES)
                out = keep if t < 4 else swap
                out[1, c, sl, lanes] = jnp.where(low, traces[0][c][t], traces[1][c][t])
        return 0

    lax.fori_loop(0, updated.shape[1] // 2, two_groups, 0)
    for s, out in enumerate((keep, swap)):
        for c in range(2):
            out[1, c, :, :LANES] = jnp.dot(
                out[1, c, :, :LANES],
                matching[s],
                precision=HIGHEST,
                preferred_element_type=jnp.float32,
            )


VM = pl.BlockSpec(memory_space=pltpu.VMEM)
SM = pl.BlockSpec(memory_space=pltpu.SMEM)
PARAMS = pltpu.CompilerParams(vmem_limit_bytes=VMEM_LIMIT)


def shape(*dims, dtype=jnp.float32):
    return jax.ShapeDtypeStruct(dims, dtype)


def sum_parts(energy):
    swap = [(0, 1), (1, 0)]
    energy = energy + lax.ppermute(energy, "rep", swap)
    size = lax.axis_size("freq")
    if size & (size - 1):
        return [lax.psum(energy, "freq")]
    axes = ("freq", "rep")

    def crossed(k):
        return [(2 * i + r, 2 * (i ^ k) + 1 - r) for i in range(size) for r in range(2)]

    if size <= 4:
        return [energy] + [lax.ppermute(energy, axes, crossed(k)) for k in range(1, size)]
    k = 1
    while k < size:
        energy = energy + lax.ppermute(energy, axes, crossed(k))
        k *= 2
    return [energy]


def per_device(recorded, geometry, present, intersection_index, pattern, group_scale):
    frequencies = recorded.shape[1]
    traces = recorded.shape[3]
    windows = lax.axis_size("win")
    nfreq = frequencies * lax.axis_size("freq")
    half = frequencies // 2
    groups = half // GROUP
    amplitude = 1.0 / math.sqrt(traces * lax.axis_size("rep"))
    win, rep = lax.axis_index("win"), lax.axis_index("rep")
    first = lax.axis_index("freq") * frequencies + rep * half
    place = jnp.stack([win, rep, first]).astype(jnp.int32)
    width = 2 * traces
    swap = [(0, 1), (1, 0)]

    payload = shape(2 * half + 8, traces)
    keep, send = pl.pallas_call(
        pack_kernel,
        out_shape=(payload, payload),
        in_specs=[SM] + [VM] * 5,
        out_specs=(VM, VM),
        compiler_params=PARAMS,
        name="pack",
    )(
        place,
        recorded[:, :, 0, :],
        geometry[:, 0, :],
        present,
        intersection_index[0],
        pattern.reshape(frequencies, -1),
    )
    received = lax.ppermute(send, "rep", swap)
    if windows == 2:
        diagonal = [(2 * i + r, 2 * (1 - i) + 1 - r) for i in range(2) for r in range(2)]
        pays = [
            keep,
            received,
            lax.ppermute(keep, "win", swap),
            lax.ppermute(send, ("win", "rep"), diagonal),
        ]
    else:
        pays = [lax.all_gather(keep, "win"), lax.all_gather(received, "win")]

    rows = 2 * PX * GROUP
    state = shape(windows, groups, rows, LANES)
    energy_shape = shape(4 * windows, LANES)
    scratch = [
        pltpu.VMEM((windows, rows, width), jnp.bfloat16),
        pltpu.VMEM((windows, rows // 2, LANES), jnp.float32),
    ]
    cross, inline, observed, mask, matching, updated, energy = pl.pallas_call(
        functools.partial(table_kernel, windows, nfreq, amplitude, len(pays)),
        out_shape=(
            shape(windows, groups, 2 * PY * GROUP, width, dtype=jnp.bfloat16),
            shape(windows, groups, rows, width, dtype=jnp.bfloat16),
            shape(2, windows, groups, 8, width),
            shape(windows, 8, width),
            shape(2, LANES, LANES),
            state,
            energy_shape,
        ),
        in_specs=[SM] + [VM] * len(pays),
        out_specs=(VM,) * 7,
        scratch_shapes=[pltpu.VMEM((windows, 2, 2 * half + 8, traces), jnp.float32)]
        + scratch
        + [pltpu.VMEM((2, groups, 8, LANES), jnp.float32)],
        compiler_params=PARAMS,
        name="tables",
    )(place, *pays)

    threshold = group_scale.reshape(4, LANES)
    factor_scratch = pltpu.VMEM((windows, rows // 2, LANES), jnp.float32)
    for _ in range(ITERS - 1):
        energies = sum_parts(energy)
        updated, energy = pl.pallas_call(
            functools.partial(step_kernel, windows, nfreq, len(energies)),
            out_shape=(state, energy_shape),
            in_specs=[VM] * (len(energies) + 6),
            out_specs=(VM, VM),
            scratch_shapes=[factor_scratch] + scratch,
            compiler_params=PARAMS,
            name="step",
        )(*energies, threshold, updated, cross, inline, observed, mask)
    energies = sum_parts(energy)
    halves = shape(2, 2, half, traces)
    theirs, mine = pl.pallas_call(
        functools.partial(final_kernel, windows, nfreq, len(energies)),
        out_shape=(halves, halves),
        in_specs=[SM] + [VM] * (len(energies) + 5),
        out_specs=(VM, VM),
        scratch_shapes=[factor_scratch],
        compiler_params=PARAMS,
        name="final",
    )(place, *energies, threshold, updated, cross, inline, matching)
    theirs = lax.ppermute(theirs, "rep", swap)
    both = jnp.where(
        rep == 0,
        jnp.concatenate([mine, theirs], axis=2),
        jnp.concatenate([theirs, mine], axis=2),
    )
    return (both[0][:, :, None, :], both[1][:, :, None, :])


def solution(mesh):
    return jax.shard_map(
        per_device,
        mesh=mesh,
        in_specs=(
            P(None, "freq", ("dom", "win"), "rep"),
            P(None, ("dom", "win"), "rep"),
            P(("dom", "win"), "rep"),
            P(("dom", "win"), "rep", None),
            P("freq", None, "rep"),
            P(),
        ),
        out_specs=(P(None, "freq", ("dom", "win"), None), P(None, "freq", ("dom", "win"), "rep")),
        check_vma=False,
    )
```

```python
import functools
import math

import jax
import jax.numpy as jnp
from jax import lax
from jax.experimental import pallas as pl
from jax.experimental.pallas import tpu as pltpu
from jax.sharding import PartitionSpec as P

PX = 16
PY = 32
SPB = 64
OBS = 128
ITERS = 3
LANES = 128
GROUP = 4

step_length = 1.0
epsilon = 1e-06
HIGHEST = lax.Precision.HIGHEST


def iota(shape, dim):
    return lax.broadcasted_iota(jnp.int32, shape, dim)


def half_turns(y):
    quarter = jnp.floor(2.0 * y + 0.5)
    r = y - 0.5 * quarter
    q = quarter.astype(jnp.int32)
    r2 = r * r
    pi = math.pi
    sine = r * (
        pi
        + r2
        * (
            -(pi**3) / 6
            + r2 * (pi**5 / 120 + r2 * (-(pi**7) / 5040 + r2 * (pi**9 / 362880)))
        )
    )
    cosine = 1.0 + r2 * (
        -(pi**2) / 2 + r2 * (pi**4 / 24 + r2 * (-(pi**6) / 720 + r2 * (pi**8 / 40320)))
    )
    odd = (q & 1) == 1
    c = jnp.where(odd, sine, cosine)
    s = jnp.where(odd, cosine, sine)
    c = jnp.where(((q + 1) & 2) != 0, -c, c)
    s = jnp.where((q & 2) != 0, s, -s)
    return c, s


def times(p, q):
    return p[0] * q[0] - p[1] * q[1], p[0] * q[1] + p[1] * q[0]


def pack_kernel(place, recorded, geometry, present, intersection, pattern, keep, send):
    half = recorded.shape[1] // 2
    rep = place[1]
    for out, part in ((keep, rep), (send, 1 - rep)):
        for c in range(2):
            out[c * half : (c + 1) * half, :] = recorded[
                c, pl.ds(pl.multiple_of(part * half, 8), half), :
            ]
        base = 2 * half
        out[base : base + 8, :] = jnp.zeros((8, out.shape[1]), jnp.float32)
        pat = pattern[pl.ds(pl.multiple_of(part * half, 8), half), :].astype(jnp.float32)
        for h in range(half // 8):
            out[base : base + 8, h * LANES : h * LANES + pat.shape[1]] = pat[8 * h : 8 * h + 8]
        for t in range(4):
            sl = slice(t * LANES, (t + 1) * LANES)
            out[base + t : base + t + 1, 256:384] = geometry[0:1, sl]
            out[base + 4 + t : base + 5 + t, 256:384] = geometry[1:2, sl]
            out[base + t : base + t + 1, 384:512] = present[0:1, sl].astype(jnp.float32)
        out[base + 4 : base + 5, 384:512] = intersection[...].astype(jnp.float32)


def doubled(rows):
    turned = pltpu.roll(rows, 4, 0)
    low = iota(rows.shape, 0) < 4
    return jnp.where(low, rows, turned), jnp.where(low, turned, rows)


def project_group(hb, cross, low_rows, first_lanes, sign):
    g = lax.dot_general(hb, cross, (((1,), (1,)), ((), ())), preferred_element_type=jnp.float32)
    g = jnp.where(low_rows, g[:, :LANES], g[:, LANES:])
    g = jnp.where(first_lanes, g, 0.0)
    g = g + pltpu.roll(g, 64, 1)
    swapped = pltpu.roll(g, 32, 1)
    half = g.shape[0] // 2
    top = g[:half] + sign * swapped[half:]
    bottom = g[half:] - sign * swapped[:half]
    return top, bottom


def fold_masks():
    rows = iota((2 * PX * GROUP, LANES), 0) % GROUP
    lanes = iota((2 * PX * GROUP, LANES), 1) // 64
    low_rows = rows < 2
    first_lanes = (rows % 2) == lanes
    sign = jnp.where((iota((PX * GROUP, LANES), 1) // 32) % 2 == 0, 1.0, -1.0)
    return low_rows, first_lanes, sign


def weigh(inline, w, g, tile, r_re, r_im, hb):
    half = PX * GROUP
    sl = pl.ds(tile * LANES, LANES)
    for i in range(half // 16):
        rows = slice(16 * i, 16 * i + 16)
        low = slice(half + 16 * i, half + 16 * i + 16)
        a_re = inline[w, g, rows, sl].astype(jnp.float32)
        a_im = inline[w, g, low, sl].astype(jnp.float32)
        rr = jnp.concatenate([r_re, r_re], axis=0)
        ri = jnp.concatenate([r_im, r_im], axis=0)
        hb[w, rows, sl] = (a_re * rr + a_im * ri).astype(jnp.bfloat16)
        hb[w, low, sl] = (a_re * ri - a_im * rr).astype(jnp.bfloat16)


def pack_energy(acc, energy, windows):
    block = iota((16, LANES), 1) // 32
    own = iota((16, LANES), 0) // GROUP
    for w in range(windows):
        both = acc[w] + pltpu.roll(acc[w], 32, 1)
        for j in range(4):
            rows = jnp.where(block == own, both[16 * j : 16 * j + 16], 0.0)
            energy[w * 4 + j : w * 4 + j + 1, :] = jnp.sum(rows, axis=0, keepdims=True)


def table_kernel(
    windows, nfreq, amplitude, count, place, *refs
):
    pays = refs[:count]
    cross, inline, observed, mask, matching, updated, energy, pay, hb, acc, weights = refs[count:]
    win, first = place[0], place[2]
    half = pay.shape[2] - 8
    freqs = half // 2
    groups = freqs // GROUP
    base = half
    if count == 4:
        for s in range(2):
            pay[win, s] = pays[s][...]
            pay[1 - win, s] = pays[2 + s][...]
    else:
        for w in range(windows):
            for s in range(2):
                pay[w, s] = pays[s][w]

    for s in range(2):
        index = pay[win, s, base + 4 : base + 5, 384:512].astype(jnp.int32)
        hot = (iota((LANES, LANES), 0) == index).astype(jnp.float32)
        eye = (iota((LANES, LANES), 0) == iota((LANES, LANES), 1)).astype(jnp.float32)
        matching[s] = jnp.where(win > 0, hot, eye)
    nt = (((1,), (1,)), ((), ()))

    def align(n, _):
        w, s = 1 + n // 2, n % 2
        index = pay[w, s, base + 4 : base + 5, 384:512].astype(jnp.int32)
        hot = (iota((LANES, LANES), 0) == index).astype(jnp.float32)
        dot = functools.partial(
            lax.dot_general,
            dimension_numbers=nt,
            precision=HIGHEST,
            preferred_element_type=jnp.float32,
        )
        pay[w, s, 0:half, 0:LANES] = dot(pay[w, s, 0:half, 0:LANES], hot)
        geo = dot(pay[w, s, base : base + 8, 256:384], hot)
        pay[w, s, base : base + 1, 256:384] = geo[0:1]
        pay[w, s, base + 4 : base + 5, 256:384] = geo[4:5]
        here = dot(pay[w, s, base : base + 8, 384:512], hot)
        pay[w, s, base : base + 1, 384:512] = here[0:1]
        return 0

    lax.fori_loop(0, 2 * (windows - 1), align, 0)

    for s in range(2):
        for h in range(freqs // 8):
            low, high = doubled(pay[0, s, base : base + 8, h * LANES : (h + 1) * LANES])
            weights[s, 2 * h] = low * amplitude
            weights[s, 2 * h + 1] = high * amplitude

    sub = iota((8, LANES), 0)
    delta = 0.75 / nfreq
    start = first.astype(jnp.float32)
    scale0 = 0.25 + 0.75 * ((start + 0.5) / nfreq)
    group_scale0 = 0.25 + 0.75 * ((start + (sub % GROUP).astype(jnp.float32) + 0.5) / nfreq)
    odd_cross = (2 * sub - (PY - 1)).astype(jnp.float32)
    odd_inline = (2 * (2 * (sub // GROUP) - (PX - 1))).astype(jnp.float32)

    def strip_tables(n, _):
        w, s = n // 2, n % 2
        for t in range(4):
            off = pl.multiple_of(s * 512 + t * LANES, LANES)
            sl = pl.ds(off, LANES)
            g0 = pay[w, s, base + t : base + t + 1, 256:384]
            g1 = pay[w, s, base + 4 + t : base + 5 + t, 256:384]
            here = jnp.broadcast_to(pay[w, s, base + t : base + t + 1, 384:512], (8, LANES))
            mask[w, :, sl] = here
            now = half_turns((scale0 * g1) * odd_cross)
            more = half_turns((delta * g1) * odd_cross)
            g1b = jnp.broadcast_to(g1, (8, LANES))
            rot = half_turns((scale0 * g1b) * 16.0)
            rot_more = half_turns((delta * g1b) * 16.0)
            for f in range(freqs):
                v0 = now
                v1 = times(v0, rot)
                v2 = times(v1, rot)
                v3 = times(v2, rot)
                row = (f % GROUP) * 64
                for part in range(2):
                    cross[w, f // GROUP, row + 32 * part : row + 32 * part + 16, sl] = (
                        jnp.concatenate([v0[part], v1[part]], axis=0).astype(jnp.bfloat16)
                    )
                    cross[w, f // GROUP, row + 32 * part + 16 : row + 32 * part + 32, sl] = (
                        jnp.concatenate([v2[part], v3[part]], axis=0).astype(jnp.bfloat16)
                    )
                if f + 1 < freqs:
                    now = times(now, more)
                    rot = times(rot, rot_more)
            now = half_turns((group_scale0 * g0) * odd_inline)
            more = half_turns((GROUP * delta * g0) * odd_inline)
            rot = half_turns((group_scale0 * g0) * 8.0)
            rot_more = half_turns((GROUP * delta * jnp.broadcast_to(g0, (8, LANES))) * 8.0)
            for g in range(groups):
                v = now
                for i in range(PX // 4):
                    u = times(v, rot)
                    cv = weights[s, g, :, 8 * i + t : 8 * i + t + 1]
                    cu = weights[s, g, :, 8 * i + 4 + t : 8 * i + 5 + t]
                    for part in range(2):
                        row = part * PX * GROUP + 16 * i
                        inline[w, g, row : row + 16, sl] = jnp.concatenate(
                            [v[part] * cv, u[part] * cu], axis=0
                        ).astype(jnp.bfloat16)
                    if i + 1 < PX // 4:
                        v = times(u, rot)
                if g + 1 < groups:
                    now = times(now, more)
                    rot = times(rot, rot_more)
        for c in range(2):
            for h in range(freqs // 8):
                for t in range(4):
                    sl = pl.ds(pl.multiple_of(s * 512 + t * LANES, LANES), LANES)
                    here = jnp.broadcast_to(
                        pay[w, s, base + t : base + t + 1, 384:512], (8, LANES)
                    )
                    rows = here * pay[
                        w, s, c * freqs + 8 * h : c * freqs + 8 * h + 8, t * LANES : (t + 1) * LANES
                    ]
                    low, high = doubled(rows)
                    observed[c, w, 2 * h, :, sl] = low
                    observed[c, w, 2 * h + 1, :, sl] = high
        return 0

    lax.fori_loop(0, 2 * windows, strip_tables, 0)

    low_rows, first_lanes, sign = fold_masks()
    rows = PX * GROUP
    acc[...] = jnp.zeros_like(acc)

    def first_group(n, _):
        g, w = n % groups, n // groups
        for tile in range(8):
            sl = slice(tile * LANES, (tile + 1) * LANES)
            weigh(inline, w, g, tile, -observed[0, w, g, :, sl], -observed[1, w, g, :, sl], hb)
        top, bottom = project_group(hb[w], cross[w, g], low_rows, first_lanes, sign)
        top, bottom = -step_length * top, -step_length * bottom
        updated[w, g, :rows] = top
        updated[w, g, rows:] = bottom
        acc[w] += top * top
        return 0

    lax.fori_loop(0, windows * groups, first_group, 0)
    pack_energy(acc, energy, windows)


def spread_factor(energies, threshold, factor, windows, nfreq):
    total = energies[0][...]
    for e in energies[1:]:
        total = total + e[...]
    limit = jnp.concatenate([threshold[...]] * windows, axis=0)
    packed = jnp.maximum(0.0, 1.0 - limit / jnp.sqrt(total / nfreq + epsilon))
    block = iota((8, LANES), 1) // 32
    own = iota((8, LANES), 0) // GROUP
    for w in range(windows):
        for j in range(4):
            row = jnp.broadcast_to(packed[w * 4 + j : w * 4 + j + 1], (8, LANES))
            for k in range(2):
                y = jnp.where(block == own + 2 * k, row, 0.0)
                y = y + pltpu.roll(y, 32, 1)
                y = y + pltpu.roll(y, 64, 1)
                factor[w, 16 * j + 8 * k : 16 * j + 8 * k + 8, :] = y


def mixing_masks():
    rows = iota((2 * PX * GROUP, LANES), 0) % GROUP
    lanes = iota((2 * PX * GROUP, LANES), 1) // 64
    return rows == lanes, rows == lanes + 2


def scaled(updated, factor, w, g):
    rows = PX * GROUP
    shrink = factor[w]
    return updated[w, g, :rows] * shrink, updated[w, g, rows:] * shrink


def predict_group(current, cross, inline, w, g, masks):
    m = jnp.concatenate(current, axis=0)
    mixing = jnp.concatenate(
        [jnp.where(masks[0], m, 0.0), jnp.where(masks[1], m, 0.0)], axis=1
    ).astype(jnp.bfloat16)
    rows = PX * GROUP
    out = []
    for pair in range(4):
        part = jnp.dot(
            mixing,
            cross[w, g, :, pair * 256 : (pair + 1) * 256],
            preferred_element_type=jnp.float32,
        )
        for k in range(2):
            tile = 2 * pair + k
            sl = slice(tile * LANES, (tile + 1) * LANES)
            p_re = p_im = None
            for i in range(rows // 16):
                a_re = inline[w, g, 16 * i : 16 * i + 16, sl].astype(jnp.float32)
                a_im = inline[w, g, rows + 16 * i : rows + 16 * i + 16, sl].astype(jnp.float32)
                b_re = part[16 * i : 16 * i + 16, k * LANES : (k + 1) * LANES]
                b_im = part[rows + 16 * i : rows + 16 * i + 16, k * LANES : (k + 1) * LANES]
                re = a_re * b_re - a_im * b_im
                im = a_re * b_im + a_im * b_re
                p_re = re if p_re is None else p_re + re
                p_im = im if p_im is None else p_im + im
            p_re = p_re[:8] + p_re[8:]
            p_im = p_im[:8] + p_im[8:]
            out.append((p_re + pltpu.roll(p_re, 4, 0), p_im + pltpu.roll(p_im, 4, 0)))
    return out


def blend(predicted, windows):
    ramp = (iota((8, LANES), 1).astype(jnp.float32) + 0.5) / LANES
    for w in range(windows - 1):
        for s in range(2):
            lower, upper = predicted[w][4 * s + 3], predicted[w + 1][4 * s]
            both = tuple((1.0 - ramp) * lower[c] + ramp * upper[c] for c in range(2))
            predicted[w][4 * s + 3] = both
            predicted[w + 1][4 * s] = both
    return predicted


def step_kernel(windows, nfreq, count, *refs):
    energies = refs[:count]
    threshold, updated, cross, inline, observed, mask = refs[count : count + 6]
    new, energy, factor, hb, acc = refs[count + 6 :]
    spread_factor(energies, threshold, factor, windows, nfreq)
    masks = mixing_masks()
    low_rows, first_lanes, sign = fold_masks()
    rows = PX * GROUP
    acc[...] = jnp.zeros_like(acc)

    def one_group(g, _):
        predicted = []
        for w in range(windows):
            current = scaled(updated, factor, w, g)
            predicted.append(predict_group(current, cross, inline, w, g, masks))
        predicted = blend(predicted, windows)
        for w in range(windows):
            for tile in range(8):
                sl = slice(tile * LANES, (tile + 1) * LANES)
                here = mask[w, :, sl]
                p_re, p_im = predicted[w][tile]
                r_re = here * p_re - observed[0, w, g, :, sl]
                r_im = here * p_im - observed[1, w, g, :, sl]
                weigh(inline, w, g, tile, r_re, r_im, hb)
            top, bottom = project_group(hb[w], cross[w, g], low_rows, first_lanes, sign)
            current = scaled(updated, factor, w, g)
            top = current[0] - step_length * top
            bottom = current[1] - step_length * bottom
            new[w, g, :rows] = top
            new[w, g, rows:] = bottom
            acc[w] += top * top
        return 0

    lax.fori_loop(0, updated.shape[1], one_group, 0)
    pack_energy(acc, energy, windows)


def final_kernel(windows, nfreq, count, place, *refs):
    energies = refs[:count]
    threshold, updated, cross, inline, matching = refs[count : count + 5]
    swap, keep, factor = refs[count + 5 :]
    win = place[0]
    spread_factor(energies, threshold, factor, windows, nfreq)
    masks = mixing_masks()
    rows = PX * GROUP
    low = iota((8, LANES), 0) < 4
    even = (iota((rows, LANES), 1) // 32) % 2 == 0
    block = iota((8, LANES), 1) // 32
    own = iota((8, LANES), 0) // GROUP

    def pick(values):
        out = values[0]
        for w in range(1, windows):
            out = jnp.where(win == w, values[w], out)
        return out

    def two_groups(h, _):
        coeffs, traces = [], []
        for k in range(2):
            g = 2 * h + k
            current = [scaled(updated, factor, w, g) for w in range(windows)]
            predicted = blend(
                [predict_group(current[w], cross, inline, w, g, masks) for w in range(windows)],
                windows,
            )
            traces.append(
                [[pick([predicted[w][t][c] for w in range(windows)]) for t in range(8)] for c in range(2)]
            )
            top = pick([current[w][0] for w in range(windows)])
            bottom = pick([current[w][1] for w in range(windows)])
            parts = (jnp.where(even, top, bottom), jnp.where(even, bottom, -top))
            lines = []
            for m in parts:
                line = []
                for j in range(4):
                    v = jnp.where(block == own, m[16 * j : 16 * j + 8], 0.0) + jnp.where(
                        block == own + 2, m[16 * j + 8 : 16 * j + 16], 0.0
                    )
                    line.append(v + pltpu.roll(v, 4, 0))
                lines.append(line)
            coeffs.append(lines)
        sl = pl.ds(pl.multiple_of(8 * h, 8), 8)
        for c in range(2):
            for j in range(4):
                lanes = slice(j * LANES, (j + 1) * LANES)
                both = jnp.where(low, coeffs[0][c][j], coeffs[1][c][j])
                swap[0, c, sl, lanes] = both
                keep[0, c, sl, lanes] = both
            for t in range(8):
                lanes = slice((t % 4) * LANES, (t % 4 + 1) * LANES)
                out = keep if t < 4 else swap
                out[1, c, sl, lanes] = jnp.where(low, traces[0][c][t], traces[1][c][t])
        return 0

    lax.fori_loop(0, updated.shape[1] // 2, two_groups, 0)
    for s, out in enumerate((keep, swap)):
        for c in range(2):
            out[1, c, :, :LANES] = jnp.dot(
                out[1, c, :, :LANES],
                matching[s],
                precision=HIGHEST,
                preferred_element_type=jnp.float32,
            )


VM = pl.BlockSpec(memory_space=pltpu.VMEM)
SM = pl.BlockSpec(memory_space=pltpu.SMEM)


def params(windows):
    return pltpu.CompilerParams(vmem_limit_bytes=(16 if windows == 2 else 40) * 1024 * 1024)


def shape(*dims, dtype=jnp.float32):
    return jax.ShapeDtypeStruct(dims, dtype)


def sum_parts(energy):
    swap = [(0, 1), (1, 0)]
    energy = energy + lax.ppermute(energy, "rep", swap)
    size = lax.axis_size("freq")
    if size & (size - 1):
        return [lax.psum(energy, "freq")]
    axes = ("freq", "rep")

    def crossed(k):
        return [(2 * i + r, 2 * (i ^ k) + 1 - r) for i in range(size) for r in range(2)]

    if size <= 4:
        return [energy] + [lax.ppermute(energy, axes, crossed(k)) for k in range(1, size)]
    k = 1
    while k < size:
        energy = energy + lax.ppermute(energy, axes, crossed(k))
        k *= 2
    return [energy]


def per_device(recorded, geometry, present, intersection_index, pattern, group_scale):
    frequencies = recorded.shape[1]
    traces = recorded.shape[3]
    windows = lax.axis_size("win")
    nfreq = frequencies * lax.axis_size("freq")
    half = frequencies // 2
    groups = half // GROUP
    amplitude = 1.0 / math.sqrt(traces * lax.axis_size("rep"))
    win, rep = lax.axis_index("win"), lax.axis_index("rep")
    first = lax.axis_index("freq") * frequencies + rep * half
    place = jnp.stack([win, rep, first]).astype(jnp.int32)
    width = 2 * traces
    swap = [(0, 1), (1, 0)]

    payload = shape(2 * half + 8, traces)
    keep, send = pl.pallas_call(
        pack_kernel,
        out_shape=(payload, payload),
        in_specs=[SM] + [VM] * 5,
        out_specs=(VM, VM),
        compiler_params=params(windows),
        name="pack",
    )(
        place,
        recorded[:, :, 0, :],
        geometry[:, 0, :],
        present,
        intersection_index[0],
        pattern.reshape(frequencies, -1),
    )
    received = lax.ppermute(send, "rep", swap)
    if windows == 2:
        diagonal = [(2 * i + r, 2 * (1 - i) + 1 - r) for i in range(2) for r in range(2)]
        pays = [
            keep,
            received,
            lax.ppermute(keep, "win", swap),
            lax.ppermute(send, ("win", "rep"), diagonal),
        ]
    else:
        pays = [lax.all_gather(keep, "win"), lax.all_gather(received, "win")]

    rows = 2 * PX * GROUP
    state = shape(windows, groups, rows, LANES)
    energy_shape = shape(4 * windows, LANES)
    scratch = [
        pltpu.VMEM((windows, rows, width), jnp.bfloat16),
        pltpu.VMEM((windows, rows // 2, LANES), jnp.float32),
    ]
    cross, inline, observed, mask, matching, updated, energy = pl.pallas_call(
        functools.partial(table_kernel, windows, nfreq, amplitude, len(pays)),
        out_shape=(
            shape(windows, groups, 2 * PY * GROUP, width, dtype=jnp.bfloat16),
            shape(windows, groups, rows, width, dtype=jnp.bfloat16),
            shape(2, windows, groups, 8, width),
            shape(windows, 8, width),
            shape(2, LANES, LANES),
            state,
            energy_shape,
        ),
        in_specs=[SM] + [VM] * len(pays),
        out_specs=(VM,) * 7,
        scratch_shapes=[pltpu.VMEM((windows, 2, 2 * half + 8, traces), jnp.float32)]
        + scratch
        + [pltpu.VMEM((2, groups, 8, LANES), jnp.float32)],
        compiler_params=params(windows),
        name="tables",
    )(place, *pays)

    threshold = group_scale.reshape(4, LANES)
    factor_scratch = pltpu.VMEM((windows, rows // 2, LANES), jnp.float32)
    for _ in range(ITERS - 1):
        energies = sum_parts(energy)
        updated, energy = pl.pallas_call(
            functools.partial(step_kernel, windows, nfreq, len(energies)),
            out_shape=(state, energy_shape),
            in_specs=[VM] * (len(energies) + 6),
            out_specs=(VM, VM),
            scratch_shapes=[factor_scratch] + scratch,
            compiler_params=params(windows),
            name="step",
        )(*energies, threshold, updated, cross, inline, observed, mask)
    energies = sum_parts(energy)
    halves = shape(2, 2, half, traces)
    theirs, mine = pl.pallas_call(
        functools.partial(final_kernel, windows, nfreq, len(energies)),
        out_shape=(halves, halves),
        in_specs=[SM] + [VM] * (len(energies) + 5),
        out_specs=(VM, VM),
        scratch_shapes=[factor_scratch],
        compiler_params=params(windows),
        name="final",
    )(place, *energies, threshold, updated, cross, inline, matching)
    theirs = lax.ppermute(theirs, "rep", swap)
    both = jnp.where(
        rep == 0,
        jnp.concatenate([mine, theirs], axis=2),
        jnp.concatenate([theirs, mine], axis=2),
    )
    return (both[0][:, :, None, :], both[1][:, :, None, :])


def solution(mesh):
    return jax.shard_map(
        per_device,
        mesh=mesh,
        in_specs=(
            P(None, "freq", ("dom", "win"), "rep"),
            P(None, ("dom", "win"), "rep"),
            P(("dom", "win"), "rep"),
            P(("dom", "win"), "rep", None),
            P("freq", None, "rep"),
            P(),
        ),
        out_specs=(P(None, "freq", ("dom", "win"), None), P(None, "freq", ("dom", "win"), "rep")),
        check_vma=False,
    )
```

```python
import functools
import math

import jax
import jax.numpy as jnp
from jax import lax
from jax.experimental import pallas as pl
from jax.experimental.pallas import tpu as pltpu
from jax.sharding import PartitionSpec as P

PX = 16
PY = 32
SPB = 64
OBS = 128
ITERS = 3
LANES = 128
GROUP = 4

step_length = 1.0
epsilon = 1e-06
HIGHEST = lax.Precision.HIGHEST


def iota(shape, dim):
    return lax.broadcasted_iota(jnp.int32, shape, dim)


def half_turns(y):
    quarter = jnp.floor(2.0 * y + 0.5)
    r = y - 0.5 * quarter
    q = quarter.astype(jnp.int32)
    r2 = r * r
    pi = math.pi
    sine = r * (
        pi
        + r2
        * (
            -(pi**3) / 6
            + r2 * (pi**5 / 120 + r2 * (-(pi**7) / 5040 + r2 * (pi**9 / 362880)))
        )
    )
    cosine = 1.0 + r2 * (
        -(pi**2) / 2 + r2 * (pi**4 / 24 + r2 * (-(pi**6) / 720 + r2 * (pi**8 / 40320)))
    )
    odd = (q & 1) == 1
    c = jnp.where(odd, sine, cosine)
    s = jnp.where(odd, cosine, sine)
    c = jnp.where(((q + 1) & 2) != 0, -c, c)
    s = jnp.where((q & 2) != 0, s, -s)
    return c, s


def times(p, q):
    return p[0] * q[0] - p[1] * q[1], p[0] * q[1] + p[1] * q[0]


def pack_kernel(
    place, recorded, geometry, present, intersection, pattern, keep, send, *scratch
):
    sources = (recorded, geometry, present, intersection, pattern)
    local, sems, turned = scratch[:5], scratch[5], scratch[6]
    copies = [
        pltpu.make_async_copy(src, dst, sems.at[n]) for n, (src, dst) in enumerate(zip(sources, local))
    ]
    for copy in copies:
        copy.start()
    for copy in copies:
        copy.wait()
    recorded, geometry, present, intersection, pattern = local
    frequencies = recorded.shape[1]
    half = frequencies // 2
    rep = place[1]
    blocks, span = pattern.shape[:2]
    for i in range(blocks):
        turned[span * i : span * (i + 1), :] = pattern[i].astype(jnp.float32)
    base = 2 * half
    for out, part in ((keep, rep), (send, 1 - rep)):
        for c in range(2):
            out[c * half : (c + 1) * half, :] = recorded[c, pl.ds(part * half, half), 0, :]
        out[base : base + 8, :] = jnp.zeros((8, out.shape[1]), jnp.float32)
        chosen = iota((half, frequencies), 0) + part * half == iota((half, frequencies), 1)
        pat = lax.dot_general(
            chosen.astype(jnp.float32),
            turned[...],
            (((1,), (1,)), ((), ())),
            preferred_element_type=jnp.float32,
        )
        for h in range(half // 8):
            out[base : base + 8, h * LANES : h * LANES + pat.shape[1]] = pat[8 * h : 8 * h + 8]
        for t in range(4):
            sl = slice(t * LANES, (t + 1) * LANES)
            out[base + t : base + t + 1, 256:384] = geometry[0, :, sl]
            out[base + 4 + t : base + 5 + t, 256:384] = geometry[1, :, sl]
            out[base + t : base + t + 1, 384:512] = present[:, sl].astype(jnp.float32)
        out[base + 4 : base + 5, 384:512] = intersection[0].astype(jnp.float32)


def unpack_kernel(place, mine, theirs, coefficients, reconstruction):
    rep = place[1]
    half = mine.shape[2]
    for n, out in enumerate((coefficients, reconstruction)):
        for c in range(2):
            out[c, pl.ds(rep * half, half), 0, :] = mine[n, c]
            out[c, pl.ds((1 - rep) * half, half), 0, :] = theirs[n, c]


def doubled(rows):
    turned = pltpu.roll(rows, 4, 0)
    low = iota(rows.shape, 0) < 4
    return jnp.where(low, rows, turned), jnp.where(low, turned, rows)


def project_group(hb, cross, low_rows, first_lanes, sign):
    g = lax.dot_general(hb, cross, (((1,), (1,)), ((), ())), preferred_element_type=jnp.float32)
    g = jnp.where(low_rows, g[:, :LANES], g[:, LANES:])
    g = jnp.where(first_lanes, g, 0.0)
    g = g + pltpu.roll(g, 64, 1)
    swapped = pltpu.roll(g, 32, 1)
    half = g.shape[0] // 2
    top = g[:half] + sign * swapped[half:]
    bottom = g[half:] - sign * swapped[:half]
    return top, bottom


def fold_masks():
    rows = iota((2 * PX * GROUP, LANES), 0) % GROUP
    lanes = iota((2 * PX * GROUP, LANES), 1) // 64
    low_rows = rows < 2
    first_lanes = (rows % 2) == lanes
    sign = jnp.where((iota((PX * GROUP, LANES), 1) // 32) % 2 == 0, 1.0, -1.0)
    return low_rows, first_lanes, sign


def weigh(inline, w, g, tile, r_re, r_im, hb):
    half = PX * GROUP
    sl = pl.ds(tile * LANES, LANES)
    for i in range(half // 16):
        rows = slice(16 * i, 16 * i + 16)
        low = slice(half + 16 * i, half + 16 * i + 16)
        a_re = inline[w, g, rows, sl].astype(jnp.float32)
        a_im = inline[w, g, low, sl].astype(jnp.float32)
        rr = jnp.concatenate([r_re, r_re], axis=0)
        ri = jnp.concatenate([r_im, r_im], axis=0)
        hb[rows, sl] = (a_re * rr + a_im * ri).astype(jnp.bfloat16)
        hb[low, sl] = (a_re * ri - a_im * rr).astype(jnp.bfloat16)


def pack_energy(values, energy, row):
    block = iota((16, LANES), 1) // 32
    own = iota((16, LANES), 0) // GROUP
    both = values + pltpu.roll(values, 32, 1)
    for j in range(4):
        rows = jnp.where(block == own, both[16 * j : 16 * j + 16], 0.0)
        energy[pl.ds(row + j, 1), :] = jnp.sum(rows, axis=0, keepdims=True)


def table_kernel(windows, nfreq, amplitude, own, place, *refs):
    pays, refs = refs[:2], refs[2:]
    if own:
        cross, inline, observed, mask, updated, energy, matching = refs[:7]
        pay, hb, acc, weights = refs[7:]
    else:
        cross, inline, observed, mask, updated, energy = refs[6:12]
        pay, hb, acc, weights = refs[12:]
    win, first = place[0], place[2]
    many = pay.shape[0]
    half = pay.shape[2] - 8
    freqs = half // 2
    groups = freqs // GROUP
    base = half

    def window(n):
        return win if own else lax.rem(win + 1 + n, windows)

    for n in range(many):
        for s in range(2):
            pay[n, s] = pays[s][...] if pays[s].shape == pay.shape[2:] else pays[s][window(n)]

    def pairing(n, s):
        index = pay[n, s, base + 4 : base + 5, 384:512].astype(jnp.int32)
        index = jnp.where(window(n) > 0, index, iota((1, LANES), 1))
        return (iota((LANES, LANES), 0) == index).astype(jnp.float32)

    if own:
        for s in range(2):
            matching[s] = pairing(0, s)

    def align(n, _):
        n, s = n // 2, n % 2
        hot = pairing(n, s)
        dot = functools.partial(
            lax.dot_general,
            dimension_numbers=(((1,), (1,)), ((), ())),
            precision=HIGHEST,
            preferred_element_type=jnp.float32,
        )
        pay[n, s, 0:half, 0:LANES] = dot(pay[n, s, 0:half, 0:LANES], hot)
        geo = dot(pay[n, s, base : base + 8, 256:384], hot)
        pay[n, s, base : base + 1, 256:384] = geo[0:1]
        pay[n, s, base + 4 : base + 5, 256:384] = geo[4:5]
        here = dot(pay[n, s, base : base + 8, 384:512], hot)
        pay[n, s, base : base + 1, 384:512] = here[0:1]
        return 0

    lax.fori_loop(0, 2 * many, align, 0)

    for s in range(2):
        for h in range(freqs // 8):
            low, high = doubled(pay[0, s, base : base + 8, h * LANES : (h + 1) * LANES])
            weights[s, 2 * h] = low * amplitude
            weights[s, 2 * h + 1] = high * amplitude

    sub = iota((8, LANES), 0)
    delta = 0.75 / nfreq
    start = first.astype(jnp.float32)
    scale0 = 0.25 + 0.75 * ((start + 0.5) / nfreq)
    group_scale0 = 0.25 + 0.75 * ((start + (sub % GROUP).astype(jnp.float32) + 0.5) / nfreq)
    odd_cross = (2 * sub - (PY - 1)).astype(jnp.float32)
    odd_inline = (2 * (2 * (sub // GROUP) - (PX - 1))).astype(jnp.float32)

    def strip_tables(n, _):
        n, s = n // 2, n % 2
        w = window(n)
        for t in range(4):
            off = pl.multiple_of(s * 512 + t * LANES, LANES)
            sl = pl.ds(off, LANES)
            g0 = pay[n, s, base + t : base + t + 1, 256:384]
            g1 = pay[n, s, base + 4 + t : base + 5 + t, 256:384]
            here = jnp.broadcast_to(pay[n, s, base + t : base + t + 1, 384:512], (8, LANES))
            mask[w, :, sl] = here
            now = half_turns((scale0 * g1) * odd_cross)
            more = half_turns((delta * g1) * odd_cross)
            g1b = jnp.broadcast_to(g1, (8, LANES))
            rot = half_turns((scale0 * g1b) * 16.0)
            rot_more = half_turns((delta * g1b) * 16.0)
            for f in range(freqs):
                v0 = now
                v1 = times(v0, rot)
                v2 = times(v1, rot)
                v3 = times(v2, rot)
                row = (f % GROUP) * 64
                for part in range(2):
                    cross[w, f // GROUP, row + 32 * part : row + 32 * part + 16, sl] = (
                        jnp.concatenate([v0[part], v1[part]], axis=0).astype(jnp.bfloat16)
                    )
                    cross[w, f // GROUP, row + 32 * part + 16 : row + 32 * part + 32, sl] = (
                        jnp.concatenate([v2[part], v3[part]], axis=0).astype(jnp.bfloat16)
                    )
                if f + 1 < freqs:
                    now = times(now, more)
                    rot = times(rot, rot_more)
            now = half_turns((group_scale0 * g0) * odd_inline)
            more = half_turns((GROUP * delta * g0) * odd_inline)
            rot = half_turns((group_scale0 * g0) * 8.0)
            rot_more = half_turns((GROUP * delta * jnp.broadcast_to(g0, (8, LANES))) * 8.0)
            for g in range(groups):
                v = now
                for i in range(PX // 4):
                    u = times(v, rot)
                    cv = weights[s, g, :, 8 * i + t : 8 * i + t + 1]
                    cu = weights[s, g, :, 8 * i + 4 + t : 8 * i + 5 + t]
                    for part in range(2):
                        row = part * PX * GROUP + 16 * i
                        inline[w, g, row : row + 16, sl] = jnp.concatenate(
                            [v[part] * cv, u[part] * cu], axis=0
                        ).astype(jnp.bfloat16)
                    if i + 1 < PX // 4:
                        v = times(u, rot)
                if g + 1 < groups:
                    now = times(now, more)
                    rot = times(rot, rot_more)
        for c in range(2):
            for h in range(freqs // 8):
                for t in range(4):
                    sl = pl.ds(pl.multiple_of(s * 512 + t * LANES, LANES), LANES)
                    here = jnp.broadcast_to(
                        pay[n, s, base + t : base + t + 1, 384:512], (8, LANES)
                    )
                    rows = here * pay[
                        n, s, c * freqs + 8 * h : c * freqs + 8 * h + 8, t * LANES : (t + 1) * LANES
                    ]
                    low, high = doubled(rows)
                    observed[c, w, 2 * h, :, sl] = low
                    observed[c, w, 2 * h + 1, :, sl] = high
        return 0

    lax.fori_loop(0, 2 * many, strip_tables, 0)

    low_rows, first_lanes, sign = fold_masks()
    rows = PX * GROUP
    acc[...] = jnp.zeros_like(acc)

    def first_group(n, _):
        g, n = n % groups, n // groups
        w = window(n)
        for tile in range(8):
            sl = slice(tile * LANES, (tile + 1) * LANES)
            weigh(
                inline, w, g, tile, -observed[0, w, g, :, sl], -observed[1, w, g, :, sl], hb.at[n]
            )
        top, bottom = project_group(hb[n], cross[w, g], low_rows, first_lanes, sign)
        top, bottom = -step_length * top, -step_length * bottom
        updated[w, g, :rows] = top
        updated[w, g, rows:] = bottom
        acc[n] += top * top
        return 0

    lax.fori_loop(0, many * groups, first_group, 0, unroll=True)
    for n in range(many):
        pack_energy(acc[n], energy, window(n) * 4)


def spread_factor(energies, threshold, factor, windows, nfreq):
    total = energies[0][...]
    for e in energies[1:]:
        total = total + e[...]
    limit = jnp.concatenate([threshold[...]] * windows, axis=0)
    packed = jnp.maximum(0.0, 1.0 - limit / jnp.sqrt(total / nfreq + epsilon))
    block = iota((8, LANES), 1) // 32
    own = iota((8, LANES), 0) // GROUP
    for w in range(windows):
        for j in range(4):
            row = jnp.broadcast_to(packed[w * 4 + j : w * 4 + j + 1], (8, LANES))
            for k in range(2):
                y = jnp.where(block == own + 2 * k, row, 0.0)
                y = y + pltpu.roll(y, 32, 1)
                y = y + pltpu.roll(y, 64, 1)
                factor[w, 16 * j + 8 * k : 16 * j + 8 * k + 8, :] = y


def mixing_masks():
    rows = iota((2 * PX * GROUP, LANES), 0) % GROUP
    lanes = iota((2 * PX * GROUP, LANES), 1) // 64
    return rows == lanes, rows == lanes + 2


def scaled(updated, factor, w, g):
    rows = PX * GROUP
    shrink = factor[w]
    return updated[w, g, :rows] * shrink, updated[w, g, rows:] * shrink


def predict_group(current, cross, inline, w, g, masks):
    m = jnp.concatenate(current, axis=0)
    mixing = jnp.concatenate(
        [jnp.where(masks[0], m, 0.0), jnp.where(masks[1], m, 0.0)], axis=1
    ).astype(jnp.bfloat16)
    rows = PX * GROUP
    out = []
    for pair in range(4):
        part = jnp.dot(
            mixing,
            cross[w, g, :, pair * 256 : (pair + 1) * 256],
            preferred_element_type=jnp.float32,
        )
        for k in range(2):
            tile = 2 * pair + k
            sl = slice(tile * LANES, (tile + 1) * LANES)
            p_re = p_im = None
            for i in range(rows // 16):
                a_re = inline[w, g, 16 * i : 16 * i + 16, sl].astype(jnp.float32)
                a_im = inline[w, g, rows + 16 * i : rows + 16 * i + 16, sl].astype(jnp.float32)
                b_re = part[16 * i : 16 * i + 16, k * LANES : (k + 1) * LANES]
                b_im = part[rows + 16 * i : rows + 16 * i + 16, k * LANES : (k + 1) * LANES]
                re = a_re * b_re - a_im * b_im
                im = a_re * b_im + a_im * b_re
                p_re = re if p_re is None else p_re + re
                p_im = im if p_im is None else p_im + im
            p_re = p_re[:8] + p_re[8:]
            p_im = p_im[:8] + p_im[8:]
            out.append((p_re + pltpu.roll(p_re, 4, 0), p_im + pltpu.roll(p_im, 4, 0)))
    return out


def blend(predicted, windows):
    ramp = (iota((8, LANES), 1).astype(jnp.float32) + 0.5) / LANES
    for w in range(windows - 1):
        for s in range(2):
            lower, upper = predicted[w][4 * s + 3], predicted[w + 1][4 * s]
            both = tuple((1.0 - ramp) * lower[c] + ramp * upper[c] for c in range(2))
            predicted[w][4 * s + 3] = both
            predicted[w + 1][4 * s] = both
    return predicted


def step_kernel(windows, nfreq, count, *refs):
    energies = refs[:count]
    threshold, updated, cross, inline, observed, mask = refs[count : count + 6]
    new, energy, factor, hb, acc = refs[count + 6 :]
    spread_factor(energies, threshold, factor, windows, nfreq)
    masks = mixing_masks()
    low_rows, first_lanes, sign = fold_masks()
    rows = PX * GROUP
    acc[...] = jnp.zeros_like(acc)

    def one_group(g, _):
        predicted = []
        for w in range(windows):
            current = scaled(updated, factor, w, g)
            predicted.append(predict_group(current, cross, inline, w, g, masks))
        predicted = blend(predicted, windows)
        for w in range(windows):
            for tile in range(8):
                sl = slice(tile * LANES, (tile + 1) * LANES)
                here = mask[w, :, sl]
                p_re, p_im = predicted[w][tile]
                r_re = here * p_re - observed[0, w, g, :, sl]
                r_im = here * p_im - observed[1, w, g, :, sl]
                weigh(inline, w, g, tile, r_re, r_im, hb.at[w])
            top, bottom = project_group(hb[w], cross[w, g], low_rows, first_lanes, sign)
            current = scaled(updated, factor, w, g)
            top = current[0] - step_length * top
            bottom = current[1] - step_length * bottom
            new[w, g, :rows] = top
            new[w, g, rows:] = bottom
            acc[w] += top * top
        return 0

    lax.fori_loop(0, updated.shape[1], one_group, 0, unroll=True)
    for w in range(windows):
        pack_energy(acc[w], energy, 4 * w)


def final_kernel(windows, nfreq, count, place, *refs):
    energies = refs[:count]
    threshold, updated, cross, inline, matching = refs[count : count + 5]
    swap, keep, factor = refs[count + 5 :]
    win = place[0]
    spread_factor(energies, threshold, factor, windows, nfreq)
    masks = mixing_masks()
    rows = PX * GROUP
    low = iota((8, LANES), 0) < 4
    even = (iota((rows, LANES), 1) // 32) % 2 == 0
    block = iota((8, LANES), 1) // 32
    own = iota((8, LANES), 0) // GROUP

    def pick(values):
        out = values[0]
        for w in range(1, windows):
            out = jnp.where(win == w, values[w], out)
        return out

    def two_groups(h, _):
        coeffs, traces = [], []
        for k in range(2):
            g = 2 * h + k
            current = [scaled(updated, factor, w, g) for w in range(windows)]
            predicted = blend(
                [predict_group(current[w], cross, inline, w, g, masks) for w in range(windows)],
                windows,
            )
            traces.append(
                [[pick([predicted[w][t][c] for w in range(windows)]) for t in range(8)] for c in range(2)]
            )
            top = pick([current[w][0] for w in range(windows)])
            bottom = pick([current[w][1] for w in range(windows)])
            parts = (jnp.where(even, top, bottom), jnp.where(even, bottom, -top))
            lines = []
            for m in parts:
                line = []
                for j in range(4):
                    v = jnp.where(block == own, m[16 * j : 16 * j + 8], 0.0) + jnp.where(
                        block == own + 2, m[16 * j + 8 : 16 * j + 16], 0.0
                    )
                    line.append(v + pltpu.roll(v, 4, 0))
                lines.append(line)
            coeffs.append(lines)
        sl = pl.ds(pl.multiple_of(8 * h, 8), 8)
        for c in range(2):
            for j in range(4):
                lanes = slice(j * LANES, (j + 1) * LANES)
                both = jnp.where(low, coeffs[0][c][j], coeffs[1][c][j])
                swap[0, c, sl, lanes] = both
                keep[0, c, sl, lanes] = both
            for t in range(8):
                lanes = slice((t % 4) * LANES, (t % 4 + 1) * LANES)
                out = keep if t < 4 else swap
                out[1, c, sl, lanes] = jnp.where(low, traces[0][c][t], traces[1][c][t])
        return 0

    lax.fori_loop(0, updated.shape[1] // 2, two_groups, 0, unroll=True)
    for s, out in enumerate((keep, swap)):
        for c in range(2):
            out[1, c, :, :LANES] = jnp.dot(
                out[1, c, :, :LANES],
                matching[s],
                precision=HIGHEST,
                preferred_element_type=jnp.float32,
            )


VM = pl.BlockSpec(memory_space=pltpu.VMEM)
HB = pl.BlockSpec(memory_space=pltpu.HBM)
SM = pl.BlockSpec(memory_space=pltpu.SMEM)


def params(windows):
    return pltpu.CompilerParams(vmem_limit_bytes=(16 if windows == 2 else 40) * 1024 * 1024)


def shape(*dims, dtype=jnp.float32):
    return jax.ShapeDtypeStruct(dims, dtype)


def sum_parts(energy):
    swap = [(0, 1), (1, 0)]
    energy = energy + lax.ppermute(energy, "rep", swap)
    size = lax.axis_size("freq")
    if size & (size - 1):
        return [lax.psum(energy, "freq")]
    axes = ("freq", "rep")

    def crossed(k):
        return [(2 * i + r, 2 * (i ^ k) + 1 - r) for i in range(size) for r in range(2)]

    if size <= 4:
        return [energy] + [lax.ppermute(energy, axes, crossed(k)) for k in range(1, size)]
    k = 1
    while k < size:
        energy = energy + lax.ppermute(energy, axes, crossed(k))
        k *= 2
    return [energy]


def per_device(recorded, geometry, present, intersection_index, pattern, group_scale):
    frequencies = recorded.shape[1]
    traces = recorded.shape[3]
    windows = lax.axis_size("win")
    nfreq = frequencies * lax.axis_size("freq")
    half = frequencies // 2
    groups = half // GROUP
    amplitude = 1.0 / math.sqrt(traces * lax.axis_size("rep"))
    win, rep = lax.axis_index("win"), lax.axis_index("rep")
    first = lax.axis_index("freq") * frequencies + rep * half
    place = jnp.stack([win, rep, first]).astype(jnp.int32)
    width = 2 * traces
    swap = [(0, 1), (1, 0)]

    payload = shape(2 * half + 8, traces)
    turned = jnp.transpose(pattern, (1, 2, 0))
    sources = (recorded, geometry, present, intersection_index, turned)
    keep, send = pl.pallas_call(
        pack_kernel,
        out_shape=(payload, payload),
        in_specs=[SM] + [HB] * 5,
        out_specs=(VM, VM),
        scratch_shapes=[pltpu.VMEM(x.shape, x.dtype) for x in sources]
        + [
            pltpu.SemaphoreType.DMA((5,)),
            pltpu.VMEM((turned.shape[0] * turned.shape[1], frequencies), jnp.float32),
        ],
        compiler_params=pltpu.CompilerParams(vmem_limit_bytes=60 * 1024 * 1024),
        name="pack",
    )(place, *sources)
    received = lax.ppermute(send, "rep", swap)
    if windows == 2:
        diagonal = [(2 * i + r, 2 * (1 - i) + 1 - r) for i in range(2) for r in range(2)]
        others = [lax.ppermute(keep, "win", swap), lax.ppermute(send, ("win", "rep"), diagonal)]
    else:
        others = [lax.all_gather(keep, "win"), lax.all_gather(received, "win")]

    rows = 2 * PX * GROUP
    state = shape(windows, groups, rows, LANES)
    energy_shape = shape(4 * windows, LANES)
    tables = (
        shape(windows, groups, 2 * PY * GROUP, width, dtype=jnp.bfloat16),
        shape(windows, groups, rows, width, dtype=jnp.bfloat16),
        shape(2, windows, groups, 8, width),
        shape(windows, 8, width),
        state,
        energy_shape,
    )

    def scratch(many):
        return [
            pltpu.VMEM((many, rows, width), jnp.bfloat16),
            pltpu.VMEM((many, rows // 2, LANES), jnp.float32),
        ]

    def build(own, inputs, many):
        return pl.pallas_call(
            functools.partial(table_kernel, windows, nfreq, amplitude, own),
            out_shape=tables + ((shape(2, LANES, LANES),) if own else ()),
            in_specs=[SM] + [VM] * (len(inputs)),
            out_specs=(VM,) * (len(tables) + own),
            scratch_shapes=[pltpu.VMEM((many, 2, 2 * half + 8, traces), jnp.float32)]
            + scratch(many)
            + [pltpu.VMEM((2, groups, 8, LANES), jnp.float32)],
            input_output_aliases={} if own else {3 + n: n for n in range(len(tables))},
            compiler_params=params(windows),
            cost_estimate=pl.CostEstimate(flops=4 * 10**9, bytes_accessed=0, transcendentals=0),
            name="tables",
        )(place, *inputs)

    *mine, matching = build(True, [keep, received], 1)
    cross, inline, observed, mask, updated, energy = mine
    if windows > 1:
        cross, inline, observed, mask, updated, energy = build(
            False, others + list(mine), windows - 1
        )

    threshold = group_scale.reshape(4, LANES)
    factor_scratch = pltpu.VMEM((windows, rows // 2, LANES), jnp.float32)
    for _ in range(ITERS - 1):
        energies = sum_parts(energy)
        updated, energy = pl.pallas_call(
            functools.partial(step_kernel, windows, nfreq, len(energies)),
            out_shape=(state, energy_shape),
            in_specs=[VM] * (len(energies) + 6),
            out_specs=(VM, VM),
            scratch_shapes=[factor_scratch] + scratch(windows),
            compiler_params=params(windows),
            name="step",
        )(*energies, threshold, updated, cross, inline, observed, mask)
    energies = sum_parts(energy)
    halves = shape(2, 2, half, traces)
    theirs, mine = pl.pallas_call(
        functools.partial(final_kernel, windows, nfreq, len(energies)),
        out_shape=(halves, halves),
        in_specs=[SM] + [VM] * (len(energies) + 5),
        out_specs=(VM, VM),
        scratch_shapes=[factor_scratch],
        compiler_params=params(windows),
        name="final",
    )(place, *energies, threshold, updated, cross, inline, matching)
    theirs = lax.ppermute(theirs, "rep", swap)
    out = shape(2, frequencies, 1, traces)
    return pl.pallas_call(
        unpack_kernel,
        out_shape=(out, out),
        in_specs=[SM, VM, VM],
        out_specs=(VM, VM),
        compiler_params=params(windows),
        name="unpack",
    )(place, mine, theirs)


def solution(mesh):
    return jax.shard_map(
        per_device,
        mesh=mesh,
        in_specs=(
            P(None, "freq", ("dom", "win"), "rep"),
            P(None, ("dom", "win"), "rep"),
            P(("dom", "win"), "rep"),
            P(("dom", "win"), "rep", None),
            P("freq", None, "rep"),
            P(),
        ),
        out_specs=(P(None, "freq", ("dom", "win"), None), P(None, "freq", ("dom", "win"), "rep")),
        check_vma=False,
    )
```

```python
import functools
import math

import jax
import jax.numpy as jnp
from jax import lax
from jax.experimental import pallas as pl
from jax.experimental.pallas import tpu as pltpu
from jax.sharding import PartitionSpec as P

PX = 16
PY = 32
SPB = 64
OBS = 128
ITERS = 3
LANES = 128
GROUP = 8
HALF = PX * GROUP
FOLD = PY // 2
SPAN = 2 * FOLD

step_length = 1.0
epsilon = 1e-06
HIGHEST = lax.Precision.HIGHEST


def iota(shape, dim):
    return lax.broadcasted_iota(jnp.int32, shape, dim)


def half_turns(y):
    quarter = jnp.floor(2.0 * y + 0.5)
    r = y - 0.5 * quarter
    q = quarter.astype(jnp.int32)
    r2 = r * r
    pi = math.pi
    sine = r * (
        pi
        + r2
        * (
            -(pi**3) / 6
            + r2 * (pi**5 / 120 + r2 * (-(pi**7) / 5040 + r2 * (pi**9 / 362880)))
        )
    )
    cosine = 1.0 + r2 * (
        -(pi**2) / 2 + r2 * (pi**4 / 24 + r2 * (-(pi**6) / 720 + r2 * (pi**8 / 40320)))
    )
    odd = (q & 1) == 1
    c = jnp.where(odd, sine, cosine)
    s = jnp.where(odd, cosine, sine)
    c = jnp.where(((q + 1) & 2) != 0, -c, c)
    s = jnp.where((q & 2) != 0, s, -s)
    return c, s


def rounded(x):
    return x.astype(jnp.bfloat16).astype(jnp.float32)


def times(p, q):
    return p[0] * q[0] - p[1] * q[1], p[0] * q[1] + p[1] * q[0]


def pack_kernel(
    recorded, geometry, present, intersection, pattern, keep, send, *scratch
):
    sources = (recorded, geometry, present, intersection, pattern)
    local, sems, turned = scratch[:5], scratch[5], scratch[6]
    copies = [
        pltpu.make_async_copy(src, dst, sems.at[n]) for n, (src, dst) in enumerate(zip(sources, local))
    ]
    for copy in copies:
        copy.start()
    for copy in copies:
        copy.wait()
    recorded, geometry, present, intersection, pattern = local
    frequencies = recorded.shape[1]
    half = frequencies // 2
    rep = lax.axis_index("rep")
    blocks, span = pattern.shape[:2]
    for i in range(blocks):
        turned[span * i : span * (i + 1), :] = pattern[i].astype(jnp.float32)
    base = 2 * half
    for out, part in ((keep, rep), (send, 1 - rep)):
        for c in range(2):
            out[c * half : (c + 1) * half, :] = recorded[c, pl.ds(part * half, half), 0, :]
        out[base : base + 8, :] = jnp.zeros((8, out.shape[1]), jnp.float32)
        chosen = iota((half, frequencies), 0) + part * half == iota((half, frequencies), 1)
        pat = lax.dot_general(
            chosen.astype(jnp.float32),
            turned[...],
            (((1,), (1,)), ((), ())),
            preferred_element_type=jnp.float32,
        )
        for h in range(half // 8):
            out[base : base + 8, h * LANES : h * LANES + pat.shape[1]] = pat[8 * h : 8 * h + 8]
        for t in range(4):
            sl = slice(t * LANES, (t + 1) * LANES)
            out[base + t : base + t + 1, 256:384] = geometry[0, :, sl]
            out[base + 4 + t : base + 5 + t, 256:384] = geometry[1, :, sl]
            out[base + t : base + t + 1, 384:512] = present[:, sl].astype(jnp.float32)
        out[base + 4 : base + 5, 384:512] = intersection[0].astype(jnp.float32)


def unpack_kernel(mine, theirs, coefficients, reconstruction):
    rep = lax.axis_index("rep")
    half = mine.shape[2]
    for n, out in enumerate((coefficients, reconstruction)):
        for c in range(2):
            out[c, pl.ds(rep * half, half), 0, :] = mine[n, c]
            out[c, pl.ds((1 - rep) * half, half), 0, :] = theirs[n, c]


def low_half(dims):
    return (iota(dims, 1) // FOLD) % 2 == 0


def swapped(values):
    return pltpu.roll(values, FOLD, 1)


def side_by_side(ref, w, g, first, count):
    return jnp.concatenate([ref[w][g, first + n] for n in range(count)], axis=1)


def project_group(hb, cross, w, g, masks, sign):
    tiles = hb.shape[0]
    g = lax.dot_general(
        jnp.concatenate([hb[n] for n in range(tiles)], axis=1),
        side_by_side(cross, w, g, 0, tiles),
        (((1,), (1,)), ((), ())),
        preferred_element_type=jnp.float32,
    )
    g = jnp.where(masks[0], g[:, :LANES], jnp.where(masks[1], g[:, LANES:], 0.0))
    g = g + pltpu.roll(g, 32, 1)
    g = g + pltpu.roll(g, 64, 1)
    top, bottom = g[:HALF], sign * swapped(g[HALF:])
    return top + bottom, top - bottom


def group_masks():
    rows = iota((2 * HALF, LANES), 0) % GROUP
    lanes = iota((2 * HALF, LANES), 1) // SPAN
    return rows == lanes, rows == lanes + 4


def half_sign():
    return jnp.where(low_half((HALF, LANES)), 1.0, -1.0)


def weigh(inline, g, tile, r_re, r_im, hb):
    sl = pl.ds(tile * LANES, LANES)
    for i in range(HALF // 16):
        rows = slice(16 * i, 16 * i + 16)
        low = slice(HALF + 16 * i, HALF + 16 * i + 16)
        a_re = inline[g, rows, sl]
        a_im = inline[g, low, sl]
        rr = jnp.concatenate([r_re, r_re], axis=0)
        ri = jnp.concatenate([r_im, r_im], axis=0)
        hb[tile, rows, :] = (a_re * rr + a_im * ri).astype(jnp.bfloat16)
        hb[tile, low, :] = (a_re * ri - a_im * rr).astype(jnp.bfloat16)


def pack_energy(values, energy, row):
    both = values + swapped(values)
    both = jnp.where(low_half((HALF, LANES)), both[:HALF], both[HALF:])
    block = iota((GROUP, LANES), 1) // SPAN
    for j in range(4):
        total = None
        for q in range(4):
            a = 4 * j + q
            part = jnp.where(block == q, both[GROUP * a : GROUP * (a + 1)], 0.0)
            total = part if total is None else total + part
        energy[pl.ds(row + j, 1), :] = jnp.sum(total, axis=0, keepdims=True)


def table_kernel(windows, nfreq, amplitude, own, *refs):
    pays, refs = refs[:2], refs[2:]
    extra, refs = refs[0], refs[1:]
    cross, inline, observed, mask, updated, energy, *refs = refs
    if own:
        matching, threshold, pay, hb, acc = refs
        lane = iota((LANES, LANES), 1)
        at = lane % SPAN
        source = jnp.where(at < FOLD, lane, lane + PY - 1 + FOLD - 2 * at)
        order = (iota((LANES, LANES), 0) == source).astype(jnp.float32)
        threshold[...] = jnp.dot(
            extra[...], order, precision=HIGHEST, preferred_element_type=jnp.float32
        )
    else:
        pay, hb, acc = refs
        energy[0:4, :] = extra[...]
    many = pay.shape[0]
    half = pay.shape[2] - 8
    freqs = half // 2
    win = lax.axis_index("win")
    first = (2 * lax.axis_index("freq") + lax.axis_index("rep")) * freqs
    groups = freqs // GROUP
    base = half

    def window(n):
        return win if own else lax.rem(win + 1 + n, windows)

    for n in range(many):
        for s in range(2):
            pay[n, s] = pays[s][...] if pays[s].shape == pay.shape[2:] else pays[s][window(n)]

    def pairing(n, s):
        index = pay[n, s, base + 4 : base + 5, 384:512].astype(jnp.int32)
        index = jnp.where(window(n) > 0, index, iota((1, LANES), 1))
        return (iota((LANES, LANES), 0) == index).astype(jnp.float32)

    if own:
        for s in range(2):
            matching[s] = pairing(0, s)

    def align(n, _):
        n, s = n // 2, n % 2
        hot = pairing(n, s)
        dot = functools.partial(
            lax.dot_general,
            dimension_numbers=(((1,), (1,)), ((), ())),
            precision=HIGHEST,
            preferred_element_type=jnp.float32,
        )
        pay[n, s, 0:half, 0:LANES] = dot(pay[n, s, 0:half, 0:LANES], hot)
        geo = dot(pay[n, s, base : base + 8, 256:384], hot)
        pay[n, s, base : base + 1, 256:384] = geo[0:1]
        pay[n, s, base + 4 : base + 5, 256:384] = geo[4:5]
        here = dot(pay[n, s, base : base + 8, 384:512], hot)
        pay[n, s, base : base + 1, 384:512] = here[0:1]
        return 0

    lax.fori_loop(0, 2 * many, align, 0)

    sub = iota((8, LANES), 0)
    delta = 0.75 / nfreq
    start = first.astype(jnp.float32)
    scale0 = 0.25 + 0.75 * ((start + 0.5) / nfreq)
    odd_cross = (2 * sub - (PY - 1)).astype(jnp.float32)

    def strip_tables(n, _):
        n, s = n // 2, n % 2
        for t in range(4):
            off = pl.multiple_of(s * 512 + t * LANES, LANES)
            sl = pl.ds(off, LANES)
            g0 = pay[n, s, base + t : base + t + 1, 256:384]
            g1 = pay[n, s, base + 4 + t : base + 5 + t, 256:384]
            here = jnp.broadcast_to(pay[n, s, base + t : base + t + 1, 384:512], (8, LANES))
            mask[n, :, sl] = here
            now = half_turns((scale0 * g1) * odd_cross)
            more = half_turns((delta * g1) * odd_cross)
            g1b = jnp.broadcast_to(g1, (8, LANES))
            rot = half_turns((scale0 * g1b) * 16.0)
            rot_more = half_turns((delta * g1b) * 16.0)
            for f in range(freqs):
                v0 = now
                v1 = times(v0, rot)
                row = (f % GROUP) * SPAN
                for part in range(2):
                    cross[n, f // GROUP, 4 * s + t, row + FOLD * part : row + FOLD * (part + 1), :] = (
                        jnp.concatenate([v0[part], v1[part]], axis=0).astype(jnp.bfloat16)
                    )
                if f + 1 < freqs:
                    now = times(now, more)
                    rot = times(rot, rot_more)
            for g in range(groups):
                level = start + (sub + g * GROUP).astype(jnp.float32)
                scale = 0.25 + 0.75 * ((level + 0.5) / nfreq)
                v = half_turns((scale * g0) * 2.0)
                rot = half_turns((scale * g0) * 4.0)
                v = (v[0] * amplitude, v[1] * amplitude)
                for a in range(PX // 2, PX, 2):
                    u = times(v, rot)
                    i, mirror = a // 2, (PX - 1 - a) // 2
                    lane = g * LANES + t
                    col = pay[n, s, base : base + 8, lane + 4 * i : lane + 4 * i + 1]
                    other = pay[n, s, base : base + 8, lane + 4 * mirror : lane + 4 * mirror + 1]
                    low = GROUP * (PX - 2 - a)
                    for part in range(2):
                        row = part * HALF
                        inline[n, g, row + GROUP * a : row + GROUP * (a + 2), sl] = (
                            rounded(jnp.concatenate([v[part] * col, u[part] * col], axis=0))
                        )
                        turn = -other if part else other
                        inline[n, g, row + low : row + low + 2 * GROUP, sl] = (
                            rounded(jnp.concatenate([u[part] * turn, v[part] * turn], axis=0))
                        )
                    if a + 2 < PX:
                        v = times(u, rot)
            for c in range(2):
                for g in range(groups):
                    row = c * freqs + GROUP * g
                    observed[n, c, g, :, sl] = (
                        here * pay[n, s, row : row + GROUP, t * LANES : (t + 1) * LANES]
                    )
        return 0

    lax.fori_loop(0, 2 * many, strip_tables, 0)

    masks, sign = group_masks(), half_sign()
    acc[...] = jnp.zeros_like(acc)

    def first_group(k, _):
        g, n = k % groups, k // groups
        buffer = hb.at[k % hb.shape[0]]
        for tile in range(8):
            sl = slice(tile * LANES, (tile + 1) * LANES)
            r_re, r_im = -observed[n, 0, g, :, sl], -observed[n, 1, g, :, sl]
            weigh(inline.at[n], g, tile, r_re, r_im, buffer)
        slopes = project_group(buffer, [cross.at[n]], 0, g, masks, sign)
        for part, slope in enumerate(slopes):
            rows = slice(part * HALF, (part + 1) * HALF)
            value = -step_length * slope
            updated[n, g, rows] = value
            acc[n, rows] += value * value
        return 0

    lax.fori_loop(0, many * groups, first_group, 0, unroll=True)
    for n in range(many):
        pack_energy(acc[n], energy, 4 * (n + (not own)))


def spread_factor(energies, threshold, factor, windows, nfreq):
    total = energies[0][...]
    for e in energies[1:]:
        total = total + e[...]
    limit = jnp.concatenate([threshold[...]] * windows, axis=0)
    packed = jnp.maximum(0.0, 1.0 - limit / jnp.sqrt(total / nfreq + epsilon))
    block = iota((8, LANES), 1) // SPAN
    low = low_half((8, LANES))
    for w in range(windows):
        for a in range(PX):
            row = w * 4 + a // 4
            y = jnp.where(block == a % 4, jnp.broadcast_to(packed[row : row + 1], (8, LANES)), 0.0)
            y = y + pltpu.roll(y, 32, 1)
            y = y + pltpu.roll(y, 64, 1)
            turned = swapped(y)
            factor[w, GROUP * a : GROUP * (a + 1), :] = jnp.where(low, y, turned)
            factor[w, HALF + GROUP * a : HALF + GROUP * (a + 1), :] = jnp.where(low, turned, y)


def mix(current, masks, sign):
    first, second = current[:HALF], current[HALF:]
    m = jnp.concatenate([first + second, swapped(sign * (first - second))], axis=0)
    return jnp.concatenate(
        [jnp.where(masks[0], m, 0.0), jnp.where(masks[1], m, 0.0)], axis=1
    ).astype(jnp.bfloat16)


def predict_tile(inline, part):
    p_re = p_im = None
    for i in range(HALF // 16):
        a_re = inline[16 * i : 16 * i + 16]
        a_im = inline[HALF + 16 * i : HALF + 16 * i + 16]
        b_re = part[16 * i : 16 * i + 16]
        b_im = part[HALF + 16 * i : HALF + 16 * i + 16]
        re = a_re * b_re - a_im * b_im
        im = a_re * b_im + a_im * b_re
        p_re = re if p_re is None else p_re + re
        p_im = im if p_im is None else p_im + im
    return p_re[:8] + p_re[8:], p_im[:8] + p_im[8:]


def predict_strip(mixing, cross, inline, w, g, s):
    out = []
    for first in (4 * s, 4 * s + 2):
        part = jnp.dot(
            mixing, side_by_side(cross, w, g, first, 2), preferred_element_type=jnp.float32
        )
        for k in range(2):
            table = inline[w][g, :, (first + k) * LANES : (first + k + 1) * LANES]
            out.append(predict_tile(table, part[:, k * LANES : (k + 1) * LANES]))
    return out


def predict_edges(mixing, cross, inline, w, g, tile):
    out = []
    for s in range(2):
        sl = slice((tile + 4 * s) * LANES, (tile + 4 * s + 1) * LANES)
        part = jnp.dot(mixing, cross[w][g, tile + 4 * s], preferred_element_type=jnp.float32)
        out.append(predict_tile(inline[w][g, :, sl], part))
    return out


def join(lower, upper):
    ramp = (iota((8, LANES), 1).astype(jnp.float32) + 0.5) / LANES
    return tuple((1.0 - ramp) * lower[c] + ramp * upper[c] for c in range(2))


def both_orders(own, others, windows):
    return [own.at[0]] + [others.at[n] for n in range(windows - 1)]


def blend(predicted, windows, win):
    joined = {}
    for n in range(windows if windows > 1 else 0):
        above = (n + 1) % windows
        apart = lax.rem(win + n, windows) == windows - 1
        trail, lead = predicted[n][3], predicted[above][0]
        both = join(trail, lead)
        joined[n, 3] = tuple(jnp.where(apart, trail[c], both[c]) for c in range(2))
        joined[above, 0] = tuple(jnp.where(apart, lead[c], both[c]) for c in range(2))
    for (n, tile), value in joined.items():
        predicted[n][tile] = value
    return predicted


def step_kernel(windows, nfreq, count, *refs):
    energies, refs = refs[:count], refs[count:]
    threshold, refs = refs[0], refs[1:]
    if windows > 1:
        cross, inline, observed, mask, updated = (
            both_orders(refs[n], refs[5 + n], windows) for n in range(5)
        )
        new = both_orders(refs[10], refs[11], windows)
        energy, factor, hb, acc = refs[12:]
    else:
        cross, inline, observed, mask, updated = ([refs[n].at[0]] for n in range(5))
        new = [refs[5].at[0]]
        energy, factor, hb, acc = refs[6:]
    win = lax.axis_index("win")
    spread_factor(energies, threshold, factor, windows, nfreq)
    masks, sign = group_masks(), half_sign()
    acc[...] = jnp.zeros_like(acc)
    for g in range(updated[0].shape[0]):
        mixing = [mix(updated[w][g] * factor[w], masks, sign) for w in range(windows)]
        buffers = [hb.at[(g * windows + w) % hb.shape[0]] for w in range(windows)]
        for s in range(2):
            predicted = blend(
                [predict_strip(mixing[w], cross, inline, w, g, s) for w in range(windows)],
                windows,
                win,
            )
            for w in range(windows):
                for t in range(4):
                    tile = 4 * s + t
                    sl = slice(tile * LANES, (tile + 1) * LANES)
                    here = mask[w][:, sl]
                    p_re, p_im = predicted[w][t]
                    r_re = here * p_re - observed[w][0, g, :, sl]
                    r_im = here * p_im - observed[w][1, g, :, sl]
                    weigh(inline[w], g, tile, r_re, r_im, buffers[w])
        for w in range(windows):
            slopes = project_group(buffers[w], cross, w, g, masks, sign)
            for part, slope in enumerate(slopes):
                rows = slice(part * HALF, (part + 1) * HALF)
                value = updated[w][g, rows] * factor[w, rows] - step_length * slope
                new[w][g, rows] = value
                acc[w, rows] += value * value
    for w in range(windows):
        pack_energy(acc[w], energy, 4 * w)


def final_kernel(windows, nfreq, count, *refs):
    energies, refs = refs[:count], refs[count:]
    threshold, matching, refs = refs[0], refs[1], refs[2:]
    if windows > 1:
        cross, inline, updated = (both_orders(refs[n], refs[3 + n], windows) for n in range(3))
        refs = refs[6:]
    else:
        cross, inline, updated = ([refs[n].at[0]] for n in range(3))
        refs = refs[3:]
    swap, keep, factor = refs
    win = lax.axis_index("win")
    spread_factor(energies, threshold, factor, windows, nfreq)
    masks, sign = group_masks(), half_sign()
    block = iota((GROUP, LANES), 1) // SPAN
    wide = iota((HALF, LANES), 1) // SPAN
    line, lane = iota((LANES, 2 * LANES), 0), iota((LANES, 2 * LANES), 1)
    b, imag = lane % PY, lane // LANES
    source = jnp.where(b < FOLD, b, SPAN + PY - 1 - b) + FOLD * imag
    value = jnp.where((imag == 1) & (b < FOLD), -1.0, 1.0)
    order = jnp.where(line == source, value, 0.0)

    for g in range(updated[0].shape[0]):
        current = updated[0][g] * factor[0]
        mixing = mix(current, masks, sign)
        traces = [x for s in range(2) for x in predict_strip(mixing, cross, inline, 0, g, s)]
        if windows > 1:
            mixed = [
                mix(updated[w][g] * factor[w], masks, sign) for w in sorted({1, windows - 1})
            ]
            above = predict_edges(mixed[0], cross, inline, 1, g, 0)
            below = predict_edges(mixed[-1], cross, inline, windows - 1, g, 3)
            for s in range(2):
                lead, trail = traces[4 * s], traces[4 * s + 3]
                low, high = join(below[s], lead), join(trail, above[s])
                traces[4 * s] = tuple(jnp.where(win > 0, low[c], lead[c]) for c in range(2))
                traces[4 * s + 3] = tuple(
                    jnp.where(win < windows - 1, high[c], trail[c]) for c in range(2)
                )
        spans = jnp.where(wide == 0, current[:HALF], jnp.where(wide == 1, current[HALF:], 0.0))
        spans = jnp.dot(spans, order, precision=HIGHEST, preferred_element_type=jnp.float32)
        sl = slice(GROUP * g, GROUP * (g + 1))
        for c in range(2):
            for j in range(4):
                lanes = slice(j * LANES, (j + 1) * LANES)
                values = None
                for q in range(4):
                    a = 4 * j + q
                    part = spans[GROUP * a : GROUP * (a + 1), c * LANES : (c + 1) * LANES]
                    part = jnp.where(block == q, part, 0.0)
                    values = part if values is None else values + part
                swap[0, c, sl, lanes] = values
                keep[0, c, sl, lanes] = values
            for t in range(8):
                lanes = slice((t % 4) * LANES, (t % 4 + 1) * LANES)
                out = keep if t < 4 else swap
                out[1, c, sl, lanes] = traces[t][c]
    for s, out in enumerate((keep, swap)):
        for c in range(2):
            out[1, c, :, :LANES] = jnp.dot(
                out[1, c, :, :LANES],
                matching[s],
                precision=HIGHEST,
                preferred_element_type=jnp.float32,
            )


VM = pl.BlockSpec(memory_space=pltpu.VMEM)
HB = pl.BlockSpec(memory_space=pltpu.HBM)


def params(windows):
    return pltpu.CompilerParams(vmem_limit_bytes=(16 if windows <= 2 else 60) * 1024 * 1024)


def shape(*dims, dtype=jnp.float32):
    return jax.ShapeDtypeStruct(dims, dtype)


def sum_parts(energy):
    swap = [(0, 1), (1, 0)]
    energy = energy + lax.ppermute(energy, "rep", swap)
    size = lax.axis_size("freq")
    if size & (size - 1):
        return [lax.psum(energy, "freq")]
    axes = ("freq", "rep")

    def crossed(k):
        return [(2 * i + r, 2 * (i ^ k) + 1 - r) for i in range(size) for r in range(2)]

    if size <= 4:
        return [energy] + [lax.ppermute(energy, axes, crossed(k)) for k in range(1, size)]
    k = 1
    while k < size:
        energy = energy + lax.ppermute(energy, axes, crossed(k))
        k *= 2
    return [energy]


def per_device(recorded, geometry, present, intersection_index, pattern, group_scale):
    frequencies = recorded.shape[1]
    traces = recorded.shape[3]
    windows = lax.axis_size("win")
    nfreq = frequencies * lax.axis_size("freq")
    half = frequencies // 2
    groups = half // GROUP
    amplitude = 1.0 / math.sqrt(traces * lax.axis_size("rep"))
    width = 2 * traces
    swap = [(0, 1), (1, 0)]

    payload = shape(2 * half + 8, traces)
    turned = jnp.transpose(pattern, (1, 2, 0))
    sources = tuple(
        pltpu.with_memory_space_constraint(x, pltpu.HBM)
        for x in (recorded, geometry, present, intersection_index, turned)
    )
    keep, send = pl.pallas_call(
        pack_kernel,
        out_shape=(payload, payload),
        in_specs=[HB] * 5,
        out_specs=(VM, VM),
        scratch_shapes=[pltpu.VMEM(x.shape, x.dtype) for x in sources]
        + [
            pltpu.SemaphoreType.DMA((5,)),
            pltpu.VMEM((turned.shape[0] * turned.shape[1], frequencies), jnp.float32),
        ],
        compiler_params=params(windows),
        name="pack",
    )(*sources)
    received = lax.ppermute(send, "rep", swap)
    if windows == 2:
        diagonal = [(2 * i + r, 2 * (1 - i) + 1 - r) for i in range(2) for r in range(2)]
        others = [lax.ppermute(keep, "win", swap), lax.ppermute(send, ("win", "rep"), diagonal)]
    else:
        others = [lax.all_gather(keep, "win"), lax.all_gather(received, "win")]

    rows = 2 * HALF
    energy_shape = shape(4 * windows, LANES)

    def scratch(many):
        buffers = many * groups if windows <= 2 else windows
        return [
            pltpu.VMEM((buffers, width // LANES, rows, LANES), jnp.bfloat16),
            pltpu.VMEM((many, rows, LANES), jnp.float32),
        ]

    def build(own, inputs):
        many = 1 if own else windows - 1
        out_shape = (
            shape(many, groups, width // LANES, SPAN * GROUP, LANES, dtype=jnp.bfloat16),
            shape(many, groups, rows, width),
            shape(many, 2, groups, GROUP, width),
            shape(many, 8, width),
            shape(many, groups, rows, LANES),
            shape(4, LANES) if own else energy_shape,
        )
        if own:
            out_shape += (shape(2, LANES, LANES), shape(4, LANES))
        return pl.pallas_call(
            functools.partial(table_kernel, windows, nfreq, amplitude, own),
            out_shape=out_shape,
            in_specs=[VM] * len(inputs),
            out_specs=(VM,) * len(out_shape),
            scratch_shapes=[pltpu.VMEM((many, 2, 2 * half + 8, traces), jnp.float32)]
            + scratch(many),
            compiler_params=params(windows),
            cost_estimate=pl.CostEstimate(flops=4 * 10**9, bytes_accessed=0, transcendentals=0),
            name="tables",
        )(*inputs)

    *tables, updated, energy, matching, threshold = build(
        True, [keep, received, group_scale.reshape(4, LANES)]
    )
    tables, states = [tables], [updated]
    if windows > 1:
        *others, updated, energy = build(False, others + [energy])
        tables.append(others)
        states.append(updated)

    factor_scratch = pltpu.VMEM((windows, rows, LANES), jnp.float32)
    for _ in range(ITERS - 1):
        inputs = [threshold]
        for table, state in zip(tables, states):
            inputs += [*table, state]
        energies = sum_parts(energy)
        *states, energy = pl.pallas_call(
            functools.partial(step_kernel, windows, nfreq, len(energies)),
            out_shape=tuple(shape(*x.shape) for x in states) + (energy_shape,),
            in_specs=[VM] * (len(energies) + len(inputs)),
            out_specs=(VM,) * (len(states) + 1),
            scratch_shapes=[factor_scratch] + scratch(windows),
            compiler_params=params(windows),
            name="step",
        )(*energies, *inputs)
    energies = sum_parts(energy)
    halves = shape(2, 2, half, traces)
    inputs = [threshold, matching]
    for table, state in zip(tables, states):
        inputs += [*table[:2], state]
    theirs, mine = pl.pallas_call(
        functools.partial(final_kernel, windows, nfreq, len(energies)),
        out_shape=(halves, halves),
        in_specs=[VM] * (len(energies) + len(inputs)),
        out_specs=(VM, VM),
        scratch_shapes=[factor_scratch],
        compiler_params=params(windows),
        name="final",
    )(*energies, *inputs)
    theirs = lax.ppermute(theirs, "rep", swap)
    out = shape(2, frequencies, 1, traces)
    return pl.pallas_call(
        unpack_kernel,
        out_shape=(out, out),
        in_specs=[VM, VM],
        out_specs=(VM, VM),
        compiler_params=params(windows),
        name="unpack",
    )(mine, theirs)


def solution(mesh):
    return jax.shard_map(
        per_device,
        mesh=mesh,
        in_specs=(
            P(None, "freq", ("dom", "win"), "rep"),
            P(None, ("dom", "win"), "rep"),
            P(("dom", "win"), "rep"),
            P(("dom", "win"), "rep", None),
            P("freq", None, "rep"),
            P(),
        ),
        out_specs=(P(None, "freq", ("dom", "win"), None), P(None, "freq", ("dom", "win"), "rep")),
        check_vma=False,
    )
```

```python
import functools
import math

import jax
import jax.numpy as jnp
from jax import lax
from jax.experimental import pallas as pl
from jax.experimental.pallas import tpu as pltpu
from jax.sharding import PartitionSpec as P

PX = 16
PY = 32
SPB = 64
OBS = 128
ITERS = 3
LANES = 128
GROUP = 8
HALF = PX * GROUP
FOLD = PY // 2
SPAN = 2 * FOLD

step_length = 1.0
epsilon = 1e-06
HIGHEST = lax.Precision.HIGHEST


def iota(shape, dim):
    return lax.broadcasted_iota(jnp.int32, shape, dim)


def half_turns(y):
    quarter = jnp.floor(2.0 * y + 0.5)
    r = y - 0.5 * quarter
    q = quarter.astype(jnp.int32)
    r2 = r * r
    pi = math.pi
    sine = r * (
        pi
        + r2
        * (
            -(pi**3) / 6
            + r2 * (pi**5 / 120 + r2 * (-(pi**7) / 5040 + r2 * (pi**9 / 362880)))
        )
    )
    cosine = 1.0 + r2 * (
        -(pi**2) / 2 + r2 * (pi**4 / 24 + r2 * (-(pi**6) / 720 + r2 * (pi**8 / 40320)))
    )
    odd = (q & 1) == 1
    c = jnp.where(odd, sine, cosine)
    s = jnp.where(odd, cosine, sine)
    c = jnp.where(((q + 1) & 2) != 0, -c, c)
    s = jnp.where((q & 2) != 0, s, -s)
    return c, s


def rounded(x):
    return x.astype(jnp.bfloat16).astype(jnp.float32)


def times(p, q):
    return p[0] * q[0] - p[1] * q[1], p[0] * q[1] + p[1] * q[0]


def pack_kernel(
    recorded, geometry, present, intersection, pattern, keep, send, keep_coded, send_coded, *scratch
):
    sources = (recorded, geometry, present, intersection, pattern)
    local, sems, turned = scratch[:5], scratch[5], scratch[6]
    copies = [
        pltpu.make_async_copy(src, dst, sems.at[n]) for n, (src, dst) in enumerate(zip(sources, local))
    ]
    for copy in copies:
        copy.start()
    for copy in copies:
        copy.wait()
    recorded, geometry, present, intersection, pattern = local
    frequencies = recorded.shape[1]
    half = frequencies // 2
    rep = lax.axis_index("rep")
    blocks, span = pattern.shape[:2]
    for i in range(blocks):
        turned[span * i : span * (i + 1), :] = pattern[i].astype(jnp.float32)
    base = 2 * half
    for out, coded, part in ((keep, keep_coded, rep), (send, send_coded, 1 - rep)):
        for c in range(2):
            out[c * half : (c + 1) * half, :] = recorded[c, pl.ds(part * half, half), 0, :]
        out[base : base + 8, :] = jnp.zeros((8, out.shape[1]), jnp.float32)
        chosen = iota((half, frequencies), 0) + part * half == iota((half, frequencies), 1)
        pat = lax.dot_general(
            chosen.astype(jnp.float32),
            turned[...],
            (((1,), (1,)), ((), ())),
            preferred_element_type=jnp.float32,
        )
        for h in range(half // 8):
            out[base : base + 8, h * LANES : h * LANES + pat.shape[1]] = pat[8 * h : 8 * h + 8]
        for t in range(4):
            sl = slice(t * LANES, (t + 1) * LANES)
            out[base + t : base + t + 1, 256:384] = geometry[0, :, sl]
            out[base + 4 + t : base + 5 + t, 256:384] = geometry[1, :, sl]
            out[base + t : base + t + 1, 384:512] = present[:, sl].astype(jnp.float32)
        out[base + 4 : base + 5, 384:512] = intersection[0].astype(jnp.float32)
        coded[0:base, :] = out[0:base, :].astype(jnp.bfloat16)
        small = out[base : base + 8, :]
        rest = small[:, 256:384] - rounded(small[:, 256:384])
        parts = [rounded(rest), rounded(rest - rounded(rest)), jnp.zeros((8, 256), jnp.float32)]
        coded[base : base + 16, :] = jnp.concatenate(
            [small, jnp.concatenate(parts, axis=1)], axis=0
        ).astype(jnp.bfloat16)


def unpack_kernel(mine, theirs, coefficients, reconstruction):
    rep = lax.axis_index("rep")
    half = mine.shape[2]
    for n, out in enumerate((coefficients, reconstruction)):
        for c in range(2):
            out[c, pl.ds(rep * half, half), 0, :] = mine[n, c]
            out[c, pl.ds((1 - rep) * half, half), 0, :] = theirs[n, c]


def low_half(dims):
    return (iota(dims, 1) // FOLD) % 2 == 0


def swapped(values):
    return pltpu.roll(values, FOLD, 1)


def side_by_side(ref, w, g, first, count):
    return jnp.concatenate([ref[w][g, first + n] for n in range(count)], axis=1)


def project_group(hb, cross, w, g, masks, sign):
    tiles = hb.shape[0]
    g = lax.dot_general(
        jnp.concatenate([hb[n] for n in range(tiles)], axis=1),
        side_by_side(cross, w, g, 0, tiles),
        (((1,), (1,)), ((), ())),
        preferred_element_type=jnp.float32,
    )
    g = jnp.where(masks[0], g[:, :LANES], jnp.where(masks[1], g[:, LANES:], 0.0))
    g = g + pltpu.roll(g, 32, 1)
    g = g + pltpu.roll(g, 64, 1)
    top, bottom = g[:HALF], sign * swapped(g[HALF:])
    return top + bottom, top - bottom


def group_masks():
    rows = iota((2 * HALF, LANES), 0) % GROUP
    lanes = iota((2 * HALF, LANES), 1) // SPAN
    return rows == lanes, rows == lanes + 4


def half_sign():
    return jnp.where(low_half((HALF, LANES)), 1.0, -1.0)


def weigh(inline, g, tile, r_re, r_im, hb):
    sl = pl.ds(tile * LANES, LANES)
    for i in range(HALF // 16):
        rows = slice(16 * i, 16 * i + 16)
        low = slice(HALF + 16 * i, HALF + 16 * i + 16)
        a_re = inline[g, rows, sl]
        a_im = inline[g, low, sl]
        rr = jnp.concatenate([r_re, r_re], axis=0)
        ri = jnp.concatenate([r_im, r_im], axis=0)
        hb[tile, rows, :] = (a_re * rr + a_im * ri).astype(jnp.bfloat16)
        hb[tile, low, :] = (a_re * ri - a_im * rr).astype(jnp.bfloat16)


def pack_energy(values, energy, row):
    both = values + swapped(values)
    both = jnp.where(low_half((HALF, LANES)), both[:HALF], both[HALF:])
    block = iota((GROUP, LANES), 1) // SPAN
    for j in range(4):
        total = None
        for q in range(4):
            a = 4 * j + q
            part = jnp.where(block == q, both[GROUP * a : GROUP * (a + 1)], 0.0)
            total = part if total is None else total + part
        energy[pl.ds(row + j, 1), :] = jnp.sum(total, axis=0, keepdims=True)


def table_kernel(windows, nfreq, amplitude, own, *refs):
    pays, refs = refs[:2], refs[2:]
    extra, refs = refs[0], refs[1:]
    cross, inline, observed, mask, updated, energy, *refs = refs
    if own:
        matching, threshold, pay, hb, acc, scale_local, sem = refs
        scale_copy = pltpu.make_async_copy(extra, scale_local, sem)
        scale_copy.start()
    else:
        pay, hb, acc = refs
        energy[0:4, :] = extra[...]
    many = pay.shape[0]
    half = pay.shape[2] - 8
    freqs = half // 2
    win = lax.axis_index("win")
    first = (2 * lax.axis_index("freq") + lax.axis_index("rep")) * freqs
    groups = freqs // GROUP
    base = half

    def window(n):
        return win if own else lax.rem(win + 1 + n, windows)

    for n in range(many):
        for s in range(2):
            source = pays[s] if len(pays[s].shape) == 2 else pays[s].at[window(n)]
            if own:
                pay[n, s] = source[...]
                continue
            pay[n, s, 0:base, :] = source[0:base, :].astype(jnp.float32)
            small = source[base : base + 16, :].astype(jnp.float32)
            pay[n, s, base : base + 8, :] = small[:8]
            pay[n, s, base : base + 8, 256:384] = (
                small[:8, 256:384] + small[8:, :LANES] + small[8:, LANES:256]
            )

    def pairing(n, s):
        index = pay[n, s, base + 4 : base + 5, 384:512].astype(jnp.int32)
        index = jnp.where(window(n) > 0, index, iota((1, LANES), 1))
        return (iota((LANES, LANES), 0) == index).astype(jnp.float32)

    if own:
        for s in range(2):
            matching[s] = pairing(0, s)

    def align(n, _):
        n, s = n // 2, n % 2
        hot = pairing(n, s)
        dot = functools.partial(
            lax.dot_general,
            dimension_numbers=(((1,), (1,)), ((), ())),
            precision=HIGHEST,
            preferred_element_type=jnp.float32,
        )
        pay[n, s, 0:half, 0:LANES] = dot(pay[n, s, 0:half, 0:LANES], hot)
        geo = dot(pay[n, s, base : base + 8, 256:384], hot)
        pay[n, s, base : base + 1, 256:384] = geo[0:1]
        pay[n, s, base + 4 : base + 5, 256:384] = geo[4:5]
        here = dot(pay[n, s, base : base + 8, 384:512], hot)
        pay[n, s, base : base + 1, 384:512] = here[0:1]
        return 0

    lax.fori_loop(0, 2 * many, align, 0)

    sub = iota((8, LANES), 0)
    delta = 0.75 / nfreq
    start = first.astype(jnp.float32)
    scale0 = 0.25 + 0.75 * ((start + 0.5) / nfreq)
    odd_cross = (2 * sub - (PY - 1)).astype(jnp.float32)

    def strip_tables(n, _):
        n, s = n // 2, n % 2
        for t in range(4):
            off = pl.multiple_of(s * 512 + t * LANES, LANES)
            sl = pl.ds(off, LANES)
            g0 = pay[n, s, base + t : base + t + 1, 256:384]
            g1 = pay[n, s, base + 4 + t : base + 5 + t, 256:384]
            here = jnp.broadcast_to(pay[n, s, base + t : base + t + 1, 384:512], (8, LANES))
            mask[n, :, sl] = here
            now = half_turns((scale0 * g1) * odd_cross)
            more = half_turns((delta * g1) * odd_cross)
            g1b = jnp.broadcast_to(g1, (8, LANES))
            rot = half_turns((scale0 * g1b) * 16.0)
            rot_more = half_turns((delta * g1b) * 16.0)
            for f in range(freqs):
                v0 = now
                v1 = times(v0, rot)
                row = (f % GROUP) * SPAN
                for part in range(2):
                    cross[n, f // GROUP, 4 * s + t, row + FOLD * part : row + FOLD * (part + 1), :] = (
                        jnp.concatenate([v0[part], v1[part]], axis=0).astype(jnp.bfloat16)
                    )
                if f + 1 < freqs:
                    now = times(now, more)
                    rot = times(rot, rot_more)
            for g in range(groups):
                level = start + (sub + g * GROUP).astype(jnp.float32)
                scale = 0.25 + 0.75 * ((level + 0.5) / nfreq)
                v = half_turns((scale * g0) * 2.0)
                rot = half_turns((scale * g0) * 4.0)
                v = (v[0] * amplitude, v[1] * amplitude)
                for a in range(PX // 2, PX, 2):
                    u = times(v, rot)
                    i, mirror = a // 2, (PX - 1 - a) // 2
                    lane = g * LANES + t
                    col = pay[n, s, base : base + 8, lane + 4 * i : lane + 4 * i + 1]
                    other = pay[n, s, base : base + 8, lane + 4 * mirror : lane + 4 * mirror + 1]
                    low = GROUP * (PX - 2 - a)
                    for part in range(2):
                        row = part * HALF
                        inline[n, g, row + GROUP * a : row + GROUP * (a + 2), sl] = (
                            rounded(jnp.concatenate([v[part] * col, u[part] * col], axis=0))
                        )
                        turn = -other if part else other
                        inline[n, g, row + low : row + low + 2 * GROUP, sl] = (
                            rounded(jnp.concatenate([u[part] * turn, v[part] * turn], axis=0))
                        )
                    if a + 2 < PX:
                        v = times(u, rot)
            for c in range(2):
                for g in range(groups):
                    row = c * freqs + GROUP * g
                    observed[n, c, g, :, sl] = (
                        here * pay[n, s, row : row + GROUP, t * LANES : (t + 1) * LANES]
                    )
        return 0

    lax.fori_loop(0, 2 * many, strip_tables, 0)

    masks, sign = group_masks(), half_sign()
    acc[...] = jnp.zeros_like(acc)

    def first_group(k, _):
        g, n = k % groups, k // groups
        buffer = hb.at[k % hb.shape[0]]
        for tile in range(8):
            sl = slice(tile * LANES, (tile + 1) * LANES)
            r_re, r_im = -observed[n, 0, g, :, sl], -observed[n, 1, g, :, sl]
            weigh(inline.at[n], g, tile, r_re, r_im, buffer)
        slopes = project_group(buffer, [cross.at[n]], 0, g, masks, sign)
        for part, slope in enumerate(slopes):
            rows = slice(part * HALF, (part + 1) * HALF)
            value = -step_length * slope
            updated[n, g, rows] = value
            acc[n, rows] += value * value
        return 0

    lax.fori_loop(0, many * groups, first_group, 0, unroll=True)
    for n in range(many):
        pack_energy(acc[n], energy, 4 * (n + (not own)))
    if own:
        scale_copy.wait()
        lane = iota((LANES, LANES), 1)
        at = lane % SPAN
        source = jnp.where(at < FOLD, lane, lane + PY - 1 + FOLD - 2 * at)
        order = (iota((LANES, LANES), 0) == source).astype(jnp.float32)
        threshold[...] = jnp.dot(
            scale_local[...], order, precision=HIGHEST, preferred_element_type=jnp.float32
        )


def spread_factor(energies, threshold, factor, windows, nfreq):
    total = energies[0][...]
    for e in energies[1:]:
        total = total + e[...]
    limit = jnp.concatenate([threshold[...]] * windows, axis=0)
    packed = jnp.maximum(0.0, 1.0 - limit / jnp.sqrt(total / nfreq + epsilon))
    block = iota((8, LANES), 1) // SPAN
    low = low_half((8, LANES))
    for w in range(windows):
        for a in range(PX):
            row = w * 4 + a // 4
            y = jnp.where(block == a % 4, jnp.broadcast_to(packed[row : row + 1], (8, LANES)), 0.0)
            y = y + pltpu.roll(y, 32, 1)
            y = y + pltpu.roll(y, 64, 1)
            turned = swapped(y)
            factor[w, GROUP * a : GROUP * (a + 1), :] = jnp.where(low, y, turned)
            factor[w, HALF + GROUP * a : HALF + GROUP * (a + 1), :] = jnp.where(low, turned, y)


def mix(current, masks, sign):
    first, second = current[:HALF], current[HALF:]
    m = jnp.concatenate([first + second, swapped(sign * (first - second))], axis=0)
    return jnp.concatenate(
        [jnp.where(masks[0], m, 0.0), jnp.where(masks[1], m, 0.0)], axis=1
    ).astype(jnp.bfloat16)


def predict_tile(inline, part):
    p_re = p_im = None
    for i in range(HALF // 16):
        a_re = inline[16 * i : 16 * i + 16]
        a_im = inline[HALF + 16 * i : HALF + 16 * i + 16]
        b_re = part[16 * i : 16 * i + 16]
        b_im = part[HALF + 16 * i : HALF + 16 * i + 16]
        re = a_re * b_re - a_im * b_im
        im = a_re * b_im + a_im * b_re
        p_re = re if p_re is None else p_re + re
        p_im = im if p_im is None else p_im + im
    return p_re[:8] + p_re[8:], p_im[:8] + p_im[8:]


def predict_strip(mixing, cross, inline, w, g, s):
    out = []
    for first in (4 * s, 4 * s + 2):
        part = jnp.dot(
            mixing, side_by_side(cross, w, g, first, 2), preferred_element_type=jnp.float32
        )
        for k in range(2):
            table = inline[w][g, :, (first + k) * LANES : (first + k + 1) * LANES]
            out.append(predict_tile(table, part[:, k * LANES : (k + 1) * LANES]))
    return out


def predict_edges(mixing, cross, inline, w, g, tile):
    out = []
    for s in range(2):
        sl = slice((tile + 4 * s) * LANES, (tile + 4 * s + 1) * LANES)
        part = jnp.dot(mixing, cross[w][g, tile + 4 * s], preferred_element_type=jnp.float32)
        out.append(predict_tile(inline[w][g, :, sl], part))
    return out


def join(lower, upper):
    ramp = (iota((8, LANES), 1).astype(jnp.float32) + 0.5) / LANES
    return tuple((1.0 - ramp) * lower[c] + ramp * upper[c] for c in range(2))


def both_orders(own, others, windows):
    return [own.at[0]] + [others.at[n] for n in range(windows - 1)]


def blend(predicted, windows, win):
    joined = {}
    for n in range(windows if windows > 1 else 0):
        above = (n + 1) % windows
        apart = lax.rem(win + n, windows) == windows - 1
        trail, lead = predicted[n][3], predicted[above][0]
        both = join(trail, lead)
        joined[n, 3] = tuple(jnp.where(apart, trail[c], both[c]) for c in range(2))
        joined[above, 0] = tuple(jnp.where(apart, lead[c], both[c]) for c in range(2))
    for (n, tile), value in joined.items():
        predicted[n][tile] = value
    return predicted


def step_kernel(windows, nfreq, count, *refs):
    energies, refs = refs[:count], refs[count:]
    threshold, refs = refs[0], refs[1:]
    if windows > 1:
        cross, inline, observed, mask, updated = (
            both_orders(refs[n], refs[5 + n], windows) for n in range(5)
        )
        new = both_orders(refs[10], refs[11], windows)
        energy, factor, hb, acc = refs[12:]
    else:
        cross, inline, observed, mask, updated = ([refs[n].at[0]] for n in range(5))
        new = [refs[5].at[0]]
        energy, factor, hb, acc = refs[6:]
    win = lax.axis_index("win")
    spread_factor(energies, threshold, factor, windows, nfreq)
    masks, sign = group_masks(), half_sign()
    acc[...] = jnp.zeros_like(acc)
    for g in range(updated[0].shape[0]):
        mixing = [mix(updated[w][g] * factor[w], masks, sign) for w in range(windows)]
        buffers = [hb.at[(g * windows + w) % hb.shape[0]] for w in range(windows)]
        for s in range(2):
            predicted = blend(
                [predict_strip(mixing[w], cross, inline, w, g, s) for w in range(windows)],
                windows,
                win,
            )
            for w in range(windows):
                for t in range(4):
                    tile = 4 * s + t
                    sl = slice(tile * LANES, (tile + 1) * LANES)
                    here = mask[w][:, sl]
                    p_re, p_im = predicted[w][t]
                    r_re = here * p_re - observed[w][0, g, :, sl]
                    r_im = here * p_im - observed[w][1, g, :, sl]
                    weigh(inline[w], g, tile, r_re, r_im, buffers[w])
        for w in range(windows):
            slopes = project_group(buffers[w], cross, w, g, masks, sign)
            for part, slope in enumerate(slopes):
                rows = slice(part * HALF, (part + 1) * HALF)
                value = updated[w][g, rows] * factor[w, rows] - step_length * slope
                new[w][g, rows] = value
                acc[w, rows] += value * value
    for w in range(windows):
        pack_energy(acc[w], energy, 4 * w)


def final_kernel(windows, nfreq, count, *refs):
    energies, refs = refs[:count], refs[count:]
    threshold, matching, refs = refs[0], refs[1], refs[2:]
    if windows > 1:
        cross, inline, updated = (both_orders(refs[n], refs[3 + n], windows) for n in range(3))
        refs = refs[6:]
    else:
        cross, inline, updated = ([refs[n].at[0]] for n in range(3))
        refs = refs[3:]
    swap, keep, factor = refs
    win = lax.axis_index("win")
    spread_factor(energies, threshold, factor, windows, nfreq)
    masks, sign = group_masks(), half_sign()
    block = iota((GROUP, LANES), 1) // SPAN
    wide = iota((HALF, LANES), 1) // SPAN
    line, lane = iota((LANES, 2 * LANES), 0), iota((LANES, 2 * LANES), 1)
    b, imag = lane % PY, lane // LANES
    source = jnp.where(b < FOLD, b, SPAN + PY - 1 - b) + FOLD * imag
    value = jnp.where((imag == 1) & (b < FOLD), -1.0, 1.0)
    order = jnp.where(line == source, value, 0.0)

    for g in range(updated[0].shape[0]):
        current = updated[0][g] * factor[0]
        mixing = mix(current, masks, sign)
        traces = [x for s in range(2) for x in predict_strip(mixing, cross, inline, 0, g, s)]
        if windows > 1:
            mixed = [
                mix(updated[w][g] * factor[w], masks, sign) for w in sorted({1, windows - 1})
            ]
            above = predict_edges(mixed[0], cross, inline, 1, g, 0)
            below = predict_edges(mixed[-1], cross, inline, windows - 1, g, 3)
            for s in range(2):
                lead, trail = traces[4 * s], traces[4 * s + 3]
                low, high = join(below[s], lead), join(trail, above[s])
                traces[4 * s] = tuple(jnp.where(win > 0, low[c], lead[c]) for c in range(2))
                traces[4 * s + 3] = tuple(
                    jnp.where(win < windows - 1, high[c], trail[c]) for c in range(2)
                )
        spans = jnp.where(wide == 0, current[:HALF], jnp.where(wide == 1, current[HALF:], 0.0))
        spans = jnp.dot(spans, order, precision=HIGHEST, preferred_element_type=jnp.float32)
        sl = slice(GROUP * g, GROUP * (g + 1))
        for c in range(2):
            for j in range(4):
                lanes = slice(j * LANES, (j + 1) * LANES)
                values = None
                for q in range(4):
                    a = 4 * j + q
                    part = spans[GROUP * a : GROUP * (a + 1), c * LANES : (c + 1) * LANES]
                    part = jnp.where(block == q, part, 0.0)
                    values = part if values is None else values + part
                swap[0, c, sl, lanes] = values
                keep[0, c, sl, lanes] = values
            for t in range(8):
                lanes = slice((t % 4) * LANES, (t % 4 + 1) * LANES)
                out = keep if t < 4 else swap
                out[1, c, sl, lanes] = traces[t][c]
    for s, out in enumerate((keep, swap)):
        for c in range(2):
            out[1, c, :, :LANES] = jnp.dot(
                out[1, c, :, :LANES],
                matching[s],
                precision=HIGHEST,
                preferred_element_type=jnp.float32,
            )


VM = pl.BlockSpec(memory_space=pltpu.VMEM)
HB = pl.BlockSpec(memory_space=pltpu.HBM)


def params(windows):
    return pltpu.CompilerParams(vmem_limit_bytes=(16 if windows <= 2 else 60) * 1024 * 1024)


def shape(*dims, dtype=jnp.float32):
    return jax.ShapeDtypeStruct(dims, dtype)


def sum_parts(energy):
    swap = [(0, 1), (1, 0)]
    energy = energy + lax.ppermute(energy, "rep", swap)
    size = lax.axis_size("freq")
    if size & (size - 1):
        return [lax.psum(energy, "freq")]
    axes = ("freq", "rep")

    def crossed(k):
        return [(2 * i + r, 2 * (i ^ k) + 1 - r) for i in range(size) for r in range(2)]

    if size <= 4:
        return [energy] + [lax.ppermute(energy, axes, crossed(k)) for k in range(1, size)]
    k = 1
    while k < size:
        energy = energy + lax.ppermute(energy, axes, crossed(k))
        k *= 2
    return [energy]


def per_device(recorded, geometry, present, intersection_index, pattern, group_scale):
    frequencies = recorded.shape[1]
    traces = recorded.shape[3]
    windows = lax.axis_size("win")
    nfreq = frequencies * lax.axis_size("freq")
    half = frequencies // 2
    groups = half // GROUP
    amplitude = 1.0 / math.sqrt(traces * lax.axis_size("rep"))
    width = 2 * traces
    swap = [(0, 1), (1, 0)]

    payload = shape(2 * half + 8, traces)
    turned = jnp.transpose(pattern, (1, 2, 0))
    sources = tuple(
        pltpu.with_memory_space_constraint(x, pltpu.HBM)
        for x in (recorded, geometry, present, intersection_index, turned)
    )
    coded = shape(2 * half + 16, traces, dtype=jnp.bfloat16)
    keep, send, keep_coded, send_coded = pl.pallas_call(
        pack_kernel,
        out_shape=(payload, payload, coded, coded),
        in_specs=[HB] * 5,
        out_specs=(VM,) * 4,
        scratch_shapes=[pltpu.VMEM(x.shape, x.dtype) for x in sources]
        + [
            pltpu.SemaphoreType.DMA((5,)),
            pltpu.VMEM((turned.shape[0] * turned.shape[1], frequencies), jnp.float32),
        ],
        compiler_params=params(windows),
        name="pack",
    )(*sources)
    received = lax.ppermute(send, "rep", swap)
    if windows == 2:
        diagonal = [(2 * i + r, 2 * (1 - i) + 1 - r) for i in range(2) for r in range(2)]
        others = [
            lax.ppermute(keep_coded, "win", swap),
            lax.ppermute(send_coded, ("win", "rep"), diagonal),
        ]
    else:
        received_coded = lax.ppermute(send_coded, "rep", swap)
        others = [lax.all_gather(x, "win") for x in (keep_coded, received_coded)]

    rows = 2 * HALF
    energy_shape = shape(4 * windows, LANES)

    def scratch(many):
        buffers = many * groups if windows <= 2 else windows
        return [
            pltpu.VMEM((buffers, width // LANES, rows, LANES), jnp.bfloat16),
            pltpu.VMEM((many, rows, LANES), jnp.float32),
        ]

    def build(own, inputs):
        many = 1 if own else windows - 1
        out_shape = (
            shape(many, groups, width // LANES, SPAN * GROUP, LANES, dtype=jnp.bfloat16),
            shape(many, groups, rows, width),
            shape(many, 2, groups, GROUP, width),
            shape(many, 8, width),
            shape(many, groups, rows, LANES),
            shape(4, LANES) if own else energy_shape,
        )
        if own:
            out_shape += (shape(2, LANES, LANES), shape(4, LANES))
        return pl.pallas_call(
            functools.partial(table_kernel, windows, nfreq, amplitude, own),
            out_shape=out_shape,
            in_specs=[VM] * (len(inputs) - 1) + [HB if own else VM],
            out_specs=(VM,) * len(out_shape),
            scratch_shapes=[pltpu.VMEM((many, 2, 2 * half + 8, traces), jnp.float32)]
            + scratch(many)
            + ([pltpu.VMEM((4, LANES), jnp.float32), pltpu.SemaphoreType.DMA] if own else []),
            compiler_params=params(windows),
            cost_estimate=pl.CostEstimate(flops=4 * 10**9, bytes_accessed=0, transcendentals=0),
            name="tables",
        )(*inputs)

    *tables, updated, energy, matching, threshold = build(
        True,
        [
            keep,
            received,
            pltpu.with_memory_space_constraint(group_scale.reshape(4, LANES), pltpu.HBM),
        ],
    )
    tables, states = [tables], [updated]
    if windows > 1:
        *others, updated, energy = build(False, others + [energy])
        tables.append(others)
        states.append(updated)

    factor_scratch = pltpu.VMEM((windows, rows, LANES), jnp.float32)
    for _ in range(ITERS - 1):
        inputs = [threshold]
        for table, state in zip(tables, states):
            inputs += [*table, state]
        energies = sum_parts(energy)
        *states, energy = pl.pallas_call(
            functools.partial(step_kernel, windows, nfreq, len(energies)),
            out_shape=tuple(shape(*x.shape) for x in states) + (energy_shape,),
            in_specs=[VM] * (len(energies) + len(inputs)),
            out_specs=(VM,) * (len(states) + 1),
            scratch_shapes=[factor_scratch] + scratch(windows),
            compiler_params=params(windows),
            name="step",
        )(*energies, *inputs)
    energies = sum_parts(energy)
    halves = shape(2, 2, half, traces)
    inputs = [threshold, matching]
    for table, state in zip(tables, states):
        inputs += [*table[:2], state]
    theirs, mine = pl.pallas_call(
        functools.partial(final_kernel, windows, nfreq, len(energies)),
        out_shape=(halves, halves),
        in_specs=[VM] * (len(energies) + len(inputs)),
        out_specs=(VM, VM),
        scratch_shapes=[factor_scratch],
        compiler_params=params(windows),
        name="final",
    )(*energies, *inputs)
    theirs = lax.ppermute(theirs, "rep", swap)
    out = shape(2, frequencies, 1, traces)
    return pl.pallas_call(
        unpack_kernel,
        out_shape=(out, out),
        in_specs=[VM, VM],
        out_specs=(VM, VM),
        compiler_params=params(windows),
        name="unpack",
    )(mine, theirs)


def solution(mesh):
    return jax.shard_map(
        per_device,
        mesh=mesh,
        in_specs=(
            P(None, "freq", ("dom", "win"), "rep"),
            P(None, ("dom", "win"), "rep"),
            P(("dom", "win"), "rep"),
            P(("dom", "win"), "rep", None),
            P("freq", None, "rep"),
            P(),
        ),
        out_specs=(P(None, "freq", ("dom", "win"), None), P(None, "freq", ("dom", "win"), "rep")),
        check_vma=False,
    )
```

```python
import functools
import math

import jax
import jax.numpy as jnp
from jax import lax
from jax.experimental import pallas as pl
from jax.experimental.pallas import tpu as pltpu
from jax.sharding import PartitionSpec as P

PX = 16
PY = 32
SPB = 64
OBS = 128
ITERS = 3
LANES = 128
GROUP = 8
HALF = PX * GROUP
FOLD = PY // 2
SPAN = 2 * FOLD

step_length = 1.0
epsilon = 1e-06
HIGHEST = lax.Precision.HIGHEST


def iota(shape, dim):
    return lax.broadcasted_iota(jnp.int32, shape, dim)


def half_turns(y):
    quarter = jnp.floor(2.0 * y + 0.5)
    r = y - 0.5 * quarter
    q = quarter.astype(jnp.int32)
    r2 = r * r
    pi = math.pi
    sine = r * (
        pi
        + r2
        * (
            -(pi**3) / 6
            + r2 * (pi**5 / 120 + r2 * (-(pi**7) / 5040 + r2 * (pi**9 / 362880)))
        )
    )
    cosine = 1.0 + r2 * (
        -(pi**2) / 2 + r2 * (pi**4 / 24 + r2 * (-(pi**6) / 720 + r2 * (pi**8 / 40320)))
    )
    odd = (q & 1) == 1
    c = jnp.where(odd, sine, cosine)
    s = jnp.where(odd, cosine, sine)
    c = jnp.where(((q + 1) & 2) != 0, -c, c)
    s = jnp.where((q & 2) != 0, s, -s)
    return c, s


def rounded(x):
    return x.astype(jnp.bfloat16).astype(jnp.float32)


def choose(values, hot, transposed=False):
    rest = values - rounded(values)
    last = rest - rounded(rest)
    parts = jnp.concatenate([values, rest, last], axis=0).astype(jnp.bfloat16)
    out = lax.dot_general(
        parts,
        hot.astype(jnp.bfloat16),
        (((1,), (1 if transposed else 0,)), ((), ())),
        preferred_element_type=jnp.float32,
    )
    n = values.shape[0]
    return out[:n] + (out[n : 2 * n] + out[2 * n :])


def times(p, q):
    return p[0] * q[0] - p[1] * q[1], p[0] * q[1] + p[1] * q[0]


def pack_kernel(
    recorded, geometry, present, intersection, pattern, keep, send, keep_coded, send_coded, *scratch
):
    sources = (recorded, geometry, present, intersection, pattern)
    local, sems, turned = scratch[:5], scratch[5], scratch[6]
    copies = [
        pltpu.make_async_copy(src, dst, sems.at[n]) for n, (src, dst) in enumerate(zip(sources, local))
    ]
    for copy in copies:
        copy.start()
    for copy in copies:
        copy.wait()
    recorded, geometry, present, intersection, pattern = local
    frequencies = recorded.shape[1]
    half = frequencies // 2
    rep = lax.axis_index("rep")
    blocks, span = pattern.shape[:2]
    for i in range(blocks):
        turned[span * i : span * (i + 1), :] = pattern[i].astype(jnp.float32)
    base = 2 * half
    for out, coded, part in ((keep, keep_coded, rep), (send, send_coded, 1 - rep)):
        for c in range(2):
            out[c * half : (c + 1) * half, :] = recorded[c, pl.ds(part * half, half), 0, :]
        out[base : base + 8, :] = jnp.zeros((8, out.shape[1]), jnp.float32)
        chosen = iota((half, frequencies), 0) + part * half == iota((half, frequencies), 1)
        pat = lax.dot_general(
            chosen.astype(jnp.float32),
            turned[...],
            (((1,), (1,)), ((), ())),
            preferred_element_type=jnp.float32,
        )
        for h in range(half // 8):
            out[base : base + 8, h * LANES : h * LANES + pat.shape[1]] = pat[8 * h : 8 * h + 8]
        for t in range(4):
            sl = slice(t * LANES, (t + 1) * LANES)
            out[base + t : base + t + 1, 256:384] = geometry[0, :, sl]
            out[base + 4 + t : base + 5 + t, 256:384] = geometry[1, :, sl]
            out[base + t : base + t + 1, 384:512] = present[:, sl].astype(jnp.float32)
        out[base + 4 : base + 5, 384:512] = intersection[0].astype(jnp.float32)
        coded[0:base, :] = out[0:base, :].astype(jnp.bfloat16)
        small = out[base : base + 8, :]
        rest = small[:, 256:384] - rounded(small[:, 256:384])
        parts = [rounded(rest), rounded(rest - rounded(rest)), jnp.zeros((8, 256), jnp.float32)]
        coded[base : base + 16, :] = jnp.concatenate(
            [small, jnp.concatenate(parts, axis=1)], axis=0
        ).astype(jnp.bfloat16)


def unpack_kernel(mine, theirs, coefficients, reconstruction):
    rep = lax.axis_index("rep")
    half = mine.shape[2]
    for n, out in enumerate((coefficients, reconstruction)):
        for c in range(2):
            out[c, pl.ds(rep * half, half), 0, :] = mine[n, c]
            out[c, pl.ds((1 - rep) * half, half), 0, :] = theirs[n, c]


def low_half(dims):
    return (iota(dims, 1) // FOLD) % 2 == 0


def swapped(values):
    return pltpu.roll(values, FOLD, 1)


def side_by_side(ref, w, g, first, count):
    return jnp.concatenate([ref[w][g, first + n] for n in range(count)], axis=1)


def project_group(hb, cross, w, g, masks, sign):
    tiles = hb.shape[0]
    g = lax.dot_general(
        jnp.concatenate([hb[n] for n in range(tiles)], axis=1),
        side_by_side(cross, w, g, 0, tiles),
        (((1,), (1,)), ((), ())),
        preferred_element_type=jnp.float32,
    )
    g = jnp.where(masks[0], g[:, :LANES], jnp.where(masks[1], g[:, LANES:], 0.0))
    g = g + pltpu.roll(g, 32, 1)
    g = g + pltpu.roll(g, 64, 1)
    top, bottom = g[:HALF], sign * swapped(g[HALF:])
    return top + bottom, top - bottom


def group_masks():
    rows = iota((2 * HALF, LANES), 0) % GROUP
    lanes = iota((2 * HALF, LANES), 1) // SPAN
    return rows == lanes, rows == lanes + 4


def half_sign():
    return jnp.where(low_half((HALF, LANES)), 1.0, -1.0)


def weigh(inline, g, tile, r_re, r_im, hb):
    sl = pl.ds(tile * LANES, LANES)
    for i in range(HALF // 16):
        rows = slice(16 * i, 16 * i + 16)
        low = slice(HALF + 16 * i, HALF + 16 * i + 16)
        a_re = inline[g, rows, sl]
        a_im = inline[g, low, sl]
        rr = jnp.concatenate([r_re, r_re], axis=0)
        ri = jnp.concatenate([r_im, r_im], axis=0)
        hb[tile, rows, :] = (a_re * rr + a_im * ri).astype(jnp.bfloat16)
        hb[tile, low, :] = (a_re * ri - a_im * rr).astype(jnp.bfloat16)


def pack_energy(values, energy, row):
    both = values + swapped(values)
    both = jnp.where(low_half((HALF, LANES)), both[:HALF], both[HALF:])
    block = iota((GROUP, LANES), 1) // SPAN
    for j in range(4):
        total = None
        for q in range(4):
            a = 4 * j + q
            part = jnp.where(block == q, both[GROUP * a : GROUP * (a + 1)], 0.0)
            total = part if total is None else total + part
        energy[pl.ds(row + j, 1), :] = jnp.sum(total, axis=0, keepdims=True)


def table_kernel(windows, nfreq, amplitude, own, *refs):
    pays, refs = refs[:2], refs[2:]
    extra, refs = refs[0], refs[1:]
    cross, inline, observed, mask, updated, energy, *refs = refs
    if own:
        matching, threshold, pay, hb, acc, scale_local, sem = refs
        scale_copy = pltpu.make_async_copy(extra, scale_local, sem)
        scale_copy.start()
    else:
        pay, hb, acc = refs
        energy[0:4, :] = extra[...]
    many = pay.shape[0]
    half = pay.shape[2] - 8
    freqs = half // 2
    win = lax.axis_index("win")
    first = (2 * lax.axis_index("freq") + lax.axis_index("rep")) * freqs
    groups = freqs // GROUP
    base = half

    def window(n):
        return win if own else lax.rem(win + 1 + n, windows)

    for n in range(many):
        for s in range(2):
            source = pays[s] if len(pays[s].shape) == 2 else pays[s].at[window(n)]
            if own:
                pay[n, s] = source[...]
                continue
            pay[n, s, 0:base, :] = source[0:base, :].astype(jnp.float32)
            small = source[base : base + 16, :].astype(jnp.float32)
            pay[n, s, base : base + 8, :] = small[:8]
            pay[n, s, base : base + 8, 256:384] = (
                small[:8, 256:384] + small[8:, :LANES] + small[8:, LANES:256]
            )

    def pairing(n, s):
        index = pay[n, s, base + 4 : base + 5, 384:512].astype(jnp.int32)
        index = jnp.where(window(n) > 0, index, iota((1, LANES), 1))
        return (iota((LANES, LANES), 0) == index).astype(jnp.float32)

    if own:
        for s in range(2):
            matching[s] = pairing(0, s)

    def align(n, _):
        n, s = n // 2, n % 2
        lead = [
            pay[n, s, 0:half, 0:LANES],
            pay[n, s, base : base + 8, 256:384],
            pay[n, s, base : base + 8, 384:512],
        ]
        lead = choose(jnp.concatenate(lead, axis=0), pairing(n, s), transposed=True)
        pay[n, s, 0:half, 0:LANES] = lead[:half]
        pay[n, s, base : base + 1, 256:384] = lead[half : half + 1]
        pay[n, s, base + 4 : base + 5, 256:384] = lead[half + 4 : half + 5]
        pay[n, s, base : base + 1, 384:512] = lead[half + 8 : half + 9]
        return 0

    lax.fori_loop(0, 2 * many, align, 0, unroll=many == 1)

    sub = iota((8, LANES), 0)
    delta = 0.75 / nfreq
    start = first.astype(jnp.float32)
    scale0 = 0.25 + 0.75 * ((start + 0.5) / nfreq)
    odd_cross = (2 * sub - (PY - 1)).astype(jnp.float32)

    def strip_tables(n, _):
        n, s = n // 2, n % 2
        for t in range(4):
            off = pl.multiple_of(s * 512 + t * LANES, LANES)
            sl = pl.ds(off, LANES)
            g0 = pay[n, s, base + t : base + t + 1, 256:384]
            g1 = pay[n, s, base + 4 + t : base + 5 + t, 256:384]
            here = jnp.broadcast_to(pay[n, s, base + t : base + t + 1, 384:512], (8, LANES))
            mask[n, :, sl] = here
            now = half_turns((scale0 * g1) * odd_cross)
            more = half_turns((delta * g1) * odd_cross)
            g1b = jnp.broadcast_to(g1, (8, LANES))
            rot = half_turns((scale0 * g1b) * 16.0)
            rot_more = half_turns((delta * g1b) * 16.0)
            for f in range(freqs):
                v0 = now
                v1 = times(v0, rot)
                row = (f % GROUP) * SPAN
                for part in range(2):
                    cross[n, f // GROUP, 4 * s + t, row + FOLD * part : row + FOLD * (part + 1), :] = (
                        jnp.concatenate([v0[part], v1[part]], axis=0).astype(jnp.bfloat16)
                    )
                if f + 1 < freqs:
                    now = times(now, more)
                    rot = times(rot, rot_more)
            for g in range(groups):
                level = start + (sub + g * GROUP).astype(jnp.float32)
                scale = 0.25 + 0.75 * ((level + 0.5) / nfreq)
                v = half_turns((scale * g0) * 2.0)
                rot = half_turns((scale * g0) * 4.0)
                v = (v[0] * amplitude, v[1] * amplitude)
                for a in range(PX // 2, PX, 2):
                    u = times(v, rot)
                    i, mirror = a // 2, (PX - 1 - a) // 2
                    lane = g * LANES + t
                    col = pay[n, s, base : base + 8, lane + 4 * i : lane + 4 * i + 1]
                    other = pay[n, s, base : base + 8, lane + 4 * mirror : lane + 4 * mirror + 1]
                    low = GROUP * (PX - 2 - a)
                    for part in range(2):
                        row = part * HALF
                        inline[n, g, row + GROUP * a : row + GROUP * (a + 2), sl] = (
                            rounded(jnp.concatenate([v[part] * col, u[part] * col], axis=0))
                        )
                        turn = -other if part else other
                        inline[n, g, row + low : row + low + 2 * GROUP, sl] = (
                            rounded(jnp.concatenate([u[part] * turn, v[part] * turn], axis=0))
                        )
                    if a + 2 < PX:
                        v = times(u, rot)
            for c in range(2):
                for g in range(groups):
                    row = c * freqs + GROUP * g
                    observed[n, c, g, :, sl] = (
                        here * pay[n, s, row : row + GROUP, t * LANES : (t + 1) * LANES]
                    )
        return 0

    lax.fori_loop(0, 2 * many, strip_tables, 0)

    masks, sign = group_masks(), half_sign()
    acc[...] = jnp.zeros_like(acc)

    def first_group(k, _):
        g, n = k % groups, k // groups
        buffer = hb.at[k % hb.shape[0]]
        for tile in range(8):
            sl = slice(tile * LANES, (tile + 1) * LANES)
            r_re, r_im = -observed[n, 0, g, :, sl], -observed[n, 1, g, :, sl]
            weigh(inline.at[n], g, tile, r_re, r_im, buffer)
        slopes = project_group(buffer, [cross.at[n]], 0, g, masks, sign)
        for part, slope in enumerate(slopes):
            rows = slice(part * HALF, (part + 1) * HALF)
            value = -step_length * slope
            updated[n, g, rows] = value
            acc[n, rows] += value * value
        return 0

    lax.fori_loop(0, many * groups, first_group, 0, unroll=True)
    for n in range(many):
        pack_energy(acc[n], energy, 4 * (n + (not own)))
    if own:
        scale_copy.wait()
        lane = iota((LANES, LANES), 1)
        at = lane % SPAN
        source = jnp.where(at < FOLD, lane, lane + PY - 1 + FOLD - 2 * at)
        order = (iota((LANES, LANES), 0) == source).astype(jnp.float32)
        threshold[...] = jnp.dot(
            scale_local[...], order, precision=HIGHEST, preferred_element_type=jnp.float32
        )


def spread_factor(energies, threshold, factor, windows, nfreq):
    total = energies[0][...]
    for e in energies[1:]:
        total = total + e[...]
    limit = jnp.concatenate([threshold[...]] * windows, axis=0)
    packed = jnp.maximum(0.0, 1.0 - limit / jnp.sqrt(total / nfreq + epsilon))
    block = iota((8, LANES), 1) // SPAN
    low = low_half((8, LANES))
    for w in range(windows):
        for a in range(PX):
            row = w * 4 + a // 4
            y = jnp.where(block == a % 4, jnp.broadcast_to(packed[row : row + 1], (8, LANES)), 0.0)
            y = y + pltpu.roll(y, 32, 1)
            y = y + pltpu.roll(y, 64, 1)
            turned = swapped(y)
            factor[w, GROUP * a : GROUP * (a + 1), :] = jnp.where(low, y, turned)
            factor[w, HALF + GROUP * a : HALF + GROUP * (a + 1), :] = jnp.where(low, turned, y)


def mix(current, masks, sign):
    first, second = current[:HALF], current[HALF:]
    m = jnp.concatenate([first + second, swapped(sign * (first - second))], axis=0)
    return jnp.concatenate(
        [jnp.where(masks[0], m, 0.0), jnp.where(masks[1], m, 0.0)], axis=1
    ).astype(jnp.bfloat16)


def predict_tile(inline, part):
    p_re = p_im = None
    for i in range(HALF // 16):
        a_re = inline[16 * i : 16 * i + 16]
        a_im = inline[HALF + 16 * i : HALF + 16 * i + 16]
        b_re = part[16 * i : 16 * i + 16]
        b_im = part[HALF + 16 * i : HALF + 16 * i + 16]
        re = a_re * b_re - a_im * b_im
        im = a_re * b_im + a_im * b_re
        p_re = re if p_re is None else p_re + re
        p_im = im if p_im is None else p_im + im
    return p_re[:8] + p_re[8:], p_im[:8] + p_im[8:]


def predict_strip(mixing, cross, inline, w, g, s):
    out = []
    for first in (4 * s, 4 * s + 2):
        part = jnp.dot(
            mixing, side_by_side(cross, w, g, first, 2), preferred_element_type=jnp.float32
        )
        for k in range(2):
            table = inline[w][g, :, (first + k) * LANES : (first + k + 1) * LANES]
            out.append(predict_tile(table, part[:, k * LANES : (k + 1) * LANES]))
    return out


def predict_edges(mixing, cross, inline, w, g, tile):
    out = []
    for s in range(2):
        sl = slice((tile + 4 * s) * LANES, (tile + 4 * s + 1) * LANES)
        part = jnp.dot(mixing, cross[w][g, tile + 4 * s], preferred_element_type=jnp.float32)
        out.append(predict_tile(inline[w][g, :, sl], part))
    return out


def join(lower, upper):
    ramp = (iota((8, LANES), 1).astype(jnp.float32) + 0.5) / LANES
    return tuple((1.0 - ramp) * lower[c] + ramp * upper[c] for c in range(2))


def both_orders(own, others, windows):
    return [own.at[0]] + [others.at[n] for n in range(windows - 1)]


def blend(predicted, windows, win):
    joined = {}
    for n in range(windows if windows > 1 else 0):
        above = (n + 1) % windows
        apart = lax.rem(win + n, windows) == windows - 1
        trail, lead = predicted[n][3], predicted[above][0]
        both = join(trail, lead)
        joined[n, 3] = tuple(jnp.where(apart, trail[c], both[c]) for c in range(2))
        joined[above, 0] = tuple(jnp.where(apart, lead[c], both[c]) for c in range(2))
    for (n, tile), value in joined.items():
        predicted[n][tile] = value
    return predicted


def step_kernel(windows, nfreq, count, *refs):
    energies, refs = refs[:count], refs[count:]
    threshold, refs = refs[0], refs[1:]
    if windows > 1:
        cross, inline, observed, mask, updated = (
            both_orders(refs[n], refs[5 + n], windows) for n in range(5)
        )
        new = both_orders(refs[10], refs[11], windows)
        energy, factor, hb, acc = refs[12:]
    else:
        cross, inline, observed, mask, updated = ([refs[n].at[0]] for n in range(5))
        new = [refs[5].at[0]]
        energy, factor, hb, acc = refs[6:]
    win = lax.axis_index("win")
    spread_factor(energies, threshold, factor, windows, nfreq)
    masks, sign = group_masks(), half_sign()
    acc[...] = jnp.zeros_like(acc)
    for g in range(updated[0].shape[0]):
        mixing = [mix(updated[w][g] * factor[w], masks, sign) for w in range(windows)]
        buffers = [hb.at[(g * windows + w) % hb.shape[0]] for w in range(windows)]
        for s in range(2):
            predicted = blend(
                [predict_strip(mixing[w], cross, inline, w, g, s) for w in range(windows)],
                windows,
                win,
            )
            for w in range(windows):
                for t in range(4):
                    tile = 4 * s + t
                    sl = slice(tile * LANES, (tile + 1) * LANES)
                    here = mask[w][:, sl]
                    p_re, p_im = predicted[w][t]
                    r_re = here * p_re - observed[w][0, g, :, sl]
                    r_im = here * p_im - observed[w][1, g, :, sl]
                    weigh(inline[w], g, tile, r_re, r_im, buffers[w])
        for w in range(windows):
            slopes = project_group(buffers[w], cross, w, g, masks, sign)
            for part, slope in enumerate(slopes):
                rows = slice(part * HALF, (part + 1) * HALF)
                value = updated[w][g, rows] * factor[w, rows] - step_length * slope
                new[w][g, rows] = value
                acc[w, rows] += value * value
    for w in range(windows):
        pack_energy(acc[w], energy, 4 * w)


def final_kernel(windows, nfreq, count, *refs):
    energies, refs = refs[:count], refs[count:]
    threshold, matching, refs = refs[0], refs[1], refs[2:]
    if windows > 1:
        cross, inline, updated = (both_orders(refs[n], refs[3 + n], windows) for n in range(3))
        refs = refs[6:]
    else:
        cross, inline, updated = ([refs[n].at[0]] for n in range(3))
        refs = refs[3:]
    swap, keep, factor = refs
    win = lax.axis_index("win")
    spread_factor(energies, threshold, factor, windows, nfreq)
    masks, sign = group_masks(), half_sign()
    block = iota((GROUP, LANES), 1) // SPAN
    wide = iota((HALF, LANES), 1) // SPAN
    line, lane = iota((LANES, 2 * LANES), 0), iota((LANES, 2 * LANES), 1)
    b, imag = lane % PY, lane // LANES
    source = jnp.where(b < FOLD, b, SPAN + PY - 1 - b) + FOLD * imag
    value = jnp.where((imag == 1) & (b < FOLD), -1.0, 1.0)
    order = jnp.where(line == source, value, 0.0)

    for g in range(updated[0].shape[0]):
        current = updated[0][g] * factor[0]
        mixing = mix(current, masks, sign)
        traces = [x for s in range(2) for x in predict_strip(mixing, cross, inline, 0, g, s)]
        if windows > 1:
            mixed = [
                mix(updated[w][g] * factor[w], masks, sign) for w in sorted({1, windows - 1})
            ]
            above = predict_edges(mixed[0], cross, inline, 1, g, 0)
            below = predict_edges(mixed[-1], cross, inline, windows - 1, g, 3)
            for s in range(2):
                lead, trail = traces[4 * s], traces[4 * s + 3]
                low, high = join(below[s], lead), join(trail, above[s])
                traces[4 * s] = tuple(jnp.where(win > 0, low[c], lead[c]) for c in range(2))
                traces[4 * s + 3] = tuple(
                    jnp.where(win < windows - 1, high[c], trail[c]) for c in range(2)
                )
        spans = jnp.where(wide == 0, current[:HALF], jnp.where(wide == 1, current[HALF:], 0.0))
        spans = choose(spans, order)
        sl = slice(GROUP * g, GROUP * (g + 1))
        for c in range(2):
            for j in range(4):
                lanes = slice(j * LANES, (j + 1) * LANES)
                values = None
                for q in range(4):
                    a = 4 * j + q
                    part = spans[GROUP * a : GROUP * (a + 1), c * LANES : (c + 1) * LANES]
                    part = jnp.where(block == q, part, 0.0)
                    values = part if values is None else values + part
                swap[0, c, sl, lanes] = values
                keep[0, c, sl, lanes] = values
            for t in range(8):
                lanes = slice((t % 4) * LANES, (t % 4 + 1) * LANES)
                out = keep if t < 4 else swap
                out[1, c, sl, lanes] = traces[t][c]
    for s, out in enumerate((keep, swap)):
        lead = choose(
            jnp.concatenate([out[1, c, :, :LANES] for c in range(2)], axis=0), matching[s]
        )
        for c in range(2):
            out[1, c, :, :LANES] = lead[c * out.shape[2] : (c + 1) * out.shape[2]]


VM = pl.BlockSpec(memory_space=pltpu.VMEM)
HB = pl.BlockSpec(memory_space=pltpu.HBM)


def params(windows):
    return pltpu.CompilerParams(vmem_limit_bytes=(16 if windows <= 2 else 60) * 1024 * 1024)


def shape(*dims, dtype=jnp.float32):
    return jax.ShapeDtypeStruct(dims, dtype)


def sum_parts(energy):
    swap = [(0, 1), (1, 0)]
    energy = energy + lax.ppermute(energy, "rep", swap)
    size = lax.axis_size("freq")
    if size & (size - 1):
        return [lax.psum(energy, "freq")]
    axes = ("freq", "rep")

    def crossed(k):
        return [(2 * i + r, 2 * (i ^ k) + 1 - r) for i in range(size) for r in range(2)]

    if size <= 4:
        return [energy] + [lax.ppermute(energy, axes, crossed(k)) for k in range(1, size)]
    k = 1
    while k < size:
        energy = energy + lax.ppermute(energy, axes, crossed(k))
        k *= 2
    return [energy]


def per_device(recorded, geometry, present, intersection_index, pattern, group_scale):
    frequencies = recorded.shape[1]
    traces = recorded.shape[3]
    windows = lax.axis_size("win")
    nfreq = frequencies * lax.axis_size("freq")
    half = frequencies // 2
    groups = half // GROUP
    amplitude = 1.0 / math.sqrt(traces * lax.axis_size("rep"))
    width = 2 * traces
    swap = [(0, 1), (1, 0)]

    payload = shape(2 * half + 8, traces)
    turned = jnp.transpose(pattern, (1, 2, 0))
    sources = tuple(
        pltpu.with_memory_space_constraint(x, pltpu.HBM)
        for x in (recorded, geometry, present, intersection_index, turned)
    )
    coded = shape(2 * half + 16, traces, dtype=jnp.bfloat16)
    keep, send, keep_coded, send_coded = pl.pallas_call(
        pack_kernel,
        out_shape=(payload, payload, coded, coded),
        in_specs=[HB] * 5,
        out_specs=(VM,) * 4,
        scratch_shapes=[pltpu.VMEM(x.shape, x.dtype) for x in sources]
        + [
            pltpu.SemaphoreType.DMA((5,)),
            pltpu.VMEM((turned.shape[0] * turned.shape[1], frequencies), jnp.float32),
        ],
        compiler_params=params(windows),
        name="pack",
    )(*sources)
    received = lax.ppermute(send, "rep", swap)
    if windows == 2:
        diagonal = [(2 * i + r, 2 * (1 - i) + 1 - r) for i in range(2) for r in range(2)]
        others = [
            lax.ppermute(keep_coded, "win", swap),
            lax.ppermute(send_coded, ("win", "rep"), diagonal),
        ]
    else:
        received_coded = lax.ppermute(send_coded, "rep", swap)
        others = [lax.all_gather(x, "win") for x in (keep_coded, received_coded)]

    rows = 2 * HALF
    energy_shape = shape(4 * windows, LANES)

    def scratch(many):
        buffers = many * groups if windows <= 2 else windows
        return [
            pltpu.VMEM((buffers, width // LANES, rows, LANES), jnp.bfloat16),
            pltpu.VMEM((many, rows, LANES), jnp.float32),
        ]

    def build(own, inputs):
        many = 1 if own else windows - 1
        out_shape = (
            shape(many, groups, width // LANES, SPAN * GROUP, LANES, dtype=jnp.bfloat16),
            shape(many, groups, rows, width),
            shape(many, 2, groups, GROUP, width),
            shape(many, 8, width),
            shape(many, groups, rows, LANES),
            shape(4, LANES) if own else energy_shape,
        )
        if own:
            out_shape += (shape(2, LANES, LANES), shape(4, LANES))
        return pl.pallas_call(
            functools.partial(table_kernel, windows, nfreq, amplitude, own),
            out_shape=out_shape,
            in_specs=[VM] * (len(inputs) - 1) + [HB if own else VM],
            out_specs=(VM,) * len(out_shape),
            scratch_shapes=[pltpu.VMEM((many, 2, 2 * half + 8, traces), jnp.float32)]
            + scratch(many)
            + ([pltpu.VMEM((4, LANES), jnp.float32), pltpu.SemaphoreType.DMA] if own else []),
            compiler_params=params(windows),
            cost_estimate=pl.CostEstimate(flops=4 * 10**9, bytes_accessed=0, transcendentals=0),
            name="tables",
        )(*inputs)

    *tables, updated, energy, matching, threshold = build(
        True,
        [
            keep,
            received,
            pltpu.with_memory_space_constraint(group_scale.reshape(4, LANES), pltpu.HBM),
        ],
    )
    tables, states = [tables], [updated]
    if windows > 1:
        *others, updated, energy = build(False, others + [energy])
        tables.append(others)
        states.append(updated)

    factor_scratch = pltpu.VMEM((windows, rows, LANES), jnp.float32)
    for _ in range(ITERS - 1):
        inputs = [threshold]
        for table, state in zip(tables, states):
            inputs += [*table, state]
        energies = sum_parts(energy)
        *states, energy = pl.pallas_call(
            functools.partial(step_kernel, windows, nfreq, len(energies)),
            out_shape=tuple(shape(*x.shape) for x in states) + (energy_shape,),
            in_specs=[VM] * (len(energies) + len(inputs)),
            out_specs=(VM,) * (len(states) + 1),
            scratch_shapes=[factor_scratch] + scratch(windows),
            compiler_params=params(windows),
            name="step",
        )(*energies, *inputs)
    energies = sum_parts(energy)
    halves = shape(2, 2, half, traces)
    inputs = [threshold, matching]
    for table, state in zip(tables, states):
        inputs += [*table[:2], state]
    theirs, mine = pl.pallas_call(
        functools.partial(final_kernel, windows, nfreq, len(energies)),
        out_shape=(halves, halves),
        in_specs=[VM] * (len(energies) + len(inputs)),
        out_specs=(VM, VM),
        scratch_shapes=[factor_scratch],
        compiler_params=params(windows),
        name="final",
    )(*energies, *inputs)
    theirs = lax.ppermute(theirs, "rep", swap)
    out = shape(2, frequencies, 1, traces)
    return pl.pallas_call(
        unpack_kernel,
        out_shape=(out, out),
        in_specs=[VM, VM],
        out_specs=(VM, VM),
        compiler_params=params(windows),
        name="unpack",
    )(mine, theirs)


def solution(mesh):
    return jax.shard_map(
        per_device,
        mesh=mesh,
        in_specs=(
            P(None, "freq", ("dom", "win"), "rep"),
            P(None, ("dom", "win"), "rep"),
            P(("dom", "win"), "rep"),
            P(("dom", "win"), "rep", None),
            P("freq", None, "rep"),
            P(),
        ),
        out_specs=(P(None, "freq", ("dom", "win"), None), P(None, "freq", ("dom", "win"), "rep")),
        check_vma=False,
    )
```

```python
import functools
import math

import jax
import jax.numpy as jnp
from jax import lax
from jax.experimental import pallas as pl
from jax.experimental.pallas import tpu as pltpu
from jax.sharding import PartitionSpec as P

PX = 16
PY = 32
SPB = 64
OBS = 128
ITERS = 3
LANES = 128
GROUP = 8
HALF = PX * GROUP
FOLD = PY // 2
SPAN = 2 * FOLD

step_length = 1.0
epsilon = 1e-06
HIGHEST = lax.Precision.HIGHEST


def iota(shape, dim):
    return lax.broadcasted_iota(jnp.int32, shape, dim)


def half_turns(y):
    quarter = jnp.floor(2.0 * y + 0.5)
    r = y - 0.5 * quarter
    q = quarter.astype(jnp.int32)
    r2 = r * r
    pi = math.pi
    sine = r * (
        pi
        + r2
        * (
            -(pi**3) / 6
            + r2 * (pi**5 / 120 + r2 * (-(pi**7) / 5040 + r2 * (pi**9 / 362880)))
        )
    )
    cosine = 1.0 + r2 * (
        -(pi**2) / 2 + r2 * (pi**4 / 24 + r2 * (-(pi**6) / 720 + r2 * (pi**8 / 40320)))
    )
    odd = (q & 1) == 1
    c = jnp.where(odd, sine, cosine)
    s = jnp.where(odd, cosine, sine)
    c = jnp.where(((q + 1) & 2) != 0, -c, c)
    s = jnp.where((q & 2) != 0, s, -s)
    return c, s


def rounded(x):
    return x.astype(jnp.bfloat16).astype(jnp.float32)


def choose(values, hot, transposed=False):
    rest = values - rounded(values)
    last = rest - rounded(rest)
    parts = jnp.concatenate([values, rest, last], axis=0).astype(jnp.bfloat16)
    out = lax.dot_general(
        parts,
        hot.astype(jnp.bfloat16),
        (((1,), (1 if transposed else 0,)), ((), ())),
        preferred_element_type=jnp.float32,
    )
    n = values.shape[0]
    return out[:n] + (out[n : 2 * n] + out[2 * n :])


def times(p, q):
    return p[0] * q[0] - p[1] * q[1], p[0] * q[1] + p[1] * q[0]


def pack_kernel(
    recorded, geometry, present, intersection, pattern, keep, send, keep_coded, send_coded, *scratch
):
    sources = (recorded, geometry, present, intersection, pattern)
    local, sems, turned = scratch[:5], scratch[5], scratch[6]
    copies = [
        pltpu.make_async_copy(src, dst, sems.at[n]) for n, (src, dst) in enumerate(zip(sources, local))
    ]
    for copy in copies:
        copy.start()
    for copy in copies:
        copy.wait()
    recorded, geometry, present, intersection, pattern = local
    frequencies = recorded.shape[1]
    half = frequencies // 2
    rep = lax.axis_index("rep")
    blocks, span = pattern.shape[:2]
    for i in range(blocks):
        turned[span * i : span * (i + 1), :] = pattern[i].astype(jnp.float32)
    base = 2 * half
    for out, coded, part in ((keep, keep_coded, rep), (send, send_coded, 1 - rep)):
        for c in range(2):
            out[c * half : (c + 1) * half, :] = recorded[c, pl.ds(part * half, half), 0, :]
        out[base : base + 8, :] = jnp.zeros((8, out.shape[1]), jnp.float32)
        chosen = iota((half, frequencies), 0) + part * half == iota((half, frequencies), 1)
        pat = lax.dot_general(
            chosen.astype(jnp.float32),
            turned[...],
            (((1,), (1,)), ((), ())),
            preferred_element_type=jnp.float32,
        )
        for h in range(half // 8):
            out[base : base + 8, h * LANES : h * LANES + pat.shape[1]] = pat[8 * h : 8 * h + 8]
        for t in range(4):
            sl = slice(t * LANES, (t + 1) * LANES)
            out[base + t : base + t + 1, 256:384] = geometry[0, :, sl]
            out[base + 4 + t : base + 5 + t, 256:384] = geometry[1, :, sl]
            out[base + t : base + t + 1, 384:512] = present[:, sl].astype(jnp.float32)
        out[base + 4 : base + 5, 384:512] = intersection[0].astype(jnp.float32)
        coded[0:base, :] = out[0:base, :].astype(jnp.bfloat16)
        small = out[base : base + 8, :]
        rest = small[:, 256:384] - rounded(small[:, 256:384])
        parts = [rounded(rest), rounded(rest - rounded(rest)), jnp.zeros((8, 256), jnp.float32)]
        coded[base : base + 16, :] = jnp.concatenate(
            [small, jnp.concatenate(parts, axis=1)], axis=0
        ).astype(jnp.bfloat16)


def unpack_kernel(mine, theirs, coefficients, reconstruction):
    rep = lax.axis_index("rep")
    half = mine.shape[2]
    for n, out in enumerate((coefficients, reconstruction)):
        for c in range(2):
            out[c, pl.ds(rep * half, half), 0, :] = mine[n, c]
            out[c, pl.ds((1 - rep) * half, half), 0, :] = theirs[n, c]


def low_half(dims):
    return (iota(dims, 1) // FOLD) % 2 == 0


def swapped(values):
    return pltpu.roll(values, FOLD, 1)


def side_by_side(ref, w, g, first, count):
    return jnp.concatenate([ref[w][g, first + n] for n in range(count)], axis=1)


def project_group(hb, cross, w, g, masks, sign):
    tiles = hb.shape[0]
    half = tiles // 2
    first, second = (
        lax.dot_general(
            jnp.concatenate([hb[n] for n in range(k, k + half)], axis=1),
            side_by_side(cross, w, g, k, half),
            (((1,), (1,)), ((), ())),
            preferred_element_type=jnp.float32,
        )
        for k in (0, half)
    )
    g = first + second
    g = jnp.where(masks[0], g[:, :LANES], jnp.where(masks[1], g[:, LANES:], 0.0))
    g = g + pltpu.roll(g, 32, 1)
    g = g + pltpu.roll(g, 64, 1)
    top, bottom = g[:HALF], sign * swapped(g[HALF:])
    return top + bottom, top - bottom


def group_masks():
    rows = iota((2 * HALF, LANES), 0) % GROUP
    lanes = iota((2 * HALF, LANES), 1) // SPAN
    return rows == lanes, rows == lanes + 4


def half_sign():
    return jnp.where(low_half((HALF, LANES)), 1.0, -1.0)


def weigh(inline, g, tile, r_re, r_im, hb):
    sl = pl.ds(tile * LANES, LANES)
    for i in range(HALF // 16):
        rows = slice(16 * i, 16 * i + 16)
        low = slice(HALF + 16 * i, HALF + 16 * i + 16)
        a_re = inline[g, rows, sl]
        a_im = inline[g, low, sl]
        rr = jnp.concatenate([r_re, r_re], axis=0)
        ri = jnp.concatenate([r_im, r_im], axis=0)
        hb[tile, rows, :] = (a_re * rr + a_im * ri).astype(jnp.bfloat16)
        hb[tile, low, :] = (a_re * ri - a_im * rr).astype(jnp.bfloat16)


def pack_energy(values, energy, row):
    both = values + swapped(values)
    both = jnp.where(low_half((HALF, LANES)), both[:HALF], both[HALF:])
    block = iota((GROUP, LANES), 1) // SPAN
    for j in range(4):
        total = None
        for q in range(4):
            a = 4 * j + q
            part = jnp.where(block == q, both[GROUP * a : GROUP * (a + 1)], 0.0)
            total = part if total is None else total + part
        energy[pl.ds(row + j, 1), :] = jnp.sum(total, axis=0, keepdims=True)


def table_kernel(windows, nfreq, amplitude, own, *refs):
    pays, refs = refs[:2], refs[2:]
    extra, refs = refs[0], refs[1:]
    cross, inline, observed, mask, updated, energy, *refs = refs
    if own:
        matching, threshold, pay, hb, acc, scale_local, sem = refs
        scale_copy = pltpu.make_async_copy(extra, scale_local, sem)
        scale_copy.start()
    else:
        pay, hb, acc = refs
        energy[0:4, :] = extra[...]
    many = pay.shape[0]
    half = pay.shape[2] - 8
    freqs = half // 2
    win = lax.axis_index("win")
    first = (2 * lax.axis_index("freq") + lax.axis_index("rep")) * freqs
    groups = freqs // GROUP
    base = half

    def window(n):
        return win if own else lax.rem(win + 1 + n, windows)

    for n in range(many):
        for s in range(2):
            source = pays[s] if len(pays[s].shape) == 2 else pays[s].at[window(n)]
            if own:
                pay[n, s] = source[...]
                continue
            pay[n, s, 0:base, :] = source[0:base, :].astype(jnp.float32)
            small = source[base : base + 16, :].astype(jnp.float32)
            pay[n, s, base : base + 8, :] = small[:8]
            pay[n, s, base : base + 8, 256:384] = (
                small[:8, 256:384] + small[8:, :LANES] + small[8:, LANES:256]
            )

    def pairing(n, s):
        index = pay[n, s, base + 4 : base + 5, 384:512].astype(jnp.int32)
        index = jnp.where(window(n) > 0, index, iota((1, LANES), 1))
        return (iota((LANES, LANES), 0) == index).astype(jnp.float32)

    if own:
        for s in range(2):
            matching[s] = pairing(0, s)

    def align(n, _):
        n, s = n // 2, n % 2
        lead = [
            pay[n, s, 0:half, 0:LANES],
            pay[n, s, base : base + 8, 256:384],
            pay[n, s, base : base + 8, 384:512],
        ]
        lead = choose(jnp.concatenate(lead, axis=0), pairing(n, s), transposed=True)
        pay[n, s, 0:half, 0:LANES] = lead[:half]
        pay[n, s, base : base + 1, 256:384] = lead[half : half + 1]
        pay[n, s, base + 4 : base + 5, 256:384] = lead[half + 4 : half + 5]
        pay[n, s, base : base + 1, 384:512] = lead[half + 8 : half + 9]
        return 0

    lax.fori_loop(0, 2 * many, align, 0, unroll=many == 1)

    sub = iota((8, LANES), 0)
    delta = 0.75 / nfreq
    start = first.astype(jnp.float32)
    scale0 = 0.25 + 0.75 * ((start + 0.5) / nfreq)
    odd_cross = (2 * sub - (PY - 1)).astype(jnp.float32)

    def strip_tables(n, _):
        n, s = n // 2, n % 2
        for t in range(4):
            off = pl.multiple_of(s * 512 + t * LANES, LANES)
            sl = pl.ds(off, LANES)
            g0 = pay[n, s, base + t : base + t + 1, 256:384]
            g1 = pay[n, s, base + 4 + t : base + 5 + t, 256:384]
            here = jnp.broadcast_to(pay[n, s, base + t : base + t + 1, 384:512], (8, LANES))
            mask[n, :, sl] = here
            now = half_turns((scale0 * g1) * odd_cross)
            more = half_turns((delta * g1) * odd_cross)
            g1b = jnp.broadcast_to(g1, (8, LANES))
            rot = half_turns((scale0 * g1b) * 16.0)
            rot_more = half_turns((delta * g1b) * 16.0)
            for f in range(freqs):
                v0 = now
                v1 = times(v0, rot)
                row = (f % GROUP) * SPAN
                for part in range(2):
                    cross[n, f // GROUP, 4 * s + t, row + FOLD * part : row + FOLD * (part + 1), :] = (
                        jnp.concatenate([v0[part], v1[part]], axis=0).astype(jnp.bfloat16)
                    )
                if f + 1 < freqs:
                    now = times(now, more)
                    rot = times(rot, rot_more)
            for g in range(groups):
                level = start + (sub + g * GROUP).astype(jnp.float32)
                scale = 0.25 + 0.75 * ((level + 0.5) / nfreq)
                v = half_turns((scale * g0) * 2.0)
                rot = half_turns((scale * g0) * 4.0)
                v = (v[0] * amplitude, v[1] * amplitude)
                for a in range(PX // 2, PX, 2):
                    u = times(v, rot)
                    i, mirror = a // 2, (PX - 1 - a) // 2
                    lane = g * LANES + t
                    col = pay[n, s, base : base + 8, lane + 4 * i : lane + 4 * i + 1]
                    other = pay[n, s, base : base + 8, lane + 4 * mirror : lane + 4 * mirror + 1]
                    low = GROUP * (PX - 2 - a)
                    for part in range(2):
                        row = part * HALF
                        inline[n, g, row + GROUP * a : row + GROUP * (a + 2), sl] = (
                            rounded(jnp.concatenate([v[part] * col, u[part] * col], axis=0))
                        )
                        turn = -other if part else other
                        inline[n, g, row + low : row + low + 2 * GROUP, sl] = (
                            rounded(jnp.concatenate([u[part] * turn, v[part] * turn], axis=0))
                        )
                    if a + 2 < PX:
                        v = times(u, rot)
            for c in range(2):
                for g in range(groups):
                    row = c * freqs + GROUP * g
                    observed[n, c, g, :, sl] = (
                        here * pay[n, s, row : row + GROUP, t * LANES : (t + 1) * LANES]
                    )
        return 0

    lax.fori_loop(0, 2 * many, strip_tables, 0)

    masks, sign = group_masks(), half_sign()
    acc[...] = jnp.zeros_like(acc)

    def first_group(k, _):
        g, n = k % groups, k // groups
        buffer = hb.at[k % hb.shape[0]]
        for tile in range(8):
            sl = slice(tile * LANES, (tile + 1) * LANES)
            r_re, r_im = -observed[n, 0, g, :, sl], -observed[n, 1, g, :, sl]
            weigh(inline.at[n], g, tile, r_re, r_im, buffer)
        slopes = project_group(buffer, [cross.at[n]], 0, g, masks, sign)
        for part, slope in enumerate(slopes):
            rows = slice(part * HALF, (part + 1) * HALF)
            value = -step_length * slope
            updated[n, g, rows] = value
            acc[n, rows] += value * value
        return 0

    lax.fori_loop(0, many * groups, first_group, 0, unroll=True)
    for n in range(many):
        pack_energy(acc[n], energy, 4 * (n + (not own)))
    if own:
        scale_copy.wait()
        lane = iota((LANES, LANES), 1)
        at = lane % SPAN
        source = jnp.where(at < FOLD, lane, lane + PY - 1 + FOLD - 2 * at)
        order = (iota((LANES, LANES), 0) == source).astype(jnp.float32)
        threshold[...] = jnp.dot(
            scale_local[...], order, precision=HIGHEST, preferred_element_type=jnp.float32
        )


def spread_factor(energies, threshold, factor, windows, nfreq):
    total = energies[0][...]
    for e in energies[1:]:
        total = total + e[...]
    limit = jnp.concatenate([threshold[...]] * windows, axis=0)
    packed = jnp.maximum(0.0, 1.0 - limit / jnp.sqrt(total / nfreq + epsilon))
    block = iota((8, LANES), 1) // SPAN
    low = low_half((8, LANES))
    for w in range(windows):
        for a in range(PX):
            row = w * 4 + a // 4
            y = jnp.where(block == a % 4, jnp.broadcast_to(packed[row : row + 1], (8, LANES)), 0.0)
            y = y + pltpu.roll(y, 32, 1)
            y = y + pltpu.roll(y, 64, 1)
            turned = swapped(y)
            factor[w, GROUP * a : GROUP * (a + 1), :] = jnp.where(low, y, turned)
            factor[w, HALF + GROUP * a : HALF + GROUP * (a + 1), :] = jnp.where(low, turned, y)


def mix(current, masks, sign):
    first, second = current[:HALF], current[HALF:]
    m = jnp.concatenate([first + second, swapped(sign * (first - second))], axis=0)
    return jnp.concatenate(
        [jnp.where(masks[0], m, 0.0), jnp.where(masks[1], m, 0.0)], axis=1
    ).astype(jnp.bfloat16)


def predict_tile(inline, part):
    p_re = p_im = None
    for i in range(HALF // 16):
        a_re = inline[16 * i : 16 * i + 16]
        a_im = inline[HALF + 16 * i : HALF + 16 * i + 16]
        b_re = part[16 * i : 16 * i + 16]
        b_im = part[HALF + 16 * i : HALF + 16 * i + 16]
        re = a_re * b_re - a_im * b_im
        im = a_re * b_im + a_im * b_re
        p_re = re if p_re is None else p_re + re
        p_im = im if p_im is None else p_im + im
    return p_re[:8] + p_re[8:], p_im[:8] + p_im[8:]


def predict_strip(mixing, cross, inline, w, g, s):
    out = []
    for first in (4 * s, 4 * s + 2):
        part = jnp.dot(
            mixing, side_by_side(cross, w, g, first, 2), preferred_element_type=jnp.float32
        )
        for k in range(2):
            table = inline[w][g, :, (first + k) * LANES : (first + k + 1) * LANES]
            out.append(predict_tile(table, part[:, k * LANES : (k + 1) * LANES]))
    return out


def predict_edges(mixing, cross, inline, w, g, tile):
    out = []
    for s in range(2):
        sl = slice((tile + 4 * s) * LANES, (tile + 4 * s + 1) * LANES)
        part = jnp.dot(mixing, cross[w][g, tile + 4 * s], preferred_element_type=jnp.float32)
        out.append(predict_tile(inline[w][g, :, sl], part))
    return out


def join(lower, upper):
    ramp = (iota((8, LANES), 1).astype(jnp.float32) + 0.5) / LANES
    return tuple((1.0 - ramp) * lower[c] + ramp * upper[c] for c in range(2))


def both_orders(own, others, windows):
    return [own.at[0]] + [others.at[n] for n in range(windows - 1)]


def blend(predicted, windows, win):
    joined = {}
    for n in range(windows if windows > 1 else 0):
        above = (n + 1) % windows
        apart = lax.rem(win + n, windows) == windows - 1
        trail, lead = predicted[n][3], predicted[above][0]
        both = join(trail, lead)
        joined[n, 3] = tuple(jnp.where(apart, trail[c], both[c]) for c in range(2))
        joined[above, 0] = tuple(jnp.where(apart, lead[c], both[c]) for c in range(2))
    for (n, tile), value in joined.items():
        predicted[n][tile] = value
    return predicted


def step_kernel(windows, nfreq, count, *refs):
    energies, refs = refs[:count], refs[count:]
    threshold, refs = refs[0], refs[1:]
    if windows > 1:
        cross, inline, observed, mask, updated = (
            both_orders(refs[n], refs[5 + n], windows) for n in range(5)
        )
        new = both_orders(refs[10], refs[11], windows)
        energy, factor, hb, acc = refs[12:]
    else:
        cross, inline, observed, mask, updated = ([refs[n].at[0]] for n in range(5))
        new = [refs[5].at[0]]
        energy, factor, hb, acc = refs[6:]
    win = lax.axis_index("win")
    spread_factor(energies, threshold, factor, windows, nfreq)
    masks, sign = group_masks(), half_sign()
    acc[...] = jnp.zeros_like(acc)
    for g in range(updated[0].shape[0]):
        mixing = [mix(updated[w][g] * factor[w], masks, sign) for w in range(windows)]
        buffers = [hb.at[(g * windows + w) % hb.shape[0]] for w in range(windows)]
        for s in range(2):
            predicted = blend(
                [predict_strip(mixing[w], cross, inline, w, g, s) for w in range(windows)],
                windows,
                win,
            )
            for w in range(windows):
                for t in range(4):
                    tile = 4 * s + t
                    sl = slice(tile * LANES, (tile + 1) * LANES)
                    here = mask[w][:, sl]
                    p_re, p_im = predicted[w][t]
                    r_re = here * p_re - observed[w][0, g, :, sl]
                    r_im = here * p_im - observed[w][1, g, :, sl]
                    weigh(inline[w], g, tile, r_re, r_im, buffers[w])
        for w in range(windows):
            slopes = project_group(buffers[w], cross, w, g, masks, sign)
            for part, slope in enumerate(slopes):
                rows = slice(part * HALF, (part + 1) * HALF)
                value = updated[w][g, rows] * factor[w, rows] - step_length * slope
                new[w][g, rows] = value
                acc[w, rows] += value * value
    for w in range(windows):
        pack_energy(acc[w], energy, 4 * w)


def final_kernel(windows, nfreq, count, *refs):
    energies, refs = refs[:count], refs[count:]
    threshold, matching, refs = refs[0], refs[1], refs[2:]
    if windows > 1:
        cross, inline, updated = (both_orders(refs[n], refs[3 + n], windows) for n in range(3))
        refs = refs[6:]
    else:
        cross, inline, updated = ([refs[n].at[0]] for n in range(3))
        refs = refs[3:]
    swap, keep, factor = refs
    win = lax.axis_index("win")
    spread_factor(energies, threshold, factor, windows, nfreq)
    masks, sign = group_masks(), half_sign()
    block = iota((GROUP, LANES), 1) // SPAN
    wide = iota((HALF, LANES), 1) // SPAN
    line, lane = iota((LANES, 2 * LANES), 0), iota((LANES, 2 * LANES), 1)
    b, imag = lane % PY, lane // LANES
    source = jnp.where(b < FOLD, b, SPAN + PY - 1 - b) + FOLD * imag
    value = jnp.where((imag == 1) & (b < FOLD), -1.0, 1.0)
    order = jnp.where(line == source, value, 0.0)

    for g in range(updated[0].shape[0]):
        current = updated[0][g] * factor[0]
        mixing = mix(current, masks, sign)
        traces = [x for s in range(2) for x in predict_strip(mixing, cross, inline, 0, g, s)]
        if windows > 1:
            mixed = [
                mix(updated[w][g] * factor[w], masks, sign) for w in sorted({1, windows - 1})
            ]
            above = predict_edges(mixed[0], cross, inline, 1, g, 0)
            below = predict_edges(mixed[-1], cross, inline, windows - 1, g, 3)
            for s in range(2):
                lead, trail = traces[4 * s], traces[4 * s + 3]
                low, high = join(below[s], lead), join(trail, above[s])
                traces[4 * s] = tuple(jnp.where(win > 0, low[c], lead[c]) for c in range(2))
                traces[4 * s + 3] = tuple(
                    jnp.where(win < windows - 1, high[c], trail[c]) for c in range(2)
                )
        spans = jnp.where(wide == 0, current[:HALF], jnp.where(wide == 1, current[HALF:], 0.0))
        spans = choose(spans, order)
        sl = slice(GROUP * g, GROUP * (g + 1))
        for c in range(2):
            for j in range(4):
                lanes = slice(j * LANES, (j + 1) * LANES)
                values = None
                for q in range(4):
                    a = 4 * j + q
                    part = spans[GROUP * a : GROUP * (a + 1), c * LANES : (c + 1) * LANES]
                    part = jnp.where(block == q, part, 0.0)
                    values = part if values is None else values + part
                swap[0, c, sl, lanes] = values
                keep[0, c, sl, lanes] = values
            for t in range(8):
                lanes = slice((t % 4) * LANES, (t % 4 + 1) * LANES)
                out = keep if t < 4 else swap
                out[1, c, sl, lanes] = traces[t][c]
    for s, out in enumerate((keep, swap)):
        lead = choose(
            jnp.concatenate([out[1, c, :, :LANES] for c in range(2)], axis=0), matching[s]
        )
        for c in range(2):
            out[1, c, :, :LANES] = lead[c * out.shape[2] : (c + 1) * out.shape[2]]


VM = pl.BlockSpec(memory_space=pltpu.VMEM)
HB = pl.BlockSpec(memory_space=pltpu.HBM)


def params(windows):
    return pltpu.CompilerParams(vmem_limit_bytes=(16 if windows <= 2 else 60) * 1024 * 1024)


def shape(*dims, dtype=jnp.float32):
    return jax.ShapeDtypeStruct(dims, dtype)


def sum_parts(energy):
    swap = [(0, 1), (1, 0)]
    energy = energy + lax.ppermute(energy, "rep", swap)
    size = lax.axis_size("freq")
    if size & (size - 1):
        return [lax.psum(energy, "freq")]
    axes = ("freq", "rep")

    def crossed(k):
        return [(2 * i + r, 2 * (i ^ k) + 1 - r) for i in range(size) for r in range(2)]

    if size <= 4:
        return [energy] + [lax.ppermute(energy, axes, crossed(k)) for k in range(1, size)]
    k = 1
    while k < size:
        energy = energy + lax.ppermute(energy, axes, crossed(k))
        k *= 2
    return [energy]


def per_device(recorded, geometry, present, intersection_index, pattern, group_scale):
    frequencies = recorded.shape[1]
    traces = recorded.shape[3]
    windows = lax.axis_size("win")
    nfreq = frequencies * lax.axis_size("freq")
    half = frequencies // 2
    groups = half // GROUP
    amplitude = 1.0 / math.sqrt(traces * lax.axis_size("rep"))
    width = 2 * traces
    swap = [(0, 1), (1, 0)]

    payload = shape(2 * half + 8, traces)
    turned = jnp.transpose(pattern, (1, 2, 0))
    sources = tuple(
        pltpu.with_memory_space_constraint(x, pltpu.HBM)
        for x in (recorded, geometry, present, intersection_index, turned)
    )
    coded = shape(2 * half + 16, traces, dtype=jnp.bfloat16)
    keep, send, keep_coded, send_coded = pl.pallas_call(
        pack_kernel,
        out_shape=(payload, payload, coded, coded),
        in_specs=[HB] * 5,
        out_specs=(VM,) * 4,
        scratch_shapes=[pltpu.VMEM(x.shape, x.dtype) for x in sources]
        + [
            pltpu.SemaphoreType.DMA((5,)),
            pltpu.VMEM((turned.shape[0] * turned.shape[1], frequencies), jnp.float32),
        ],
        compiler_params=params(windows),
        name="pack",
    )(*sources)
    received = lax.ppermute(send, "rep", swap)
    if windows == 2:
        diagonal = [(2 * i + r, 2 * (1 - i) + 1 - r) for i in range(2) for r in range(2)]
        others = [
            lax.ppermute(keep_coded, "win", swap),
            lax.ppermute(send_coded, ("win", "rep"), diagonal),
        ]
    else:
        received_coded = lax.ppermute(send_coded, "rep", swap)
        others = [lax.all_gather(x, "win") for x in (keep_coded, received_coded)]

    rows = 2 * HALF
    energy_shape = shape(4 * windows, LANES)

    def scratch(many):
        buffers = many * groups if windows <= 2 else windows
        return [
            pltpu.VMEM((buffers, width // LANES, rows, LANES), jnp.bfloat16),
            pltpu.VMEM((many, rows, LANES), jnp.float32),
        ]

    def build(own, inputs):
        many = 1 if own else windows - 1
        out_shape = (
            shape(many, groups, width // LANES, SPAN * GROUP, LANES, dtype=jnp.bfloat16),
            shape(many, groups, rows, width),
            shape(many, 2, groups, GROUP, width),
            shape(many, 8, width),
            shape(many, groups, rows, LANES),
            shape(4, LANES) if own else energy_shape,
        )
        if own:
            out_shape += (shape(2, LANES, LANES), shape(4, LANES))
        return pl.pallas_call(
            functools.partial(table_kernel, windows, nfreq, amplitude, own),
            out_shape=out_shape,
            in_specs=[VM] * (len(inputs) - 1) + [HB if own else VM],
            out_specs=(VM,) * len(out_shape),
            scratch_shapes=[pltpu.VMEM((many, 2, 2 * half + 8, traces), jnp.float32)]
            + scratch(many)
            + ([pltpu.VMEM((4, LANES), jnp.float32), pltpu.SemaphoreType.DMA] if own else []),
            compiler_params=params(windows),
            cost_estimate=pl.CostEstimate(flops=4 * 10**9, bytes_accessed=0, transcendentals=0),
            name="tables",
        )(*inputs)

    *tables, updated, energy, matching, threshold = build(
        True,
        [
            keep,
            received,
            pltpu.with_memory_space_constraint(group_scale.reshape(4, LANES), pltpu.HBM),
        ],
    )
    tables, states = [tables], [updated]
    if windows > 1:
        *others, updated, energy = build(False, others + [energy])
        tables.append(others)
        states.append(updated)

    factor_scratch = pltpu.VMEM((windows, rows, LANES), jnp.float32)
    for _ in range(ITERS - 1):
        inputs = [threshold]
        for table, state in zip(tables, states):
            inputs += [*table, state]
        energies = sum_parts(energy)
        *states, energy = pl.pallas_call(
            functools.partial(step_kernel, windows, nfreq, len(energies)),
            out_shape=tuple(shape(*x.shape) for x in states) + (energy_shape,),
            in_specs=[VM] * (len(energies) + len(inputs)),
            out_specs=(VM,) * (len(states) + 1),
            scratch_shapes=[factor_scratch] + scratch(windows),
            compiler_params=params(windows),
            name="step",
        )(*energies, *inputs)
    energies = sum_parts(energy)
    halves = shape(2, 2, half, traces)
    inputs = [threshold, matching]
    for table, state in zip(tables, states):
        inputs += [*table[:2], state]
    theirs, mine = pl.pallas_call(
        functools.partial(final_kernel, windows, nfreq, len(energies)),
        out_shape=(halves, halves),
        in_specs=[VM] * (len(energies) + len(inputs)),
        out_specs=(VM, VM),
        scratch_shapes=[factor_scratch],
        compiler_params=params(windows),
        name="final",
    )(*energies, *inputs)
    theirs = lax.ppermute(theirs, "rep", swap)
    out = shape(2, frequencies, 1, traces)
    return pl.pallas_call(
        unpack_kernel,
        out_shape=(out, out),
        in_specs=[VM, VM],
        out_specs=(VM, VM),
        compiler_params=params(windows),
        name="unpack",
    )(mine, theirs)


def solution(mesh):
    return jax.shard_map(
        per_device,
        mesh=mesh,
        in_specs=(
            P(None, "freq", ("dom", "win"), "rep"),
            P(None, ("dom", "win"), "rep"),
            P(("dom", "win"), "rep"),
            P(("dom", "win"), "rep", None),
            P("freq", None, "rep"),
            P(),
        ),
        out_specs=(P(None, "freq", ("dom", "win"), None), P(None, "freq", ("dom", "win"), "rep")),
        check_vma=False,
    )
```
